32 devices in a mesh: groups: 2 (over y), rows: 4 (over z), cols: 2 (over x), section: 2 (over core).
Axes of the slice: x: 2, y: 2, z: 4, core: 2. Of those that a mesh axis runs over, the one named last changes fastest.
Arguments:
- state: float32 [2, 64, 512], P(None, ('groups', 'rows'), ('cols', 'section')), parts along dimension 1, may hold values from -6 to 6
- cotangent: float32 [2, 64, 512], P(None, ('groups', 'rows'), ('cols', 'section')), parts along dimension 1, may hold values from -6 to 6
- first_weight: bfloat16 [64, 18], replicated, may hold values from -1.5 to 1.5
- second_weight: bfloat16 [64, 64], replicated, may hold values from -0.75 to 0.75
- third_weight: bfloat16 [32, 64], replicated, may hold values from -0.75 to 0.75
Outputs:
- velocity: float32 [2, 64, 512], P(None, ('groups', 'rows'), ('cols', 'section')), parts along dimension 1
- grad_first: float32 [128, 18], P('groups'), parts along dimension 0
- grad_second: float32 [128, 64], P('groups'), parts along dimension 0
- grad_third: float32 [64, 64], P('groups'), parts along dimension 0
The draws below stay inside these ranges and needn't reach their ends.
There are 2 independent parts, one for each index of `groups`. The reference program is written for one: setup_inputs(seed, part) draws one part's arguments, and reference() takes and returns one part's arrays. A program takes and returns all parts, laid end to end along the dimension named above; an argument that names none is the same for every part. Nothing has to cross between parts.
All inputs are finite; a program needn't handle non-finite values.
Results may differ from the reference program's by a relative error of at most 0.0045.
Values sent between devices are 32-bit elements; how exact they have to be, the bound alone decides.
No kernel may reach another device: no remote copies, remote signals or barrier semaphores. Data moves between devices by JAX's collectives and lax.ppermute only.
A program may use at most 64 MiB of HBM per device.

```python
import math
import jax
import jax.numpy as jnp
from jax import lax

CHANNELS = 64
TAPS = 18
COEFS = 32
STEPS = 4
SWEEPS = 3
NX = 32
NY = 512


def block_scale(key, extent, cuts, low, high):
    gain, own = 1.0, jax.random.fold_in(key, 6)
    for position, blocks in cuts:
        steps = jnp.exp(jax.random.uniform(jax.random.fold_in(own, position), (blocks,), jnp.float32, low / len(cuts), high / len(cuts)))
        gain = gain * jnp.repeat(steps, extent[position] // blocks).reshape([-1 if axis == position else 1 for axis in range(len(extent))])
    return gain


def normal_values(stream_key, shape, spread, limit, cuts=(), kind=jnp.bfloat16):
    result = spread * jax.random.normal(stream_key, shape, jnp.float32)
    if cuts:
        result = result * block_scale(stream_key, shape, cuts, -0.22, 0.18)
    return jnp.clip(result, -limit, limit).astype(kind)


def setup_inputs(seed: int = 0, part: int = 0) -> dict:
    arg_keys = jax.random.split(jax.random.key(seed), 6)
    part_splits = jax.random.split(jax.random.fold_in(arg_keys[5], part), 6)
    return {
        "state": normal_values(part_splits[0], (2, NX, NY), 1.0, 6.0, ((1, 4), (2, 4)), jnp.float32),
        "cotangent": normal_values(part_splits[1], (2, NX, NY), 1.0, 6.0, ((1, 4), (2, 4)), jnp.float32),
        "first_weight": normal_values(arg_keys[2], (CHANNELS, TAPS), TAPS ** -0.5, 1.5),
        "second_weight": normal_values(arg_keys[3], (CHANNELS, CHANNELS), CHANNELS ** -0.5, 0.75),
        "third_weight": normal_values(arg_keys[4], (COEFS, CHANNELS), CHANNELS ** -0.5, 0.75),
    }


time_step = 0.1
viscosity = 0.2
correction_gain = 0.25
gradient_gain = 10.0

def base_table():
    return jnp.array([[0.5 if tap_number in (5, 9) else 0.0 for tap_number in range(16)], [0.5 if tap_number in (5, 6) else 0.0 for tap_number in range(16)]], jnp.float32)

def patches(extended):
    height = extended.shape[1] - 3
    breadth = extended.shape[2] - 3
    pieces = [extended[:, offset_row:offset_row + height, offset_col:offset_col + breadth] for offset_row in range(3) for offset_col in range(3)]
    return jnp.stack(pieces, 1).reshape(18, height * breadth)

def network(inputs, first_weight, second_weight, third_weight):
    rounded = inputs.astype(jnp.bfloat16)
    first_pre = jnp.dot(first_weight, rounded, preferred_element_type=jnp.float32)
    first_act = jax.nn.gelu(first_pre).astype(jnp.bfloat16)
    second_pre = jnp.dot(second_weight, first_act, preferred_element_type=jnp.float32)
    second_act = jax.nn.gelu(second_pre).astype(jnp.bfloat16)
    coefficients = jnp.dot(third_weight, second_act, preferred_element_type=jnp.float32)
    return (rounded, first_pre, first_act, second_pre, second_act, coefficients)

def physics(extended, coefficients):
    height = extended.shape[1] - 3
    breadth = extended.shape[2] - 3
    inner_rows = height - 1
    inner_cols = breadth - 1
    raw_output = coefficients.reshape(2, 16, height, breadth)
    weights = base_table()[:, :, None, None] + correction_gain * (raw_output - lax.optimization_barrier(jnp.mean(raw_output, axis=1, keepdims=True)))
    stencil = jnp.stack([extended[:, offset_row:offset_row + height, offset_col:offset_col + breadth] for offset_row in range(4) for offset_col in range(4)], 0)
    face_rows = lax.optimization_barrier(jnp.sum(weights[0][:, None] * stencil, axis=0))
    face_cols = lax.optimization_barrier(jnp.sum(weights[1][:, None] * stencil, axis=0))
    speed_rows = 0.5 * (extended[0, 1:1 + height, 1:1 + breadth] + extended[0, 2:2 + height, 1:1 + breadth])
    speed_cols = 0.5 * (extended[1, 1:1 + height, 1:1 + breadth] + extended[1, 1:1 + height, 2:2 + breadth])
    flux_rows = speed_rows * face_rows
    flux_cols = speed_cols * face_cols
    transport = flux_rows[:, 1:, 1:] - flux_rows[:, :-1, 1:] + flux_cols[:, 1:, 1:] - flux_cols[:, 1:, :-1]
    centre = extended[:, 2:2 + inner_rows, 2:2 + inner_cols]
    laplace = extended[:, 1:1 + inner_rows, 2:2 + inner_cols] + extended[:, 3:3 + inner_rows, 2:2 + inner_cols] + extended[:, 2:2 + inner_rows, 1:1 + inner_cols] + extended[:, 2:2 + inner_rows, 3:3 + inner_cols] - 4.0 * centre
    return centre - time_step * transport + time_step * viscosity * laplace

def advance(extended, first_weight, second_weight, third_weight):
    outputs = network(patches(extended), first_weight, second_weight, third_weight)
    return physics(extended, outputs[5])

def gelu_back(preact, upstream):
    return jax.vjp(jax.nn.gelu, preact)[1](upstream)[0]

def advance_back(extended, first_weight, second_weight, third_weight, upstream):
    inputs, patch_back = jax.vjp(patches, extended)
    rounded, first_pre, first_act, second_pre, second_act, coefficients = network(inputs, first_weight, second_weight, third_weight)
    advanced, physics_back = jax.vjp(physics, extended, coefficients)
    extended_grad, coef_grad = physics_back(upstream)
    coef_round = coef_grad.astype(jnp.bfloat16)
    outer = (((1,), (1,)), ((), ()))
    inner = (((0,), (0,)), ((), ()))
    third_grad = lax.dot_general(coef_round, second_act, outer, preferred_element_type=jnp.float32)
    second_back = gelu_back(second_pre, lax.dot_general(third_weight, coef_round, inner, preferred_element_type=jnp.float32)).astype(jnp.bfloat16)
    second_grad = lax.dot_general(second_back, first_act, outer, preferred_element_type=jnp.float32)
    first_back = gelu_back(first_pre, lax.dot_general(second_weight, second_back, inner, preferred_element_type=jnp.float32)).astype(jnp.bfloat16)
    first_grad = lax.dot_general(first_back, rounded, outer, preferred_element_type=jnp.float32)
    input_grad = lax.dot_general(first_weight, first_back, inner, preferred_element_type=jnp.float32)
    extended_grad = extended_grad + patch_back(input_grad)[0]
    return (extended_grad, (first_grad, second_grad, third_grad))

def divergence(padded):
    return 0.5 * (padded[0, 2:, 1:-1] - padded[0, :-2, 1:-1] + (padded[1, 1:-1, 2:] - padded[1, 1:-1, :-2]))

def neighbours(padded):
    return padded[2:, 1:-1] + padded[:-2, 1:-1] + padded[1:-1, 2:] + padded[1:-1, :-2]

def pressure_gradient(padded):
    return jnp.stack([0.5 * (padded[2:, 1:-1] - padded[:-2, 1:-1]), 0.5 * (padded[1:-1, 2:] - padded[1:-1, :-2])])

def wrap_pad(field, margin):
    return jnp.pad(field, [(0, 0)] * (field.ndim - 2) + [(margin, margin), (margin, margin)], mode='wrap')

def fold_wrap(padded, margin):
    row_count = padded.shape[-2] - 2 * margin
    col_count = padded.shape[-1] - 2 * margin
    leading = [(0, 0)] * (padded.ndim - 1)
    middle = padded[..., margin:margin + col_count] + jnp.pad(padded[..., margin + col_count:], leading + [(0, col_count - margin)]) + jnp.pad(padded[..., :margin], leading + [(col_count - margin, 0)])
    leading_rows = [(0, 0)] * (padded.ndim - 2)
    return middle[..., margin:margin + row_count, :] + jnp.pad(middle[..., margin + row_count:, :], leading_rows + [(0, row_count - margin), (0, 0)]) + jnp.pad(middle[..., :margin, :], leading_rows + [(row_count - margin, 0), (0, 0)])

def reference(state, cotangent, first_weight, second_weight, third_weight):
    weights = (first_weight, second_weight, third_weight)
    row_total = state.shape[1]
    col_total = state.shape[2]
    blocks = row_total // 8
    block_ids = jnp.arange(blocks, dtype=jnp.int32)
    current = state
    saved = []
    for step_number in range(STEPS):
        extended = wrap_pad(current, 2)

        def one_block(block_index, extended=extended):
            part = lax.dynamic_slice_in_dim(extended, block_index * 8, 12, 1)
            return advance(part, *weights)
        stacked = lax.map(one_block, block_ids)
        moved = jnp.transpose(stacked, (1, 0, 2, 3)).reshape(2, row_total, col_total)
        velocity_pad = wrap_pad(moved, 1)
        source = divergence(velocity_pad)
        pressure = -0.25 * source
        pressure_pads = []
        for sweep_number in range(SWEEPS):
            padded = wrap_pad(pressure, 1)
            pressure_pads.append(padded)
            if sweep_number < SWEEPS - 1:
                pressure = 0.25 * (neighbours(padded) - source)
        saved.append((extended, velocity_pad, pressure_pads))
        current = moved - pressure_gradient(pressure_pads[-1])
    upstream = cotangent
    totals = (jnp.zeros(first_weight.shape, jnp.float32), jnp.zeros(second_weight.shape, jnp.float32), jnp.zeros(third_weight.shape, jnp.float32))
    for step_number in reversed(range(STEPS)):
        extended, velocity_pad, pressure_pads = saved[step_number]
        pad_grad = jax.vjp(pressure_gradient, pressure_pads[-1])[1](-upstream)[0]
        source_grad = jnp.zeros_like(upstream[0])
        for sweep_number in reversed(range(SWEEPS)):
            pressure_grad = fold_wrap(pad_grad, 1)
            source_grad = source_grad - 0.25 * pressure_grad
            if sweep_number > 0:
                pad_grad = jax.vjp(neighbours, pressure_pads[sweep_number - 1])[1](0.25 * pressure_grad)[0]
        moved_grad = upstream + fold_wrap(jax.vjp(divergence, velocity_pad)[1](source_grad)[0], 1)

        def back_block(carry, block_index, extended=extended, moved_grad=moved_grad):
            pad_total, grad_one, grad_two, grad_three = carry
            start = block_index * 8
            part = lax.dynamic_slice_in_dim(extended, start, 12, 1)
            part_up = lax.dynamic_slice_in_dim(moved_grad, start, 8, 1)
            part_grad, grads = advance_back(part, first_weight, second_weight, third_weight, part_up)
            region = lax.dynamic_slice_in_dim(pad_total, start, 12, 1)
            pad_total = lax.dynamic_update_slice_in_dim(pad_total, region + part_grad, start, 1)
            return ((pad_total, grad_one + grads[0], grad_two + grads[1], grad_three + grads[2]), None)
        carry, unused_out = lax.scan(back_block, (jnp.zeros_like(extended), totals[0], totals[1], totals[2]), block_ids)
        totals = (carry[1], carry[2], carry[3])
        upstream = fold_wrap(carry[0], 2)
    factor = gradient_gain / math.sqrt(row_total * col_total)
    return (current, totals[0] * factor, totals[1] * factor, totals[2] * factor)
```

```python
import functools
import math

import jax
import jax.numpy as jnp
from jax import lax
from jax.experimental import pallas as pl
from jax.experimental.pallas import tpu as pltpu
from jax.sharding import PartitionSpec as P

STEPS = 4
SWEEPS = 3
CHANNELS = 64
TAPS = 18
COEFS = 32
LANES = 128
HALO = 48

time_step = 0.1
viscosity = 0.2
correction_gain = 0.25
gradient_gain = 10.0

GELU_SCALE = math.sqrt(2.0 / math.pi)
GELU_CUBE = 0.044715

RANGE = (-1, 0, 1, 2)


def shift(plane, row, col):
    if row:
        plane = pltpu.roll(plane, (-row) % plane.shape[0], 0)
    if col:
        plane = pltpu.roll(plane, (-col) % plane.shape[1], 1)
    return plane


def gelu_pair(x):
    square = x * x
    t = jnp.tanh(x * (GELU_SCALE + (GELU_SCALE * GELU_CUBE) * square))
    half = 0.5 * x
    slope = (0.5 + 0.5 * t) + (half * (1.0 - t * t)) * (
        GELU_SCALE + (3.0 * GELU_SCALE * GELU_CUBE) * square
    )
    return half + half * t, slope


def neighbours(p):
    return (shift(p, 1, 0) + shift(p, -1, 0)) + (shift(p, 0, 1) + shift(p, 0, -1))


def dot(a, b):
    return jnp.dot(a, b, preferred_element_type=jnp.float32)


def dot_cells(a, b):
    return lax.dot_general(a, b, (((1,), (1,)), ((), ())), preferred_element_type=jnp.float32)


def kernel(
    core,
    chunk_rows,
    gathered,
    w1,
    w2,
    w3,
    w1t,
    w2t,
    w3t,
    velocity,
    grads,
    s_all,
    up,
    st,
    wt,
    qs,
    xs,
    co,
    x_all,
    a1_all,
    a2_all,
    g1_all,
    g2_all,
    g_first,
    g_second,
    g_third,
):
    height = s_all.shape[2]
    chunks = height // chunk_rows
    cells = chunk_rows * LANES
    z = lax.axis_index("rows")

    lane = lax.broadcasted_iota(jnp.int32, (8, LANES), 1) + (core * z - HALO)
    own = (lane >= 0) & (lane < LANES)
    amount = lax.rem(HALO - core * z + 4 * LANES, LANES)
    for i, k in enumerate((0, 2, 1, 3)):
        row = pl.multiple_of(8 * (z ^ k), 8)
        for c in range(4):
            mine = pltpu.roll(gathered[i, 0, c], amount, 1)
            other = pltpu.roll(gathered[i, 1, c], amount, 1)
            tile = jnp.where(own, mine, other)
            if c < 2:
                s_all[0, c, pl.ds(row, 8), :] = tile
            else:
                up[c - 2, pl.ds(row, 8), :] = tile

    xs[...] = jnp.zeros_like(xs)
    g_first[...] = jnp.zeros_like(g_first)
    g_second[...] = jnp.zeros_like(g_second)
    g_third[...] = jnp.zeros_like(g_third)

    def forward(step, carry):
        s = [s_all[step, c] for c in range(2)]
        for c in range(2):
            for a in RANGE:
                line = shift(s[c], a, 0)
                for b in RANGE:
                    plane = shift(line, 0, b)
                    st[step, c * 16 + (a + 1) * 4 + (b + 1)] = plane
                    if a < 2 and b < 2:
                        xs[pl.ds(c * 9 + (a + 1) * 3 + (b + 1), height, stride=32), :] = plane

        def chunk(index, carry):
            base = index * (chunk_rows * 32)
            x = jnp.concatenate(
                [xs[pl.ds(base + 32 * r, 32), :] for r in range(chunk_rows)], axis=1
            ).astype(jnp.bfloat16)
            at = pl.ds(pl.multiple_of(index * cells, cells), cells)
            x_all[step, :, at] = x
            act, slope = gelu_pair(dot(w1[...], x))
            act = act.astype(jnp.bfloat16)
            a1_all[step, :, at] = act
            g1_all[step, :, at] = slope
            act, slope = gelu_pair(dot(w2[...], act))
            act = act.astype(jnp.bfloat16)
            a2_all[step, :, at] = act
            g2_all[step, :, at] = slope
            out = dot(w3[...], act)
            for r in range(chunk_rows):
                co[pl.ds(base + 32 * r, 32), :] = out[:, r * LANES : (r + 1) * LANES]
            return carry

        lax.fori_loop(0, chunks, chunk, 0)

        q = [[None, None], [None, None]]
        for f in range(2):
            total = None
            for t in range(16):
                raw = co[pl.ds(f * 16 + t, height, stride=32), :]
                total = raw if total is None else total + raw
            mean = (correction_gain / 16.0) * total
            for t in range(16):
                raw = co[pl.ds(f * 16 + t, height, stride=32), :]
                weight = correction_gain * raw - mean
                if t in ((5, 9), (5, 6))[f]:
                    weight = weight + 0.5
                wt[step, f * 16 + t] = weight
                for c in range(2):
                    term = weight * st[step, c * 16 + t]
                    q[f][c] = term if q[f][c] is None else q[f][c] + term
        speed = [0.5 * (s[0] + shift(s[0], 1, 0)), 0.5 * (s[1] + shift(s[1], 0, 1))]
        moved = []
        for c in range(2):
            for f in range(2):
                qs[step, f * 2 + c] = q[f][c]
            rows, cols = speed[0] * q[0][c], speed[1] * q[1][c]
            transport = (rows - shift(rows, -1, 0)) + (cols - shift(cols, 0, -1))
            moved.append(
                s[c]
                - time_step * transport
                + time_step * viscosity * (neighbours(s[c]) - 4.0 * s[c])
            )
        source = 0.5 * (
            (shift(moved[0], 1, 0) - shift(moved[0], -1, 0))
            + (shift(moved[1], 0, 1) - shift(moved[1], 0, -1))
        )
        pressure = -0.25 * source
        for _ in range(SWEEPS - 1):
            pressure = 0.25 * (neighbours(pressure) - source)
        s_all[step + 1, 0] = moved[0] - 0.5 * (shift(pressure, 1, 0) - shift(pressure, -1, 0))
        s_all[step + 1, 1] = moved[1] - 0.5 * (shift(pressure, 0, 1) - shift(pressure, 0, -1))
        return carry

    lax.fori_loop(0, STEPS, forward, 0)
    velocity[...] = s_all[STEPS]

    column = lax.broadcasted_iota(jnp.int32, (1, cells), 1) % LANES
    inside = (column >= HALO) & (column < HALO + core)

    def backward(count, carry):
        step = STEPS - 1 - count
        u = [up[c] for c in range(2)]
        s = [s_all[step, c] for c in range(2)]
        p_bar = 0.5 * (
            (shift(u[0], 1, 0) - shift(u[0], -1, 0)) + (shift(u[1], 0, 1) - shift(u[1], 0, -1))
        )
        source_bar = -0.25 * p_bar
        for _ in range(SWEEPS - 1):
            p_bar = 0.25 * neighbours(p_bar)
            source_bar = source_bar - 0.25 * p_bar
        half = 0.5 * source_bar
        m_bar = [
            u[0] + (shift(half, -1, 0) - shift(half, 1, 0)),
            u[1] + (shift(half, 0, -1) - shift(half, 0, 1)),
        ]
        speed = [0.5 * (s[0] + shift(s[0], 1, 0)), 0.5 * (s[1] + shift(s[1], 0, 1))]
        speed_bar = [None, None]
        q_bar = [[None, None], [None, None]]
        for c in range(2):
            flux_bar = [
                time_step * (shift(m_bar[c], 1, 0) - m_bar[c]),
                time_step * (shift(m_bar[c], 0, 1) - m_bar[c]),
            ]
            for f in range(2):
                q_bar[f][c] = speed[f] * flux_bar[f]
                term = qs[step, f * 2 + c] * flux_bar[f]
                speed_bar[f] = term if c == 0 else speed_bar[f] + term
            up[c] = m_bar[c] + time_step * viscosity * (neighbours(m_bar[c]) - 4.0 * m_bar[c])
        up[0] = up[0] + 0.5 * (speed_bar[0] + shift(speed_bar[0], -1, 0))
        up[1] = up[1] + 0.5 * (speed_bar[1] + shift(speed_bar[1], 0, -1))

        for f in range(2):
            total = None
            for t in range(16):
                w_bar = q_bar[f][0] * st[step, t] + q_bar[f][1] * st[step, 16 + t]
                total = w_bar if total is None else total + w_bar
            mean = (1.0 / 16.0) * total
            for t in range(16):
                w_bar = q_bar[f][0] * st[step, t] + q_bar[f][1] * st[step, 16 + t]
                co[pl.ds(f * 16 + t, height, stride=32), :] = correction_gain * (w_bar - mean)

        def chunk(index, carry):
            base = index * (chunk_rows * 32)
            at = pl.ds(pl.multiple_of(index * cells, cells), cells)
            third = jnp.concatenate(
                [co[pl.ds(base + 32 * r, 32), :] for r in range(chunk_rows)], axis=1
            )
            zero = jnp.zeros((), jnp.float32)
            back = third.astype(jnp.bfloat16)
            kept = jnp.where(inside, third, zero).astype(jnp.bfloat16)
            g_third[...] += dot_cells(kept, a2_all[step, :, at])
            second = dot(w3t[...], back) * g2_all[step, :, at]
            back = second.astype(jnp.bfloat16)
            kept = jnp.where(inside, second, zero).astype(jnp.bfloat16)
            g_second[...] += dot_cells(kept, a1_all[step, :, at])
            first = dot(w2t[...], back) * g1_all[step, :, at]
            back = first.astype(jnp.bfloat16)
            kept = jnp.where(inside, first, zero).astype(jnp.bfloat16)
            g_first[...] += dot_cells(kept, x_all[step, :, at])
            out = dot(w1t[...], back)
            for r in range(chunk_rows):
                xs[pl.ds(base + 32 * r, 32), :] = out[:, r * LANES : (r + 1) * LANES]
            return carry

        lax.fori_loop(0, chunks, chunk, 0)

        for c in range(2):
            s_bar = up[c]
            for b in RANGE:
                column_sum = None
                for a in RANGE:
                    t = (a + 1) * 4 + (b + 1)
                    y = wt[step, t] * q_bar[0][c] + wt[step, 16 + t] * q_bar[1][c]
                    if a < 2 and b < 2:
                        y = y + xs[pl.ds(c * 9 + (a + 1) * 3 + (b + 1), height, stride=32), :]
                    y = shift(y, -a, 0)
                    column_sum = y if column_sum is None else column_sum + y
                s_bar = s_bar + shift(column_sum, 0, -b)
            up[c] = s_bar
        return carry

    lax.fori_loop(0, STEPS, backward, 0)
    grads[:, 0:64] = g_second[...]
    grads[:, 64:96] = g_first[...]
    grads[0:32, 96:128] = g_third[:, 0:32]
    grads[32:64, 96:128] = g_third[:, 32:64]


def strip_call(height, core, chunk_rows, gathered, weights):
    cells = height * LANES
    f32, bf16 = jnp.float32, jnp.bfloat16
    vmem = pl.BlockSpec(memory_space=pltpu.VMEM)
    return pl.pallas_call(
        functools.partial(kernel, core, chunk_rows),
        out_shape=(
            jax.ShapeDtypeStruct((2, height, LANES), f32),
            jax.ShapeDtypeStruct((CHANNELS, LANES), f32),
        ),
        in_specs=[vmem] * 7,
        out_specs=(vmem, vmem),
        scratch_shapes=[
            pltpu.VMEM((STEPS + 1, 2, height, LANES), f32),
            pltpu.VMEM((2, height, LANES), f32),
            pltpu.VMEM((STEPS, 32, height, LANES), f32),
            pltpu.VMEM((STEPS, 32, height, LANES), f32),
            pltpu.VMEM((STEPS, 4, height, LANES), f32),
            pltpu.VMEM((height * 32, LANES), f32),
            pltpu.VMEM((height * 32, LANES), f32),
            pltpu.VMEM((STEPS, 32, cells), bf16),
            pltpu.VMEM((STEPS, CHANNELS, cells), bf16),
            pltpu.VMEM((STEPS, CHANNELS, cells), bf16),
            pltpu.VMEM((STEPS, CHANNELS, cells), f32),
            pltpu.VMEM((STEPS, CHANNELS, cells), f32),
            pltpu.VMEM((CHANNELS, 32), f32),
            pltpu.VMEM((CHANNELS, CHANNELS), f32),
            pltpu.VMEM((COEFS, CHANNELS), f32),
        ],
        compiler_params=pltpu.CompilerParams(vmem_limit_bytes=48 * 1024 * 1024),
    )(gathered, *weights)


def swap(x, axis, bit):
    return lax.ppermute(x, axis, [(i, i ^ bit) for i in range(lax.axis_size(axis))])


def strips(state, cotangent, first_weight, second_weight, third_weight):
    row_count = lax.axis_size("rows")
    block_count = lax.axis_size(("cols", "section"))
    height = row_count * state.shape[1]
    core = LANES // row_count
    z = lax.axis_index("rows")

    tile = jnp.concatenate([state, cotangent], 0)
    pairs = []
    for row in range(row_count):
        step = 1 if row < row_count // 2 else block_count - 1
        for block in range(block_count):
            pairs.append((row * block_count + block, row * block_count + (block + step) % block_count))
    held = jnp.stack([tile, swap(tile, "rows", 2)])
    other = lax.ppermute(held, ("rows", "cols", "section"), pairs)
    held = jnp.stack([held, other], 1)
    held = jnp.concatenate([held, swap(held, "rows", 1)], 0)

    first = jnp.pad(first_weight, ((0, 0), (0, 32 - TAPS)))
    velocity, grads = strip_call(
        height,
        core,
        4,
        held,
        (first, second_weight, third_weight, first.T, second_weight.T, third_weight.T),
    )

    grads = grads + swap(grads, "section", 1)
    grads = grads + swap(grads, "cols", 1)
    strip = velocity[:, :, HALO : HALO + core].reshape(4, 16, core)
    strip = strip.transpose(1, 0, 2).reshape(16, LANES)
    sent = jnp.concatenate([grads, strip], 0)
    got = swap(sent, "rows", 1)
    sent = jnp.concatenate([sent[:64] + got[:64], sent[64:], got[64:]], 0)
    got = swap(sent, "rows", 2)
    grads = sent[:64] + got[:64]
    parts = jnp.concatenate([sent[64:], got[64:]], 0).reshape(4, 16, 4, core)
    parts = parts.transpose(0, 2, 1, 3).reshape(4, 2, 4, 8, core)
    mine = lax.dynamic_index_in_dim(parts, z, 2, keepdims=False)
    tile_out = jnp.concatenate(
        [lax.dynamic_index_in_dim(mine, z ^ k, 0, keepdims=False) for k in range(4)], -1
    )
    factor = gradient_gain / math.sqrt(height * LANES * block_count)
    grads = grads * factor
    return (
        tile_out,
        grads[:, 64 : 64 + TAPS],
        grads[:, 0:64],
        jnp.concatenate([grads[:32, 96:], grads[32:, 96:]], 1),
    )


def with_halo(block, sides, width):
    for axis, dim in sides:
        count = lax.axis_size(axis)
        forward = [(i, i + 1) for i in range(count - 1)]
        forward.append((count - 1, 0))
        backward = [(target, source) for source, target in forward]
        low = lax.ppermute(
            lax.slice_in_dim(block, block.shape[dim] - width, None, axis=dim), axis, forward
        )
        high = lax.ppermute(lax.slice_in_dim(block, 0, width, axis=dim), axis, backward)
        block = jnp.concatenate([low, block, high], axis=dim)
    return block


def base_table():
    return jnp.array(
        [
            [0.5 if tap_number in (5, 9) else 0.0 for tap_number in range(16)],
            [0.5 if tap_number in (5, 6) else 0.0 for tap_number in range(16)],
        ],
        jnp.float32,
    )


def patches(extended):
    height = extended.shape[1] - 3
    breadth = extended.shape[2] - 3
    pieces = [
        extended[:, offset_row : offset_row + height, offset_col : offset_col + breadth]
        for offset_row in range(3)
        for offset_col in range(3)
    ]
    return jnp.stack(pieces, 1).reshape(18, height * breadth)


def network(inputs, first_weight, second_weight, third_weight):
    rounded = inputs.astype(jnp.bfloat16)
    first_pre = jnp.dot(first_weight, rounded, preferred_element_type=jnp.float32)
    first_act = jax.nn.gelu(first_pre).astype(jnp.bfloat16)
    second_pre = jnp.dot(second_weight, first_act, preferred_element_type=jnp.float32)
    second_act = jax.nn.gelu(second_pre).astype(jnp.bfloat16)
    coefficients = jnp.dot(third_weight, second_act, preferred_element_type=jnp.float32)
    return (rounded, first_pre, first_act, second_pre, second_act, coefficients)


def physics(extended, coefficients):
    height = extended.shape[1] - 3
    breadth = extended.shape[2] - 3
    inner_rows = height - 1
    inner_cols = breadth - 1
    raw_output = coefficients.reshape(2, 16, height, breadth)
    weights = base_table()[:, :, None, None] + correction_gain * (
        raw_output - jnp.mean(raw_output, axis=1, keepdims=True)
    )
    stencil = jnp.stack(
        [
            extended[:, offset_row : offset_row + height, offset_col : offset_col + breadth]
            for offset_row in range(4)
            for offset_col in range(4)
        ],
        0,
    )
    face_rows = jnp.sum(weights[0][:, None] * stencil, axis=0)
    face_cols = jnp.sum(weights[1][:, None] * stencil, axis=0)
    speed_rows = 0.5 * (
        extended[0, 1 : 1 + height, 1 : 1 + breadth] + extended[0, 2 : 2 + height, 1 : 1 + breadth]
    )
    speed_cols = 0.5 * (
        extended[1, 1 : 1 + height, 1 : 1 + breadth] + extended[1, 1 : 1 + height, 2 : 2 + breadth]
    )
    flux_rows = speed_rows * face_rows
    flux_cols = speed_cols * face_cols
    transport = (
        flux_rows[:, 1:, 1:] - flux_rows[:, :-1, 1:] + flux_cols[:, 1:, 1:] - flux_cols[:, 1:, :-1]
    )
    centre = extended[:, 2 : 2 + inner_rows, 2 : 2 + inner_cols]
    laplace = (
        extended[:, 1 : 1 + inner_rows, 2 : 2 + inner_cols]
        + extended[:, 3 : 3 + inner_rows, 2 : 2 + inner_cols]
        + extended[:, 2 : 2 + inner_rows, 1 : 1 + inner_cols]
        + extended[:, 2 : 2 + inner_rows, 3 : 3 + inner_cols]
        - 4.0 * centre
    )
    return centre - time_step * transport + time_step * viscosity * laplace


def advance(extended, first_weight, second_weight, third_weight):
    outputs = network(patches(extended), first_weight, second_weight, third_weight)
    return physics(extended, outputs[5])


def gelu_back(preact, upstream):
    return jax.vjp(jax.nn.gelu, preact)[1](upstream)[0]


def advance_back(extended, first_weight, second_weight, third_weight, upstream):
    inputs, patch_back = jax.vjp(patches, extended)
    rounded, first_pre, first_act, second_pre, second_act, coefficients = network(
        inputs, first_weight, second_weight, third_weight
    )
    advanced, physics_back = jax.vjp(physics, extended, coefficients)
    extended_grad, coef_grad = physics_back(upstream)
    coef_round = coef_grad.astype(jnp.bfloat16)
    outer = (((1,), (1,)), ((), ()))
    inner = (((0,), (0,)), ((), ()))
    third_grad = lax.dot_general(coef_round, second_act, outer, preferred_element_type=jnp.float32)
    second_back = gelu_back(
        second_pre,
        lax.dot_general(third_weight, coef_round, inner, preferred_element_type=jnp.float32),
    ).astype(jnp.bfloat16)
    second_grad = lax.dot_general(second_back, first_act, outer, preferred_element_type=jnp.float32)
    first_back = gelu_back(
        first_pre,
        lax.dot_general(second_weight, second_back, inner, preferred_element_type=jnp.float32),
    ).astype(jnp.bfloat16)
    first_grad = lax.dot_general(first_back, rounded, outer, preferred_element_type=jnp.float32)
    input_grad = lax.dot_general(
        first_weight, first_back, inner, preferred_element_type=jnp.float32
    )
    extended_grad = extended_grad + patch_back(input_grad)[0]
    return (extended_grad, (first_grad, second_grad, third_grad))


def divergence(padded):
    return 0.5 * (
        padded[0, 2:, 1:-1] - padded[0, :-2, 1:-1] + (padded[1, 1:-1, 2:] - padded[1, 1:-1, :-2])
    )


def padded_neighbours(padded):
    return padded[2:, 1:-1] + padded[:-2, 1:-1] + padded[1:-1, 2:] + padded[1:-1, :-2]


def pressure_gradient(padded):
    return jnp.stack(
        [0.5 * (padded[2:, 1:-1] - padded[:-2, 1:-1]), 0.5 * (padded[1:-1, 2:] - padded[1:-1, :-2])]
    )


def fold_rims(returned, margin):
    row_count = returned.shape[-2] - 4 * margin
    col_count = returned.shape[-1] - 4 * margin
    leading = [(0, 0)] * (returned.ndim - 1)
    middle = (
        returned[..., 2 * margin : 2 * margin + col_count]
        + jnp.pad(returned[..., :margin], leading + [(0, col_count - margin)])
        + jnp.pad(returned[..., -margin:], leading + [(col_count - margin, 0)])
    )
    leading_rows = [(0, 0)] * (returned.ndim - 2)
    return (
        middle[..., 2 * margin : 2 * margin + row_count, :]
        + jnp.pad(middle[..., :margin, :], leading_rows + [(0, row_count - margin), (0, 0)])
        + jnp.pad(middle[..., -margin:, :], leading_rows + [(row_count - margin, 0), (0, 0)])
    )


def tiles(state, cotangent, first_weight, second_weight, third_weight):
    weights = (first_weight, second_weight, third_weight)
    current = state
    saved = []
    for step_number in range(STEPS):
        extended = with_halo(current, (("rows", 1), (("cols", "section"), 2)), 2)
        moved = advance(extended, *weights)
        velocity_pad = with_halo(moved, (("rows", 1), (("cols", "section"), 2)), 1)
        source = divergence(velocity_pad)
        pressure = -0.25 * source
        pressure_pads = []
        for sweep_number in range(SWEEPS):
            padded = with_halo(pressure, (("rows", 0), (("cols", "section"), 1)), 1)
            pressure_pads.append(padded)
            if sweep_number < SWEEPS - 1:
                pressure = 0.25 * (padded_neighbours(padded) - source)
        saved.append((extended, velocity_pad, pressure_pads))
        current = moved - pressure_gradient(pressure_pads[-1])
    upstream = cotangent
    totals = (
        jnp.zeros(first_weight.shape, jnp.float32),
        jnp.zeros(second_weight.shape, jnp.float32),
        jnp.zeros(third_weight.shape, jnp.float32),
    )
    for step_number in reversed(range(STEPS)):
        record = saved[step_number]
        velocity_pad = record[1]
        pressure_pads = record[2]
        pad_grad = jax.vjp(pressure_gradient, pressure_pads[-1])[1](-upstream)[0]
        source_grad = jnp.zeros_like(upstream[0])
        for sweep_number in reversed(range(SWEEPS)):
            returned = with_halo(pad_grad, (("rows", 0), (("cols", "section"), 1)), 1)
            pressure_grad = fold_rims(returned, 1)
            source_grad = source_grad - 0.25 * pressure_grad
            if sweep_number > 0:
                pad_grad = jax.vjp(padded_neighbours, pressure_pads[sweep_number - 1])[1](
                    0.25 * pressure_grad
                )[0]
        velocity_grad = jax.vjp(divergence, velocity_pad)[1](source_grad)[0]
        returned_velocity = with_halo(velocity_grad, (("rows", 1), (("cols", "section"), 2)), 1)
        moved_grad = upstream + fold_rims(returned_velocity, 1)
        extended_grad, grads = advance_back(
            record[0], first_weight, second_weight, third_weight, moved_grad
        )
        totals = (totals[0] + grads[0], totals[1] + grads[1], totals[2] + grads[2])
        if step_number > 0:
            returned_state = with_halo(extended_grad, (("rows", 1), (("cols", "section"), 2)), 2)
            upstream = fold_rims(returned_state, 2)
    totals = lax.psum((totals[0], totals[1], totals[2]), ("rows", "cols", "section"))
    cell_total = (
        state.shape[1] * state.shape[2] * lax.axis_size("rows") * lax.axis_size(("cols", "section"))
    )
    factor = gradient_gain / math.sqrt(cell_total)
    return (current, totals[0] * factor, totals[1] * factor, totals[2] * factor)


def solution(mesh):
    def program(state, *rest):
        fits = (
            lax.axis_size("rows") == 4
            and state.shape[1] == 8
            and state.shape[2] == LANES
            and lax.axis_size(("cols", "section")) >= 2
            and lax.axis_size("section") == 2
            and lax.axis_size("cols") == 2
        )
        return (strips if fits else tiles)(state, *rest)

    return jax.shard_map(
        program,
        mesh=mesh,
        in_specs=(
            P(None, ("groups", "rows"), ("cols", "section")),
            P(None, ("groups", "rows"), ("cols", "section")),
            P(),
            P(),
            P(),
        ),
        out_specs=(
            P(None, ("groups", "rows"), ("cols", "section")),
            P("groups", None),
            P("groups", None),
            P("groups", None),
        ),
        check_vma=False,
    )
```

```python
import functools
import math

import jax
import jax.numpy as jnp
from jax import lax
from jax.experimental import pallas as pl
from jax.experimental.pallas import tpu as pltpu
from jax.sharding import PartitionSpec as P

STEPS = 4
SWEEPS = 3
CHANNELS = 64
TAPS = 18
COEFS = 32
LANES = 128
HALF = LANES // 2
MARGIN = 16
PACKED = 16

time_step = 0.1
viscosity = 0.2
correction_gain = 0.25
gradient_gain = 10.0

GELU_SCALE = math.sqrt(2.0 / math.pi)
GELU_CUBE = 0.044715


def shift(plane, row, col):
    if row:
        plane = pltpu.roll(plane, (-row) % plane.shape[0], 0)
    if col:
        plane = pltpu.roll(plane, (-col) % plane.shape[1], 1)
    return plane


def swap_halves(x):
    return pltpu.roll(x, HALF, 1)


def neighbours(p):
    return (shift(p, 1, 0) + shift(p, -1, 0)) + (shift(p, 0, 1) + shift(p, 0, -1))


def dot(a, b):
    return jnp.dot(a, b, preferred_element_type=jnp.float32)


def dot_cells(a, b):
    return lax.dot_general(a, b, (((1,), (1,)), ((), ())), preferred_element_type=jnp.float32)


def gelu_half(h, with_slope):
    a, b = 2.0 * GELU_SCALE, 8.0 * GELU_SCALE * GELU_CUBE
    square = h * h
    t = jnp.tanh(h * (a + b * square))
    e = 1.0 + t
    act = h * e
    if not with_slope:
        return act, None
    return act, e * (1.0 + (h * (1.0 - t)) * (a + (3.0 * b) * square))


def pick_taps(shape, place_dim):
    place = lax.broadcasted_iota(jnp.int32, shape, place_dim)
    tap = lax.broadcasted_iota(jnp.int32, shape, 1 - place_dim)
    row, col = (tap // 4) % 4, tap % 4
    wanted = (tap // 16) * 9 + row * 3 + col
    return jnp.where((place == wanted) & (row < 3) & (col < 3), 1.0, 0.0)


def kernel(
    core,
    factor,
    gathered,
    w1_in,
    w2_in,
    w3_in,
    velocity,
    grads,
    s_all,
    up,
    qs,
    uu,
    ub,
    qp,
    bq,
    x_all,
    a1_all,
    a2_all,
    g1_all,
    g2_all,
    cf,
    w1,
    w1t,
    w2,
    w2t,
    w3,
    w3t,
    g_first,
    g_second,
    g_third,
):
    f32, bf16 = jnp.float32, jnp.bfloat16
    height = 2 * PACKED
    z = lax.axis_index("rows")
    left = lax.broadcasted_iota(jnp.int32, (PACKED, LANES), 1) < HALF

    lane = lax.broadcasted_iota(jnp.int32, (8, LANES), 1)
    column = jnp.where(lane < LANES - 32, lane, lane - LANES) + (core * z - MARGIN)
    own = (column >= 0) & (column < LANES)
    amount = lax.rem(MARGIN - core * z + 4 * LANES, LANES)
    for i, k in enumerate((0, 2, 1, 3)):
        row = pl.multiple_of(8 * (z ^ k), 8)
        for c in range(4):
            mine = pltpu.roll(gathered[i, 0, c], amount, 1)
            other = pltpu.roll(gathered[i, 1, c], amount, 1)
            tile = jnp.where(own, mine, other)
            if c < 2:
                s_all[0, c, pl.ds(row, 8), :] = tile
            else:
                up[c - 2, pl.ds(row, 8), :] = tile

    spread = dot(pick_taps((32, TAPS), 1).astype(bf16), w1_in[...])
    w1[...] = (0.5 * spread.T).astype(bf16)
    w1t[...] = spread.astype(bf16)
    wide = w2_in[...].astype(f32)
    w2[...] = (0.5 * wide).astype(bf16)
    w2t[...] = (0.5 * wide.T).astype(bf16)
    wide = w3_in[...].astype(f32)
    w3t[...] = ((0.5 * correction_gain) * wide.T).astype(bf16)
    for f in range(2):
        rows = wide[16 * f : 16 * f + 16]
        rows = correction_gain * (rows - jnp.mean(rows, axis=0, keepdims=True))
        high = rows.astype(bf16)
        w3[16 * f : 16 * f + 16, 0:64] = high
        w3[16 * f : 16 * f + 16, 64:128] = (rows - high.astype(f32)).astype(bf16)

    g_first[...] = jnp.zeros_like(g_first)
    g_second[...] = jnp.zeros_like(g_second)
    g_third[...] = jnp.zeros_like(g_third)

    def pack(plane, part):
        turned = swap_halves(plane)
        if part == 0:
            return jnp.where(left, plane[:PACKED], turned[PACKED:])
        return jnp.where(left, turned[:PACKED], plane[PACKED:])

    def unpack(inner, outer):
        if outer is None:
            return jnp.concatenate([inner, swap_halves(inner)], 0)
        return jnp.concatenate(
            [
                jnp.where(left, inner, swap_halves(outer)),
                jnp.where(left, swap_halves(inner), outer),
            ],
            0,
        )

    def stencil(step, part, c, ah, r):
        at = 8 * (r + 2 * ah)
        return uu[step, part, c, at : at + 8, :]

    def forward(step, last):
        s = [s_all[step, c] for c in range(2)]
        for c in range(2):
            for al in range(2):
                line = shift(s[c], al, 0)
                for b in range(4):
                    plane = shift(line, 0, b - 1)
                    for part in range(2):
                        uu[step, part, c, pl.ds(8 + 4 * al + b, PACKED, stride=8), :] = pack(
                            plane, part
                        )
            for part in range(2):
                uu[step, part, c, 0:8, :] = swap_halves(uu[step, part, c, 128:136, :])
                uu[step, part, c, 136:144, :] = swap_halves(uu[step, part, c, 8:16, :])

        for part in range(2):
            keep = part == 0 or last
            slot = step if part == 0 else STEPS
            x = jnp.concatenate(
                [
                    jnp.concatenate(
                        [stencil(step, part, c, ah, r) for c in range(2) for ah in range(2)], 0
                    ).astype(bf16)
                    for r in range(PACKED)
                ],
                1,
            )
            act, slope = gelu_half(dot(w1[...], x), keep)
            act = act.astype(bf16)
            if part == 0:
                x_all[slot] = x
                a1_all[slot] = act
            if keep:
                g1_all[slot] = slope
            act, slope = gelu_half(dot(w2[...], act), keep)
            act = act.astype(bf16)
            if part == 0:
                a2_all[slot] = act
            if keep:
                g2_all[slot] = slope
            out = dot(w3[...], jnp.concatenate([act, act], 0))
            if keep:
                cf[slot] = out
            for r in range(PACKED):
                weight = out[:, r * LANES : (r + 1) * LANES]
                for c in range(2):
                    lower = stencil(step, part, c, 0, r)
                    upper = stencil(step, part, c, 1, r)
                    for f in range(2):
                        qp[part, 2 * f + c, 8 * r : 8 * r + 8, :] = (
                            weight[16 * f : 16 * f + 8] * lower
                            + weight[16 * f + 8 : 16 * f + 16] * upper
                        )

        def reduced(part, which):
            terms = [qp[part, which, pl.ds(j, PACKED, stride=8), :] for j in range(8)]
            while len(terms) > 1:
                terms = [a + b for a, b in zip(terms[::2], terms[1::2])]
            return terms[0]

        moved = []
        near = [s[0] + shift(s[0], 1, 0), s[1] + shift(s[1], 0, 1)]
        for c in range(2):
            flux = []
            for f in range(2):
                mean = 0.5 * (s[c] + (shift(s[c], 1, 0) if f == 0 else shift(s[c], 0, 1)))
                q = mean + unpack(reduced(0, 2 * f + c), reduced(1, 2 * f + c))
                qs[step, 2 * f + c] = q
                flux.append((0.5 * near[f]) * q)
            transport = (flux[0] - shift(flux[0], -1, 0)) + (flux[1] - shift(flux[1], 0, -1))
            moved.append(
                s[c]
                - time_step * transport
                + time_step * viscosity * (neighbours(s[c]) - 4.0 * s[c])
            )
        source = 0.5 * (
            (shift(moved[0], 1, 0) - shift(moved[0], -1, 0))
            + (shift(moved[1], 0, 1) - shift(moved[1], 0, -1))
        )
        pressure = -0.25 * source
        for _ in range(SWEEPS - 1):
            pressure = 0.25 * (neighbours(pressure) - source)
        s_all[step + 1, 0] = moved[0] - 0.5 * (shift(pressure, 1, 0) - shift(pressure, -1, 0))
        s_all[step + 1, 1] = moved[1] - 0.5 * (shift(pressure, 0, 1) - shift(pressure, 0, -1))

    def backward(step, full):
        u = [up[c] for c in range(2)]
        s = [s_all[step, c] for c in range(2)]
        p_bar = 0.5 * (
            (shift(u[0], 1, 0) - shift(u[0], -1, 0)) + (shift(u[1], 0, 1) - shift(u[1], 0, -1))
        )
        source_bar = -0.25 * p_bar
        for _ in range(SWEEPS - 1):
            p_bar = 0.25 * neighbours(p_bar)
            source_bar = source_bar - 0.25 * p_bar
        half = 0.5 * source_bar
        m_bar = [
            u[0] + (shift(half, -1, 0) - shift(half, 1, 0)),
            u[1] + (shift(half, 0, -1) - shift(half, 0, 1)),
        ]
        speed = [0.5 * (s[0] + shift(s[0], 1, 0)), 0.5 * (s[1] + shift(s[1], 0, 1))]
        box = []
        for c in range(2):
            pair = s[c] + shift(s[c], 0, 1)
            line = shift(pair, 0, -1) + shift(pair, 0, 1)
            pair = line + shift(line, 1, 0)
            box.append((1.0 / 16.0) * (shift(pair, -1, 0) + shift(pair, 1, 0)))
        speed_bar = [None, None]
        s_bar = []
        mean = [None, None]
        parts = (0, 1) if full else (0,)
        for c in range(2):
            flux_bar = [
                time_step * (shift(m_bar[c], 1, 0) - m_bar[c]),
                time_step * (shift(m_bar[c], 0, 1) - m_bar[c]),
            ]
            total = m_bar[c] + time_step * viscosity * (neighbours(m_bar[c]) - 4.0 * m_bar[c])
            for f in range(2):
                q_bar = speed[f] * flux_bar[f]
                for part in parts:
                    bq[part, 2 * f + c] = pack(q_bar, part)
                term = q_bar * box[c]
                mean[f] = term if c == 0 else mean[f] + term
                term = qs[step, 2 * f + c] * flux_bar[f]
                speed_bar[f] = term if c == 0 else speed_bar[f] + term
                half = 0.5 * q_bar
                total = total + (half + (shift(half, -1, 0) if f == 0 else shift(half, 0, -1)))
            s_bar.append(total)
        half = 0.5 * speed_bar[0]
        s_bar[0] = s_bar[0] + (half + shift(half, -1, 0))
        half = 0.5 * speed_bar[1]
        s_bar[1] = s_bar[1] + (half + shift(half, 0, -1))
        for f in range(2):
            for part in parts:
                bq[part, 4 + f] = pack(mean[f], part)

        for part in parts:
            slot = step if part == 0 else STEPS

            def spread_row(which, r):
                return jnp.broadcast_to(bq[part, which, r : r + 1, :], (8, LANES))

            third = []
            for r in range(PACKED):
                pieces = []
                for f in range(2):
                    q0, q1, m = (spread_row(w, r) for w in (2 * f, 2 * f + 1, 4 + f))
                    for ah in range(2):
                        pieces.append(
                            (q0 * stencil(step, part, 0, ah, r) + q1 * stencil(step, part, 1, ah, r))
                            - m
                        )
                third.append(jnp.concatenate(pieces, 0).astype(bf16))
            third = jnp.concatenate(third, 1)
            second = (dot(w3t[...], third) * g2_all[slot]).astype(bf16)
            first = (dot(w2t[...], second) * g1_all[slot]).astype(bf16)
            if part == 0:
                cells = lax.broadcasted_iota(jnp.int32, (1, PACKED * LANES), 1) % HALF
                inside = (cells >= MARGIN) & (cells < MARGIN + core)
                zero = jnp.zeros((), bf16)
                g_third[...] += dot_cells(jnp.where(inside, third, zero), a2_all[slot])
                g_second[...] += dot_cells(jnp.where(inside, second, zero), a1_all[slot])
                g_first[...] += dot_cells(jnp.where(inside, first, zero), x_all[slot])
            out = dot(w1t[...], first)

            y = {}
            for r in range(PACKED):
                lanes = slice(r * LANES, (r + 1) * LANES)
                for c in range(2):
                    q0, q1 = spread_row(c, r), spread_row(2 + c, r)
                    for ah in range(2):
                        y[c, ah, r] = (
                            cf[slot, 8 * ah : 8 * ah + 8, lanes] * q0
                            + cf[slot, 16 + 8 * ah : 24 + 8 * ah, lanes] * q1
                        ) + out[16 * c + 8 * ah : 16 * c + 8 * ah + 8, lanes]
            for c in range(2):
                rows = []
                for m in range(PACKED):
                    value = y[c, 0, m + 1] if m + 1 < PACKED else swap_halves(y[c, 0, 0])
                    other = y[c, 1, m - 1] if m > 0 else swap_halves(y[c, 1, PACKED - 1])
                    rows.append(value + other)
                ub[part, c, 0:8, :] = swap_halves(rows[PACKED - 1])
                for m in range(PACKED):
                    ub[part, c, 8 + 8 * m : 16 + 8 * m, :] = rows[m]

        for c in range(2):
            total = s_bar[c]
            for b in range(4):
                planes = [
                    ub[part, c, pl.ds(8 + b, PACKED, stride=8), :]
                    + ub[part, c, pl.ds(4 + b, PACKED, stride=8), :]
                    for part in parts
                ]
                plane = unpack(planes[0], planes[1] if full else None)
                total = total + shift(plane, 0, 1 - b)
            up[c] = total

    for step in range(STEPS):
        forward(step, step == STEPS - 1)
    group = lax.broadcasted_iota(jnp.int32, (8, LANES), 1) // core
    for c in range(2):
        strip = jnp.zeros((8, LANES), f32)
        for k in range(LANES // core):
            rows = s_all[STEPS, c, 8 * k : 8 * k + 8, :]
            strip = jnp.where(group == k, pltpu.roll(rows, (core * k - MARGIN) % LANES, 1), strip)
        velocity[8 * c : 8 * c + 8, :] = strip
    for step in reversed(range(STEPS)):
        backward(step, step == STEPS - 1)
    grads[:, 0:64] = factor * g_second[...]
    first = lax.dot_general(
        pick_taps((TAPS, 32), 0),
        factor * g_first[...],
        (((1,), (1,)), ((), ())),
        precision=lax.Precision.HIGHEST,
        preferred_element_type=f32,
    )
    grads[0:TAPS, 64:128] = first
    grads[TAPS:32, 64:128] = jnp.zeros((32 - TAPS, CHANNELS), f32)
    grads[32:64, 64:128] = (factor * correction_gain) * g_third[...]


def strip_call(core, factor, gathered, weights):
    cells = PACKED * LANES
    f32, bf16 = jnp.float32, jnp.bfloat16
    vmem = pl.BlockSpec(memory_space=pltpu.VMEM)
    return pl.pallas_call(
        functools.partial(kernel, core, factor),
        out_shape=(
            jax.ShapeDtypeStruct((16, LANES), f32),
            jax.ShapeDtypeStruct((CHANNELS, LANES), f32),
        ),
        in_specs=[vmem] * 4,
        out_specs=(vmem, vmem),
        scratch_shapes=[
            pltpu.VMEM((STEPS + 1, 2, 2 * PACKED, LANES), f32),
            pltpu.VMEM((2, 2 * PACKED, LANES), f32),
            pltpu.VMEM((STEPS, 4, 2 * PACKED, LANES), f32),
            pltpu.VMEM((STEPS, 2, 2, 8 * (PACKED + 2), LANES), f32),
            pltpu.VMEM((2, 2, 8 * (PACKED + 1), LANES), f32),
            pltpu.VMEM((2, 4, 8 * PACKED, LANES), f32),
            pltpu.VMEM((2, 6, PACKED, LANES), f32),
            pltpu.VMEM((STEPS, 32, cells), bf16),
            pltpu.VMEM((STEPS, CHANNELS, cells), bf16),
            pltpu.VMEM((STEPS, CHANNELS, cells), bf16),
            pltpu.VMEM((STEPS + 1, CHANNELS, cells), f32),
            pltpu.VMEM((STEPS + 1, CHANNELS, cells), f32),
            pltpu.VMEM((STEPS + 1, COEFS, cells), f32),
            pltpu.VMEM((CHANNELS, 32), bf16),
            pltpu.VMEM((32, CHANNELS), bf16),
            pltpu.VMEM((CHANNELS, CHANNELS), bf16),
            pltpu.VMEM((CHANNELS, CHANNELS), bf16),
            pltpu.VMEM((COEFS, 2 * CHANNELS), bf16),
            pltpu.VMEM((CHANNELS, COEFS), bf16),
            pltpu.VMEM((CHANNELS, 32), f32),
            pltpu.VMEM((CHANNELS, CHANNELS), f32),
            pltpu.VMEM((COEFS, CHANNELS), f32),
        ],
        compiler_params=pltpu.CompilerParams(vmem_limit_bytes=48 * 1024 * 1024),
    )(gathered, *weights)


def finish(core, sent, got, tile, first, second, third):
    z = lax.axis_index("rows")
    group = lax.broadcasted_iota(jnp.int32, (8, LANES), 1) // core
    for c in range(2):
        total = jnp.zeros((8, LANES), jnp.float32)
        for k, (ref, at) in enumerate(((sent, 64), (sent, 80), (got, 64), (got, 80))):
            strip = ref[at + 8 * c : at + 8 * c + 8, :]
            owner = z ^ k
            turned = pltpu.roll(strip, lax.rem(core * (owner - z) + LANES, LANES), 1)
            total = jnp.where(group == owner, turned, total)
        tile[c] = total
    grads = sent[0:64, :] + got[0:64, :]
    first[...] = grads[0:TAPS, 64:]
    second[...] = grads[:, 0:64]
    third[...] = grads[32:, 64:]


def finish_call(core, sent, got):
    vmem = pl.BlockSpec(memory_space=pltpu.VMEM)
    f32 = jnp.float32
    return pl.pallas_call(
        functools.partial(finish, core),
        out_shape=(
            jax.ShapeDtypeStruct((2, 8, LANES), f32),
            jax.ShapeDtypeStruct((TAPS, CHANNELS), f32),
            jax.ShapeDtypeStruct((CHANNELS, CHANNELS), f32),
            jax.ShapeDtypeStruct((COEFS, CHANNELS), f32),
        ),
        in_specs=[vmem] * 2,
        out_specs=(vmem,) * 4,
        compiler_params=pltpu.CompilerParams(vmem_limit_bytes=8 * 1024 * 1024),
    )(sent, got)


def swap(x, axis, bit):
    return lax.ppermute(x, axis, [(i, i ^ bit) for i in range(lax.axis_size(axis))])


def strips(state, cotangent, first_weight, second_weight, third_weight):
    row_count = lax.axis_size("rows")
    block_count = lax.axis_size(("cols", "section"))
    height = row_count * state.shape[1]
    core = LANES // row_count
    z = lax.axis_index("rows")

    tile = jnp.concatenate([state, cotangent], 0)
    pairs = []
    for row in range(row_count):
        step = 1 if row < row_count // 2 else block_count - 1
        for block in range(block_count):
            pairs.append((row * block_count + block, row * block_count + (block + step) % block_count))
    held = jnp.stack([tile, swap(tile, "rows", 2)])
    other = lax.ppermute(held, ("rows", "cols", "section"), pairs)
    held = jnp.stack([held, other], 1)
    held = jnp.concatenate([held, swap(held, "rows", 1)], 0)

    factor = gradient_gain / math.sqrt(height * LANES * block_count)
    velocity, grads = strip_call(
        core, factor, held, (first_weight.T, second_weight, third_weight)
    )

    grads = grads + swap(grads, "section", 1)
    grads = grads + swap(grads, "cols", 1)
    sent = jnp.concatenate([grads, velocity], 0)
    got = swap(sent, "rows", 1)
    sent = jnp.concatenate([sent[:64] + got[:64], sent[64:], got[64:]], 0)
    tile, first, second, third = finish_call(core, sent, swap(sent, "rows", 2))
    return tile, first.T, second, third


def with_halo(block, sides, width):
    for axis, dim in sides:
        count = lax.axis_size(axis)
        forward = [(i, i + 1) for i in range(count - 1)]
        forward.append((count - 1, 0))
        backward = [(target, source) for source, target in forward]
        low = lax.ppermute(
            lax.slice_in_dim(block, block.shape[dim] - width, None, axis=dim), axis, forward
        )
        high = lax.ppermute(lax.slice_in_dim(block, 0, width, axis=dim), axis, backward)
        block = jnp.concatenate([low, block, high], axis=dim)
    return block


def base_table():
    return jnp.array(
        [
            [0.5 if tap_number in (5, 9) else 0.0 for tap_number in range(16)],
            [0.5 if tap_number in (5, 6) else 0.0 for tap_number in range(16)],
        ],
        jnp.float32,
    )


def patches(extended):
    height = extended.shape[1] - 3
    breadth = extended.shape[2] - 3
    pieces = [
        extended[:, offset_row : offset_row + height, offset_col : offset_col + breadth]
        for offset_row in range(3)
        for offset_col in range(3)
    ]
    return jnp.stack(pieces, 1).reshape(18, height * breadth)


def network(inputs, first_weight, second_weight, third_weight):
    rounded = inputs.astype(jnp.bfloat16)
    first_pre = jnp.dot(first_weight, rounded, preferred_element_type=jnp.float32)
    first_act = jax.nn.gelu(first_pre).astype(jnp.bfloat16)
    second_pre = jnp.dot(second_weight, first_act, preferred_element_type=jnp.float32)
    second_act = jax.nn.gelu(second_pre).astype(jnp.bfloat16)
    coefficients = jnp.dot(third_weight, second_act, preferred_element_type=jnp.float32)
    return (rounded, first_pre, first_act, second_pre, second_act, coefficients)


def physics(extended, coefficients):
    height = extended.shape[1] - 3
    breadth = extended.shape[2] - 3
    inner_rows = height - 1
    inner_cols = breadth - 1
    raw_output = coefficients.reshape(2, 16, height, breadth)
    weights = base_table()[:, :, None, None] + correction_gain * (
        raw_output - jnp.mean(raw_output, axis=1, keepdims=True)
    )
    stencil = jnp.stack(
        [
            extended[:, offset_row : offset_row + height, offset_col : offset_col + breadth]
            for offset_row in range(4)
            for offset_col in range(4)
        ],
        0,
    )
    face_rows = jnp.sum(weights[0][:, None] * stencil, axis=0)
    face_cols = jnp.sum(weights[1][:, None] * stencil, axis=0)
    speed_rows = 0.5 * (
        extended[0, 1 : 1 + height, 1 : 1 + breadth] + extended[0, 2 : 2 + height, 1 : 1 + breadth]
    )
    speed_cols = 0.5 * (
        extended[1, 1 : 1 + height, 1 : 1 + breadth] + extended[1, 1 : 1 + height, 2 : 2 + breadth]
    )
    flux_rows = speed_rows * face_rows
    flux_cols = speed_cols * face_cols
    transport = (
        flux_rows[:, 1:, 1:] - flux_rows[:, :-1, 1:] + flux_cols[:, 1:, 1:] - flux_cols[:, 1:, :-1]
    )
    centre = extended[:, 2 : 2 + inner_rows, 2 : 2 + inner_cols]
    laplace = (
        extended[:, 1 : 1 + inner_rows, 2 : 2 + inner_cols]
        + extended[:, 3 : 3 + inner_rows, 2 : 2 + inner_cols]
        + extended[:, 2 : 2 + inner_rows, 1 : 1 + inner_cols]
        + extended[:, 2 : 2 + inner_rows, 3 : 3 + inner_cols]
        - 4.0 * centre
    )
    return centre - time_step * transport + time_step * viscosity * laplace


def advance(extended, first_weight, second_weight, third_weight):
    outputs = network(patches(extended), first_weight, second_weight, third_weight)
    return physics(extended, outputs[5])


def gelu_back(preact, upstream):
    return jax.vjp(jax.nn.gelu, preact)[1](upstream)[0]


def advance_back(extended, first_weight, second_weight, third_weight, upstream):
    inputs, patch_back = jax.vjp(patches, extended)
    rounded, first_pre, first_act, second_pre, second_act, coefficients = network(
        inputs, first_weight, second_weight, third_weight
    )
    advanced, physics_back = jax.vjp(physics, extended, coefficients)
    extended_grad, coef_grad = physics_back(upstream)
    coef_round = coef_grad.astype(jnp.bfloat16)
    outer = (((1,), (1,)), ((), ()))
    inner = (((0,), (0,)), ((), ()))
    third_grad = lax.dot_general(coef_round, second_act, outer, preferred_element_type=jnp.float32)
    second_back = gelu_back(
        second_pre,
        lax.dot_general(third_weight, coef_round, inner, preferred_element_type=jnp.float32),
    ).astype(jnp.bfloat16)
    second_grad = lax.dot_general(second_back, first_act, outer, preferred_element_type=jnp.float32)
    first_back = gelu_back(
        first_pre,
        lax.dot_general(second_weight, second_back, inner, preferred_element_type=jnp.float32),
    ).astype(jnp.bfloat16)
    first_grad = lax.dot_general(first_back, rounded, outer, preferred_element_type=jnp.float32)
    input_grad = lax.dot_general(
        first_weight, first_back, inner, preferred_element_type=jnp.float32
    )
    extended_grad = extended_grad + patch_back(input_grad)[0]
    return (extended_grad, (first_grad, second_grad, third_grad))


def divergence(padded):
    return 0.5 * (
        padded[0, 2:, 1:-1] - padded[0, :-2, 1:-1] + (padded[1, 1:-1, 2:] - padded[1, 1:-1, :-2])
    )


def padded_neighbours(padded):
    return padded[2:, 1:-1] + padded[:-2, 1:-1] + padded[1:-1, 2:] + padded[1:-1, :-2]


def pressure_gradient(padded):
    return jnp.stack(
        [0.5 * (padded[2:, 1:-1] - padded[:-2, 1:-1]), 0.5 * (padded[1:-1, 2:] - padded[1:-1, :-2])]
    )


def fold_rims(returned, margin):
    row_count = returned.shape[-2] - 4 * margin
    col_count = returned.shape[-1] - 4 * margin
    leading = [(0, 0)] * (returned.ndim - 1)
    middle = (
        returned[..., 2 * margin : 2 * margin + col_count]
        + jnp.pad(returned[..., :margin], leading + [(0, col_count - margin)])
        + jnp.pad(returned[..., -margin:], leading + [(col_count - margin, 0)])
    )
    leading_rows = [(0, 0)] * (returned.ndim - 2)
    return (
        middle[..., 2 * margin : 2 * margin + row_count, :]
        + jnp.pad(middle[..., :margin, :], leading_rows + [(0, row_count - margin), (0, 0)])
        + jnp.pad(middle[..., -margin:, :], leading_rows + [(row_count - margin, 0), (0, 0)])
    )


def tiles(state, cotangent, first_weight, second_weight, third_weight):
    weights = (first_weight, second_weight, third_weight)
    current = state
    saved = []
    for step_number in range(STEPS):
        extended = with_halo(current, (("rows", 1), (("cols", "section"), 2)), 2)
        moved = advance(extended, *weights)
        velocity_pad = with_halo(moved, (("rows", 1), (("cols", "section"), 2)), 1)
        source = divergence(velocity_pad)
        pressure = -0.25 * source
        pressure_pads = []
        for sweep_number in range(SWEEPS):
            padded = with_halo(pressure, (("rows", 0), (("cols", "section"), 1)), 1)
            pressure_pads.append(padded)
            if sweep_number < SWEEPS - 1:
                pressure = 0.25 * (padded_neighbours(padded) - source)
        saved.append((extended, velocity_pad, pressure_pads))
        current = moved - pressure_gradient(pressure_pads[-1])
    upstream = cotangent
    totals = (
        jnp.zeros(first_weight.shape, jnp.float32),
        jnp.zeros(second_weight.shape, jnp.float32),
        jnp.zeros(third_weight.shape, jnp.float32),
    )
    for step_number in reversed(range(STEPS)):
        record = saved[step_number]
        velocity_pad = record[1]
        pressure_pads = record[2]
        pad_grad = jax.vjp(pressure_gradient, pressure_pads[-1])[1](-upstream)[0]
        source_grad = jnp.zeros_like(upstream[0])
        for sweep_number in reversed(range(SWEEPS)):
            returned = with_halo(pad_grad, (("rows", 0), (("cols", "section"), 1)), 1)
            pressure_grad = fold_rims(returned, 1)
            source_grad = source_grad - 0.25 * pressure_grad
            if sweep_number > 0:
                pad_grad = jax.vjp(padded_neighbours, pressure_pads[sweep_number - 1])[1](
                    0.25 * pressure_grad
                )[0]
        velocity_grad = jax.vjp(divergence, velocity_pad)[1](source_grad)[0]
        returned_velocity = with_halo(velocity_grad, (("rows", 1), (("cols", "section"), 2)), 1)
        moved_grad = upstream + fold_rims(returned_velocity, 1)
        extended_grad, grads = advance_back(
            record[0], first_weight, second_weight, third_weight, moved_grad
        )
        totals = (totals[0] + grads[0], totals[1] + grads[1], totals[2] + grads[2])
        if step_number > 0:
            returned_state = with_halo(extended_grad, (("rows", 1), (("cols", "section"), 2)), 2)
            upstream = fold_rims(returned_state, 2)
    totals = lax.psum((totals[0], totals[1], totals[2]), ("rows", "cols", "section"))
    cell_total = (
        state.shape[1] * state.shape[2] * lax.axis_size("rows") * lax.axis_size(("cols", "section"))
    )
    factor = gradient_gain / math.sqrt(cell_total)
    return (current, totals[0] * factor, totals[1] * factor, totals[2] * factor)


def solution(mesh):
    def program(state, *rest):
        fits = (
            lax.axis_size("rows") == 4
            and state.shape[1] == 8
            and state.shape[2] == LANES
            and lax.axis_size(("cols", "section")) >= 2
            and lax.axis_size("section") == 2
            and lax.axis_size("cols") == 2
        )
        return (strips if fits else tiles)(state, *rest)

    return jax.shard_map(
        program,
        mesh=mesh,
        in_specs=(
            P(None, ("groups", "rows"), ("cols", "section")),
            P(None, ("groups", "rows"), ("cols", "section")),
            P(),
            P(),
            P(),
        ),
        out_specs=(
            P(None, ("groups", "rows"), ("cols", "section")),
            P("groups", None),
            P("groups", None),
            P("groups", None),
        ),
        check_vma=False,
    )
```

```python
import functools
import math

import jax
import jax.numpy as jnp
from jax import lax
from jax.experimental import pallas as pl
from jax.experimental.pallas import tpu as pltpu
from jax.sharding import PartitionSpec as P

STEPS = 4
SWEEPS = 3
CHANNELS = 64
TAPS = 18
COEFS = 32
LANES = 128
HALF = LANES // 2
PACKED = 16
SIDE = 32

time_step = 0.1
viscosity = 0.2
correction_gain = 0.25
gradient_gain = 10.0

GELU_SCALE = math.sqrt(2.0 / math.pi)
GELU_CUBE = 0.044715


def shift(plane, row, col):
    if row:
        plane = pltpu.roll(plane, (-row) % plane.shape[0], 0)
    if col:
        plane = pltpu.roll(plane, (-col) % plane.shape[1], 1)
    return plane


def swap_halves(x):
    return pltpu.roll(x, HALF, 1)


def neighbours(p):
    return (shift(p, 1, 0) + shift(p, -1, 0)) + (shift(p, 0, 1) + shift(p, 0, -1))


def pressure_of(source):
    one = shift(source, 0, 1) + shift(source, 0, -1)
    two = shift(source, 0, 2) + shift(source, 0, -2)
    mixed = 4.0 * source + 2.0 * one
    rows = (shift(mixed, 1, 0) + shift(mixed, -1, 0)) + (shift(source, 2, 0) + shift(source, -2, 0))
    return (-1.0 / 64.0) * (((20.0 * source + 4.0 * one) + two) + rows)


def dot(a, b):
    return jnp.dot(a, b, preferred_element_type=jnp.float32)


def dot_cells(a, b):
    return lax.dot_general(a, b, (((1,), (1,)), ((), ())), preferred_element_type=jnp.float32)


def gelu_half(h, with_slope):
    a, b = 2.0 * GELU_SCALE, 8.0 * GELU_SCALE * GELU_CUBE
    square = h * h
    t = jnp.tanh(h * (a + b * square))
    e = 1.0 + t
    act = h * e
    if not with_slope:
        return act, None
    return act, e * (1.0 + (h * (1.0 - t)) * (a + (3.0 * b) * square))


def pick_taps(shape, place_dim):
    place = lax.broadcasted_iota(jnp.int32, shape, place_dim)
    tap = lax.broadcasted_iota(jnp.int32, shape, 1 - place_dim)
    row, col = (tap // 4) % 4, tap % 4
    wanted = (tap // 16) * 9 + row * 3 + col
    return jnp.where((place == wanted) & (row < 3) & (col < 3), 1.0, 0.0)


def prepare(w1_in, w2_in, w3_in, w1, w1t, w2, w2t, w3, w3t):
    f32, bf16 = jnp.float32, jnp.bfloat16
    spread = dot(pick_taps((32, TAPS), 1).astype(bf16), w1_in[...])
    w1[...] = (0.5 * spread.T).astype(bf16)
    w1t[...] = spread.astype(bf16)
    wide = w2_in[...].astype(f32)
    w2[...] = (0.5 * wide).astype(bf16)
    w2t[...] = (0.5 * wide.T).astype(bf16)
    wide = w3_in[...].astype(f32)
    w3t[...] = ((0.5 * correction_gain) * wide.T).astype(bf16)
    for f in range(2):
        rows = wide[16 * f : 16 * f + 16]
        rows = correction_gain * (rows - jnp.mean(rows, axis=0, keepdims=True))
        high = rows.astype(bf16)
        w3[16 * f : 16 * f + 16, 0:64] = high
        w3[16 * f : 16 * f + 16, 64:128] = (rows - high.astype(f32)).astype(bf16)


def prepare_call(w1_in, w2_in, w3_in):
    vmem = pl.BlockSpec(memory_space=pltpu.VMEM)
    shapes = ((CHANNELS, 32), (32, CHANNELS), (CHANNELS, CHANNELS), (CHANNELS, CHANNELS))
    shapes += ((COEFS, 2 * CHANNELS), (CHANNELS, COEFS))
    return pl.pallas_call(
        prepare,
        out_shape=tuple(jax.ShapeDtypeStruct(shape, jnp.bfloat16) for shape in shapes),
        in_specs=[vmem] * 3,
        out_specs=(vmem,) * 6,
        compiler_params=pltpu.CompilerParams(vmem_limit_bytes=8 * 1024 * 1024),
        cost_estimate=pl.CostEstimate(flops=1 << 20, bytes_accessed=1 << 16, transcendentals=0),
    )(w1_in, w2_in, w3_in)


def kernel(
    factor,
    own_near,
    own_far,
    other_near,
    other_far,
    w1,
    w1t,
    w2,
    w2t,
    w3,
    w3t,
    mine,
    theirs,
    grads,
    s_wide,
    s_all,
    up,
    qs,
    uu,
    ub,
    qp,
    bq,
    x_all,
    a1_all,
    a2_all,
    g1_all,
    g2_all,
    cf,
):
    f32, bf16 = jnp.float32, jnp.bfloat16
    z = lax.axis_index("rows")
    left = lax.broadcasted_iota(jnp.int32, (PACKED, LANES), 1) < HALF

    lane = lax.broadcasted_iota(jnp.int32, (8, LANES), 1)
    odd = (lane * 0 + z) % 2 == 1
    for k in range(4):
        row = pl.multiple_of(8 * (z ^ k), 8)
        own, other = ((own_near, other_near), (own_far, other_far))[k // 2]
        for c in range(4):
            here = own[k % 2, c]
            there = other[k % 2, c]
            turned = swap_halves(here)
            upper = jnp.where(odd, jnp.where(lane < HALF, turned, swap_halves(there)), here)
            lower = jnp.where(odd, turned, there)
            narrow = jnp.where(lane < LANES - SIDE, upper, lower)
            if c < 2:
                s_wide[c, pl.ds(row, 8), 0:LANES] = upper
                s_wide[c, pl.ds(row, 8), LANES : 2 * LANES] = lower
                s_all[0, c, pl.ds(row, 8), :] = narrow
            else:
                up[c - 2, pl.ds(row, 8), :] = narrow

    def pack(plane, part):
        plane = plane[:, LANES:] if part == 2 else plane[:, :LANES]
        turned = swap_halves(plane)
        if part == 0:
            return jnp.where(left, plane[:PACKED], turned[PACKED:])
        return jnp.where(left, turned[:PACKED], plane[PACKED:])

    def unpack(pieces):
        inner, outer = pieces[0], pieces[1]
        plane = jnp.concatenate(
            [
                jnp.where(left, inner, swap_halves(outer)),
                jnp.where(left, swap_halves(inner), outer),
            ],
            0,
        )
        if len(pieces) == 2:
            return plane
        lower = jnp.concatenate([swap_halves(pieces[2]), pieces[2]], 0)
        return jnp.concatenate([plane, lower], 1)

    def stencil(step, part, c, ah, r):
        at = 8 * (r + 2 * ah)
        return uu[step, part, c, at : at + 8, :]

    def slot_of(step, part):
        return step if part == 0 else STEPS - 1 + step

    def forward(step):
        parts = range(3) if step == 0 else range(2)
        s = [s_wide[c] if step == 0 else s_all[step, c] for c in range(2)]
        for c in range(2):
            for al in range(2):
                line = shift(s[c], al, 0)
                for b in range(4):
                    plane = shift(line, 0, b - 1)
                    for part in parts:
                        uu[step, part, c, pl.ds(8 + 4 * al + b, PACKED, stride=8), :] = pack(
                            plane, part
                        )
            for part in parts:
                uu[step, part, c, 0:8, :] = swap_halves(uu[step, part, c, 128:136, :])
                uu[step, part, c, 136:144, :] = swap_halves(uu[step, part, c, 8:16, :])

        for part in parts:
            keep = part == 0 or step > 0
            slot = slot_of(step, part)
            x = jnp.concatenate(
                [
                    jnp.concatenate(
                        [stencil(step, part, c, ah, r) for c in range(2) for ah in range(2)], 0
                    ).astype(bf16)
                    for r in range(PACKED)
                ],
                1,
            )
            act, slope = gelu_half(dot(w1[...], x), keep)
            act = act.astype(bf16)
            if part == 0:
                x_all[slot] = x
                a1_all[slot] = act
            if keep:
                g1_all[slot] = slope
            act, slope = gelu_half(dot(w2[...], act), keep)
            act = act.astype(bf16)
            if part == 0:
                a2_all[slot] = act
            if keep:
                g2_all[slot] = slope
            out = dot(w3[...], jnp.concatenate([act, act], 0))
            if keep and step > 0:
                cf[slot] = out
            for r in range(PACKED):
                weight = out[:, r * LANES : (r + 1) * LANES]
                for c in range(2):
                    lower = stencil(step, part, c, 0, r)
                    upper = stencil(step, part, c, 1, r)
                    for f in range(2):
                        qp[part, 2 * f + c, 8 * r : 8 * r + 8, :] = (
                            weight[16 * f : 16 * f + 8] * lower
                            + weight[16 * f + 8 : 16 * f + 16] * upper
                        )

        def reduced(part, which):
            terms = [qp[part, which, pl.ds(j, PACKED, stride=8), :] for j in range(8)]
            while len(terms) > 1:
                terms = [a + b for a, b in zip(terms[::2], terms[1::2])]
            return terms[0]

        moved = []
        near = [s[0] + shift(s[0], 1, 0), s[1] + shift(s[1], 0, 1)]
        for c in range(2):
            flux = []
            for f in range(2):
                mean = 0.5 * (s[c] + (shift(s[c], 1, 0) if f == 0 else shift(s[c], 0, 1)))
                q = mean + unpack([reduced(part, 2 * f + c) for part in parts])
                if step > 0:
                    qs[step, 2 * f + c] = q
                flux.append((0.5 * near[f]) * q)
            transport = (flux[0] - shift(flux[0], -1, 0)) + (flux[1] - shift(flux[1], 0, -1))
            moved.append(
                s[c]
                - time_step * transport
                + time_step * viscosity * (neighbours(s[c]) - 4.0 * s[c])
            )
        source = 0.5 * (
            (shift(moved[0], 1, 0) - shift(moved[0], -1, 0))
            + (shift(moved[1], 0, 1) - shift(moved[1], 0, -1))
        )
        pressure = pressure_of(source)
        after = [
            moved[0] - 0.5 * (shift(pressure, 1, 0) - shift(pressure, -1, 0)),
            moved[1] - 0.5 * (shift(pressure, 0, 1) - shift(pressure, 0, -1)),
        ]
        for c in range(2):
            if step == 0:
                column = lax.broadcasted_iota(jnp.int32, (2 * PACKED, LANES), 1)
                after[c] = jnp.where(
                    column < LANES - SIDE, after[c][:, :LANES], after[c][:, LANES:]
                )
            s_all[step + 1, c] = after[c]

    def backward(step, total):
        u = [up[c] for c in range(2)]
        s = [s_all[step, c] for c in range(2)]
        p_bar = 0.5 * (
            (shift(u[0], 1, 0) - shift(u[0], -1, 0)) + (shift(u[1], 0, 1) - shift(u[1], 0, -1))
        )
        half = 0.5 * pressure_of(p_bar)
        m_bar = [
            u[0] + (shift(half, -1, 0) - shift(half, 1, 0)),
            u[1] + (shift(half, 0, -1) - shift(half, 0, 1)),
        ]
        speed = [0.5 * (s[0] + shift(s[0], 1, 0)), 0.5 * (s[1] + shift(s[1], 0, 1))]
        box = []
        for c in range(2):
            pair = s[c] + shift(s[c], 0, 1)
            line = shift(pair, 0, -1) + shift(pair, 0, 1)
            pair = line + shift(line, 1, 0)
            box.append((1.0 / 16.0) * (shift(pair, -1, 0) + shift(pair, 1, 0)))
        speed_bar = [None, None]
        s_bar = []
        mean = [None, None]
        parts = range(2) if step > 0 else range(1)
        for c in range(2):
            flux_bar = [
                time_step * (shift(m_bar[c], 1, 0) - m_bar[c]),
                time_step * (shift(m_bar[c], 0, 1) - m_bar[c]),
            ]
            if step > 0:
                kept = m_bar[c] + time_step * viscosity * (neighbours(m_bar[c]) - 4.0 * m_bar[c])
            for f in range(2):
                q_bar = speed[f] * flux_bar[f]
                for part in parts:
                    bq[part, 2 * f + c] = pack(q_bar, part)
                term = q_bar * box[c]
                mean[f] = term if c == 0 else mean[f] + term
                if step > 0:
                    term = qs[step, 2 * f + c] * flux_bar[f]
                    speed_bar[f] = term if c == 0 else speed_bar[f] + term
                    half = 0.5 * q_bar
                    kept = kept + (half + (shift(half, -1, 0) if f == 0 else shift(half, 0, -1)))
            if step > 0:
                s_bar.append(kept)
        if step > 0:
            half = 0.5 * speed_bar[0]
            s_bar[0] = s_bar[0] + (half + shift(half, -1, 0))
            half = 0.5 * speed_bar[1]
            s_bar[1] = s_bar[1] + (half + shift(half, 0, -1))
        for f in range(2):
            for part in parts:
                bq[part, 4 + f] = pack(mean[f], part)

        for part in parts:
            slot = slot_of(step, part)

            def spread_row(which, r):
                return jnp.broadcast_to(bq[part, which, r : r + 1, :], (8, LANES))

            third = []
            for r in range(PACKED):
                pieces = []
                for f in range(2):
                    q0, q1, m = (spread_row(w, r) for w in (2 * f, 2 * f + 1, 4 + f))
                    for ah in range(2):
                        pieces.append(
                            (q0 * stencil(step, part, 0, ah, r) + q1 * stencil(step, part, 1, ah, r))
                            - m
                        )
                third.append(jnp.concatenate(pieces, 0).astype(bf16))
            third = jnp.concatenate(third, 1)
            second = (dot(w3t[...], third) * g2_all[slot]).astype(bf16)
            first = (dot(w2t[...], second) * g1_all[slot]).astype(bf16)
            if part == 0:
                terms = (
                    dot_cells(first, x_all[slot]),
                    dot_cells(second, a1_all[slot]),
                    dot_cells(third, a2_all[slot]),
                )
                total = terms if total is None else tuple(a + b for a, b in zip(total, terms))
            if step == 0:
                return total
            out = dot(w1t[...], first)

            y = {}
            for r in range(PACKED):
                lanes = slice(r * LANES, (r + 1) * LANES)
                for c in range(2):
                    q0, q1 = spread_row(c, r), spread_row(2 + c, r)
                    for ah in range(2):
                        y[c, ah, r] = (
                            cf[slot, 8 * ah : 8 * ah + 8, lanes] * q0
                            + cf[slot, 16 + 8 * ah : 24 + 8 * ah, lanes] * q1
                        ) + out[16 * c + 8 * ah : 16 * c + 8 * ah + 8, lanes]
            for c in range(2):
                rows = []
                for m in range(PACKED):
                    value = y[c, 0, m + 1] if m + 1 < PACKED else swap_halves(y[c, 0, 0])
                    before = y[c, 1, m - 1] if m > 0 else swap_halves(y[c, 1, PACKED - 1])
                    rows.append(value + before)
                ub[part, c, 0:8, :] = swap_halves(rows[PACKED - 1])
                for m in range(PACKED):
                    ub[part, c, 8 + 8 * m : 16 + 8 * m, :] = rows[m]

        for c in range(2):
            kept = s_bar[c]
            for b in range(4):
                plane = unpack(
                    [
                        ub[part, c, pl.ds(8 + b, PACKED, stride=8), :]
                        + ub[part, c, pl.ds(4 + b, PACKED, stride=8), :]
                        for part in parts
                    ]
                )
                kept = kept + shift(plane, 0, 1 - b)
            up[c] = kept
        return total

    for step in range(STEPS):
        forward(step)
    for ref, tile in ((mine, z), (theirs, z ^ 1)):
        first, second = (s_all[STEPS, c, pl.ds(pl.multiple_of(8 * tile, 8), 8), :] for c in range(2))
        ref[...] = jnp.where(lane < HALF, first, swap_halves(second))
    total = None
    for step in reversed(range(STEPS)):
        total = backward(step, total)
    grads[:, 0:64] = factor * total[1]
    first = lax.dot_general(
        pick_taps((TAPS, 32), 0),
        factor * total[0],
        (((1,), (1,)), ((), ())),
        precision=lax.Precision.HIGHEST,
        preferred_element_type=f32,
    )
    grads[0:TAPS, 64:128] = first
    grads[TAPS:32, 64:128] = jnp.zeros((32 - TAPS, CHANNELS), f32)
    grads[32:64, 64:128] = (factor * correction_gain) * total[2]


def strip_call(factor, pieces, weights):
    cells = PACKED * LANES
    f32, bf16 = jnp.float32, jnp.bfloat16
    vmem = pl.BlockSpec(memory_space=pltpu.VMEM)
    slots = 2 * STEPS - 1
    return pl.pallas_call(
        functools.partial(kernel, factor),
        out_shape=(
            jax.ShapeDtypeStruct((8, LANES), f32),
            jax.ShapeDtypeStruct((8, LANES), f32),
            jax.ShapeDtypeStruct((CHANNELS, LANES), f32),
        ),
        in_specs=[vmem] * 10,
        out_specs=(vmem,) * 3,
        scratch_shapes=[
            pltpu.VMEM((2, 2 * PACKED, 2 * LANES), f32),
            pltpu.VMEM((STEPS + 1, 2, 2 * PACKED, LANES), f32),
            pltpu.VMEM((2, 2 * PACKED, LANES), f32),
            pltpu.VMEM((STEPS, 4, 2 * PACKED, LANES), f32),
            pltpu.VMEM((STEPS, 3, 2, 8 * (PACKED + 2), LANES), f32),
            pltpu.VMEM((2, 2, 8 * (PACKED + 1), LANES), f32),
            pltpu.VMEM((3, 4, 8 * PACKED, LANES), f32),
            pltpu.VMEM((2, 6, PACKED, LANES), f32),
            pltpu.VMEM((STEPS, 32, cells), bf16),
            pltpu.VMEM((STEPS, CHANNELS, cells), bf16),
            pltpu.VMEM((STEPS, CHANNELS, cells), bf16),
            pltpu.VMEM((slots, CHANNELS, cells), f32),
            pltpu.VMEM((slots, CHANNELS, cells), f32),
            pltpu.VMEM((slots, COEFS, cells), f32),
        ],
        compiler_params=pltpu.CompilerParams(vmem_limit_bytes=48 * 1024 * 1024),
    )(*pieces, *weights)


def finish(sent, got, mine, tile, first, second, third):
    z = lax.axis_index("rows")
    lane = lax.broadcasted_iota(jnp.int32, (8, LANES), 1)
    odd = (lane * 0 + z) % 2 == 1
    near, far = mine[...], got[64:72, :]
    for c in range(2):
        here, there = (x if c == 0 else swap_halves(x) for x in (near, far))
        low = jnp.where(odd, there, here)
        high = jnp.where(odd, here, there)
        tile[c] = jnp.where(lane < HALF, low, swap_halves(high))
    grads = sent[0:64, :] + got[0:64, :]
    first[...] = grads[0:TAPS, 64:]
    second[...] = grads[:, 0:64]
    third[...] = grads[32:, 64:]


def finish_call(sent, got, mine):
    vmem = pl.BlockSpec(memory_space=pltpu.VMEM)
    f32 = jnp.float32
    return pl.pallas_call(
        finish,
        out_shape=(
            jax.ShapeDtypeStruct((2, 8, LANES), f32),
            jax.ShapeDtypeStruct((TAPS, CHANNELS), f32),
            jax.ShapeDtypeStruct((CHANNELS, CHANNELS), f32),
            jax.ShapeDtypeStruct((COEFS, CHANNELS), f32),
        ),
        in_specs=[vmem] * 3,
        out_specs=(vmem,) * 4,
        compiler_params=pltpu.CompilerParams(vmem_limit_bytes=8 * 1024 * 1024),
    )(sent, got, mine)


def swap(x, axis, bit):
    return lax.ppermute(x, axis, [(i, i ^ bit) for i in range(lax.axis_size(axis))])


def strips(state, cotangent, first_weight, second_weight, third_weight):
    row_count = lax.axis_size("rows")
    block_count = lax.axis_size(("cols", "section"))
    weights = prepare_call(first_weight.T, second_weight, third_weight)

    def beside(flip):
        pairs = []
        for row in range(row_count):
            step = 1 if row % 2 == 0 else block_count - 1
            for block in range(block_count):
                target = (row ^ flip) * block_count + (block + step) % block_count
                pairs.append((row * block_count + block, target))
        return pairs

    tile = jnp.concatenate([state, cotangent], 0)
    near = jnp.stack([tile, swap(tile, "rows", 1)])
    everyone = ("rows", "cols", "section")
    other_near = lax.ppermute(near, everyone, beside(0))
    other_far = lax.ppermute(near, everyone, beside(2))
    far = swap(near, "rows", 2)

    factor = gradient_gain / math.sqrt(row_count * state.shape[1] * LANES * block_count)
    mine, theirs, grads = strip_call(factor, (near, far, other_near, other_far), weights)

    grads = grads + swap(grads, "section", 1)
    grads = grads + swap(grads, "cols", 1)
    sent = jnp.concatenate([grads, theirs], 0)
    tile, first, second, third = finish_call(sent, swap(sent, "rows", 1), mine)
    return tile, first.T, second, third


def with_halo(block, sides, width):
    for axis, dim in sides:
        count = lax.axis_size(axis)
        forward = [(i, i + 1) for i in range(count - 1)]
        forward.append((count - 1, 0))
        backward = [(target, source) for source, target in forward]
        low = lax.ppermute(
            lax.slice_in_dim(block, block.shape[dim] - width, None, axis=dim), axis, forward
        )
        high = lax.ppermute(lax.slice_in_dim(block, 0, width, axis=dim), axis, backward)
        block = jnp.concatenate([low, block, high], axis=dim)
    return block


def base_table():
    return jnp.array(
        [
            [0.5 if tap_number in (5, 9) else 0.0 for tap_number in range(16)],
            [0.5 if tap_number in (5, 6) else 0.0 for tap_number in range(16)],
        ],
        jnp.float32,
    )


def patches(extended):
    height = extended.shape[1] - 3
    breadth = extended.shape[2] - 3
    pieces = [
        extended[:, offset_row : offset_row + height, offset_col : offset_col + breadth]
        for offset_row in range(3)
        for offset_col in range(3)
    ]
    return jnp.stack(pieces, 1).reshape(18, height * breadth)


def network(inputs, first_weight, second_weight, third_weight):
    rounded = inputs.astype(jnp.bfloat16)
    first_pre = jnp.dot(first_weight, rounded, preferred_element_type=jnp.float32)
    first_act = jax.nn.gelu(first_pre).astype(jnp.bfloat16)
    second_pre = jnp.dot(second_weight, first_act, preferred_element_type=jnp.float32)
    second_act = jax.nn.gelu(second_pre).astype(jnp.bfloat16)
    coefficients = jnp.dot(third_weight, second_act, preferred_element_type=jnp.float32)
    return (rounded, first_pre, first_act, second_pre, second_act, coefficients)


def physics(extended, coefficients):
    height = extended.shape[1] - 3
    breadth = extended.shape[2] - 3
    inner_rows = height - 1
    inner_cols = breadth - 1
    raw_output = coefficients.reshape(2, 16, height, breadth)
    weights = base_table()[:, :, None, None] + correction_gain * (
        raw_output - jnp.mean(raw_output, axis=1, keepdims=True)
    )
    stencil = jnp.stack(
        [
            extended[:, offset_row : offset_row + height, offset_col : offset_col + breadth]
            for offset_row in range(4)
            for offset_col in range(4)
        ],
        0,
    )
    face_rows = jnp.sum(weights[0][:, None] * stencil, axis=0)
    face_cols = jnp.sum(weights[1][:, None] * stencil, axis=0)
    speed_rows = 0.5 * (
        extended[0, 1 : 1 + height, 1 : 1 + breadth] + extended[0, 2 : 2 + height, 1 : 1 + breadth]
    )
    speed_cols = 0.5 * (
        extended[1, 1 : 1 + height, 1 : 1 + breadth] + extended[1, 1 : 1 + height, 2 : 2 + breadth]
    )
    flux_rows = speed_rows * face_rows
    flux_cols = speed_cols * face_cols
    transport = (
        flux_rows[:, 1:, 1:] - flux_rows[:, :-1, 1:] + flux_cols[:, 1:, 1:] - flux_cols[:, 1:, :-1]
    )
    centre = extended[:, 2 : 2 + inner_rows, 2 : 2 + inner_cols]
    laplace = (
        extended[:, 1 : 1 + inner_rows, 2 : 2 + inner_cols]
        + extended[:, 3 : 3 + inner_rows, 2 : 2 + inner_cols]
        + extended[:, 2 : 2 + inner_rows, 1 : 1 + inner_cols]
        + extended[:, 2 : 2 + inner_rows, 3 : 3 + inner_cols]
        - 4.0 * centre
    )
    return centre - time_step * transport + time_step * viscosity * laplace


def advance(extended, first_weight, second_weight, third_weight):
    outputs = network(patches(extended), first_weight, second_weight, third_weight)
    return physics(extended, outputs[5])


def gelu_back(preact, upstream):
    return jax.vjp(jax.nn.gelu, preact)[1](upstream)[0]


def advance_back(extended, first_weight, second_weight, third_weight, upstream):
    inputs, patch_back = jax.vjp(patches, extended)
    rounded, first_pre, first_act, second_pre, second_act, coefficients = network(
        inputs, first_weight, second_weight, third_weight
    )
    advanced, physics_back = jax.vjp(physics, extended, coefficients)
    extended_grad, coef_grad = physics_back(upstream)
    coef_round = coef_grad.astype(jnp.bfloat16)
    outer = (((1,), (1,)), ((), ()))
    inner = (((0,), (0,)), ((), ()))
    third_grad = lax.dot_general(coef_round, second_act, outer, preferred_element_type=jnp.float32)
    second_back = gelu_back(
        second_pre,
        lax.dot_general(third_weight, coef_round, inner, preferred_element_type=jnp.float32),
    ).astype(jnp.bfloat16)
    second_grad = lax.dot_general(second_back, first_act, outer, preferred_element_type=jnp.float32)
    first_back = gelu_back(
        first_pre,
        lax.dot_general(second_weight, second_back, inner, preferred_element_type=jnp.float32),
    ).astype(jnp.bfloat16)
    first_grad = lax.dot_general(first_back, rounded, outer, preferred_element_type=jnp.float32)
    input_grad = lax.dot_general(
        first_weight, first_back, inner, preferred_element_type=jnp.float32
    )
    extended_grad = extended_grad + patch_back(input_grad)[0]
    return (extended_grad, (first_grad, second_grad, third_grad))


def divergence(padded):
    return 0.5 * (
        padded[0, 2:, 1:-1] - padded[0, :-2, 1:-1] + (padded[1, 1:-1, 2:] - padded[1, 1:-1, :-2])
    )


def padded_neighbours(padded):
    return padded[2:, 1:-1] + padded[:-2, 1:-1] + padded[1:-1, 2:] + padded[1:-1, :-2]


def pressure_gradient(padded):
    return jnp.stack(
        [0.5 * (padded[2:, 1:-1] - padded[:-2, 1:-1]), 0.5 * (padded[1:-1, 2:] - padded[1:-1, :-2])]
    )


def fold_rims(returned, margin):
    row_count = returned.shape[-2] - 4 * margin
    col_count = returned.shape[-1] - 4 * margin
    leading = [(0, 0)] * (returned.ndim - 1)
    middle = (
        returned[..., 2 * margin : 2 * margin + col_count]
        + jnp.pad(returned[..., :margin], leading + [(0, col_count - margin)])
        + jnp.pad(returned[..., -margin:], leading + [(col_count - margin, 0)])
    )
    leading_rows = [(0, 0)] * (returned.ndim - 2)
    return (
        middle[..., 2 * margin : 2 * margin + row_count, :]
        + jnp.pad(middle[..., :margin, :], leading_rows + [(0, row_count - margin), (0, 0)])
        + jnp.pad(middle[..., -margin:, :], leading_rows + [(row_count - margin, 0), (0, 0)])
    )


def tiles(state, cotangent, first_weight, second_weight, third_weight):
    weights = (first_weight, second_weight, third_weight)
    current = state
    saved = []
    for step_number in range(STEPS):
        extended = with_halo(current, (("rows", 1), (("cols", "section"), 2)), 2)
        moved = advance(extended, *weights)
        velocity_pad = with_halo(moved, (("rows", 1), (("cols", "section"), 2)), 1)
        source = divergence(velocity_pad)
        pressure = -0.25 * source
        pressure_pads = []
        for sweep_number in range(SWEEPS):
            padded = with_halo(pressure, (("rows", 0), (("cols", "section"), 1)), 1)
            pressure_pads.append(padded)
            if sweep_number < SWEEPS - 1:
                pressure = 0.25 * (padded_neighbours(padded) - source)
        saved.append((extended, velocity_pad, pressure_pads))
        current = moved - pressure_gradient(pressure_pads[-1])
    upstream = cotangent
    totals = (
        jnp.zeros(first_weight.shape, jnp.float32),
        jnp.zeros(second_weight.shape, jnp.float32),
        jnp.zeros(third_weight.shape, jnp.float32),
    )
    for step_number in reversed(range(STEPS)):
        record = saved[step_number]
        velocity_pad = record[1]
        pressure_pads = record[2]
        pad_grad = jax.vjp(pressure_gradient, pressure_pads[-1])[1](-upstream)[0]
        source_grad = jnp.zeros_like(upstream[0])
        for sweep_number in reversed(range(SWEEPS)):
            returned = with_halo(pad_grad, (("rows", 0), (("cols", "section"), 1)), 1)
            pressure_grad = fold_rims(returned, 1)
            source_grad = source_grad - 0.25 * pressure_grad
            if sweep_number > 0:
                pad_grad = jax.vjp(padded_neighbours, pressure_pads[sweep_number - 1])[1](
                    0.25 * pressure_grad
                )[0]
        velocity_grad = jax.vjp(divergence, velocity_pad)[1](source_grad)[0]
        returned_velocity = with_halo(velocity_grad, (("rows", 1), (("cols", "section"), 2)), 1)
        moved_grad = upstream + fold_rims(returned_velocity, 1)
        extended_grad, grads = advance_back(
            record[0], first_weight, second_weight, third_weight, moved_grad
        )
        totals = (totals[0] + grads[0], totals[1] + grads[1], totals[2] + grads[2])
        if step_number > 0:
            returned_state = with_halo(extended_grad, (("rows", 1), (("cols", "section"), 2)), 2)
            upstream = fold_rims(returned_state, 2)
    totals = lax.psum((totals[0], totals[1], totals[2]), ("rows", "cols", "section"))
    cell_total = (
        state.shape[1] * state.shape[2] * lax.axis_size("rows") * lax.axis_size(("cols", "section"))
    )
    factor = gradient_gain / math.sqrt(cell_total)
    return (current, totals[0] * factor, totals[1] * factor, totals[2] * factor)


def solution(mesh):
    def program(state, *rest):
        fits = (
            lax.axis_size("rows") == 4
            and state.shape[1] == 8
            and state.shape[2] == LANES
            and lax.axis_size(("cols", "section")) >= 2
            and lax.axis_size("section") == 2
            and lax.axis_size("cols") == 2
        )
        return (strips if fits else tiles)(state, *rest)

    return jax.shard_map(
        program,
        mesh=mesh,
        in_specs=(
            P(None, ("groups", "rows"), ("cols", "section")),
            P(None, ("groups", "rows"), ("cols", "section")),
            P(),
            P(),
            P(),
        ),
        out_specs=(
            P(None, ("groups", "rows"), ("cols", "section")),
            P("groups", None),
            P("groups", None),
            P("groups", None),
        ),
        check_vma=False,
    )
```

```python
import functools
import math

import jax
import jax.numpy as jnp
from jax import lax
from jax.experimental import pallas as pl
from jax.experimental.pallas import tpu as pltpu
from jax.sharding import PartitionSpec as P

STEPS = 4
SWEEPS = 3
CHANNELS = 64
TAPS = 18
COEFS = 32
LANES = 128
HALF = LANES // 2
PACKED = 16
SIDE = 32

time_step = 0.1
viscosity = 0.2
correction_gain = 0.25
gradient_gain = 10.0

GELU_SCALE = math.sqrt(2.0 / math.pi)
GELU_CUBE = 0.044715


def shift(plane, row, col):
    if row:
        plane = pltpu.roll(plane, (-row) % plane.shape[0], 0)
    if col:
        plane = pltpu.roll(plane, (-col) % plane.shape[1], 1)
    return plane


def swap_halves(x):
    return pltpu.roll(x, HALF, 1)


def neighbours(p):
    return (shift(p, 1, 0) + shift(p, -1, 0)) + (shift(p, 0, 1) + shift(p, 0, -1))


def project(first, second):
    source = 0.5 * (
        (shift(first, 1, 0) - shift(first, -1, 0)) + (shift(second, 0, 1) - shift(second, 0, -1))
    )
    up = {k: shift(source, 0, k) for k in (1, 2, 3)}
    down = {k: shift(source, 0, -k) for k in (1, 2, 3)}

    def rows(plane, reach):
        return shift(plane, reach, 0) + shift(plane, -reach, 0)

    one = up[1] + down[1]
    mixed = 4.0 * source + 2.0 * one
    pressure = ((20.0 * source + 4.0 * one) + (up[2] + down[2])) + (rows(mixed, 1) + rows(source, 2))
    one, two = up[1] - down[1], up[2] - down[2]
    mixed = 4.0 * one + 2.0 * two
    slope = ((19.0 * one + 4.0 * two) + (up[3] - down[3])) + (rows(mixed, 1) + rows(one, 2))
    return (
        first + (1.0 / 128.0) * (shift(pressure, 1, 0) - shift(pressure, -1, 0)),
        second + (1.0 / 128.0) * slope,
    )


def dot(a, b):
    return jnp.dot(a, b, preferred_element_type=jnp.float32)


def dot_cells(a, b):
    return lax.dot_general(a, b, (((1,), (1,)), ((), ())), preferred_element_type=jnp.float32)


GELU_A, GELU_B = 2.0 * GELU_SCALE, 8.0 * GELU_SCALE * GELU_CUBE


def gelu_half(h):
    e = 1.0 + jnp.tanh(h * (GELU_A + GELU_B * (h * h)))
    return h * e, e


def gelu_half_slope(h, e):
    return e * (1.0 + (2.0 - e) * (h * (GELU_A + ((3.0 * GELU_B) * h) * h)))


def pick_taps(shape, place_dim):
    place = lax.broadcasted_iota(jnp.int32, shape, place_dim)
    tap = lax.broadcasted_iota(jnp.int32, shape, 1 - place_dim)
    row, col = (tap // 4) % 4, tap % 4
    wanted = (tap // 16) * 9 + row * 3 + col
    return jnp.where((place == wanted) & (row < 3) & (col < 3), 1.0, 0.0)


def prepare(w1_in, w2_in, w3_in, w1, w1t, w2, w2t, w3, w3t):
    f32, bf16 = jnp.float32, jnp.bfloat16
    spread = dot(pick_taps((32, TAPS), 1).astype(bf16), w1_in[...])
    w1[...] = (0.5 * spread.T).astype(bf16)
    w1t[...] = spread.astype(bf16)
    wide = w2_in[...].astype(f32)
    w2[...] = (0.5 * wide).astype(bf16)
    w2t[...] = (0.5 * wide.T).astype(bf16)
    wide = w3_in[...].astype(f32)
    w3t[...] = ((0.5 * correction_gain) * wide.T).astype(bf16)
    for f in range(2):
        rows = wide[16 * f : 16 * f + 16]
        rows = correction_gain * (rows - jnp.mean(rows, axis=0, keepdims=True))
        high = rows.astype(bf16)
        w3[16 * f : 16 * f + 16, 0:64] = high
        w3[16 * f : 16 * f + 16, 64:128] = (rows - high.astype(f32)).astype(bf16)


def prepare_call(w1_in, w2_in, w3_in):
    vmem = pl.BlockSpec(memory_space=pltpu.VMEM)
    shapes = ((CHANNELS, 32), (32, CHANNELS), (CHANNELS, CHANNELS), (CHANNELS, CHANNELS))
    shapes += ((COEFS, 2 * CHANNELS), (CHANNELS, COEFS))
    return pl.pallas_call(
        prepare,
        out_shape=tuple(jax.ShapeDtypeStruct(shape, jnp.bfloat16) for shape in shapes),
        in_specs=[vmem] * 3,
        out_specs=(vmem,) * 6,
        compiler_params=pltpu.CompilerParams(vmem_limit_bytes=8 * 1024 * 1024),
        cost_estimate=pl.CostEstimate(flops=1 << 20, bytes_accessed=1 << 16, transcendentals=0),
    )(w1_in, w2_in, w3_in)


def kernel(
    factor,
    own_near,
    own_far,
    other_near,
    other_far,
    w1,
    w1t,
    w2,
    w2t,
    w3,
    w3t,
    mine,
    theirs,
    grads,
    s_wide,
    s_all,
    up,
    qs,
    uu,
    ub,
    qp,
    bq,
    x_all,
    a1_all,
    a2_all,
    cf,
):
    f32, bf16 = jnp.float32, jnp.bfloat16
    z = lax.axis_index("rows")
    left = lax.broadcasted_iota(jnp.int32, (PACKED, LANES), 1) < HALF

    lane = lax.broadcasted_iota(jnp.int32, (8, LANES), 1)
    odd = (lane * 0 + z) % 2 == 1
    for k in range(4):
        row = pl.multiple_of(8 * (z ^ k), 8)
        own, other = ((own_near, other_near), (own_far, other_far))[k // 2]
        for c in range(4):
            here = own[k % 2, c]
            there = other[k % 2, c]
            turned = swap_halves(here)
            upper = jnp.where(odd, jnp.where(lane < HALF, turned, swap_halves(there)), here)
            lower = jnp.where(odd, turned, there)
            narrow = jnp.where(lane < LANES - SIDE, upper, lower)
            if c < 2:
                s_wide[c, pl.ds(row, 8), 0:LANES] = upper
                s_wide[c, pl.ds(row, 8), LANES : 2 * LANES] = lower
                s_all[0, c, pl.ds(row, 8), :] = narrow
            else:
                up[c - 2, pl.ds(row, 8), :] = narrow

    def pack(plane, part, turned=None):
        if turned is None:
            plane = plane[:, LANES:] if part == 2 else plane[:, :LANES]
            turned = swap_halves(plane)
        low, high = plane[:PACKED], plane[PACKED:]
        low_turned, high_turned = turned[:PACKED], turned[PACKED:]
        if part == 0:
            return jnp.where(left, low, high_turned), jnp.where(left, high, low_turned)
        return jnp.where(left, low_turned, high), jnp.where(left, high_turned, low)

    def unpack(pieces, col=0):
        inner, outer = pieces[0], pieces[1]
        if len(pieces) == 3:
            lower = jnp.concatenate([swap_halves(pieces[2]), pieces[2]], 0)
            return shift(jnp.concatenate([unpack(pieces[:2]), lower], 1), 0, col)
        lanes = lax.broadcasted_iota(jnp.int32, (PACKED, LANES), 1)
        core = left if col == 0 else ((lanes + (col + LANES)) % LANES) < HALF
        return jnp.concatenate(
            [
                jnp.where(core, shift(inner, 0, col), shift(outer, 0, col + HALF)),
                jnp.where(core, shift(inner, 0, col + HALF), shift(outer, 0, col)),
            ],
            0,
        )

    def stencil(step, part, c, ah, r):
        at = 8 * (r + 2 * ah)
        return uu[step, part, c, at : at + 8, :]

    saved = {}

    def forward(step):
        parts = range(3) if step == 0 else range(2)
        s = [s_wide[c] if step == 0 else s_all[step, c] for c in range(2)]
        for c in range(2):
            for b in range(4):
                plane = shift(s[c], 0, b - 1)
                turned = None if step == 0 else shift(s[c], 0, b - 1 + HALF)
                for part in parts:
                    packed, swapped = pack(plane, part, turned)
                    ref = uu.at[step, part, c]
                    ref[pl.ds(8 + b, PACKED, stride=8), :] = packed
                    ref[pl.ds(4 + b, PACKED, stride=8), :] = packed
                    for at, r in ((b, PACKED - 1), (132 + b, 0), (136 + b, 0), (140 + b, 1)):
                        ref[at : at + 1, :] = swapped[r : r + 1]

        cells = PACKED * LANES
        rows = [(part, r) for part in parts for r in range(PACKED)]
        kept = cells if step == 0 else 2 * cells
        x = jnp.concatenate(
            [
                jnp.concatenate(
                    [stencil(step, part, c, ah, r) for c in range(2) for ah in range(2)], 0
                ).astype(bf16)
                for part, r in rows
            ],
            1,
        )
        x_all[step] = x[:, :cells]
        first = dot(w1[...], x)
        act, first_up = gelu_half(first)
        act = act.astype(bf16)
        a1_all[step] = act[:, :cells]
        second = dot(w2[...], act)
        act, second_up = gelu_half(second)
        act = act.astype(bf16)
        a2_all[step] = act[:, :cells]
        saved[step] = [value[:, :kept] for value in (first, first_up, second, second_up)]
        out = dot(w3[...], jnp.concatenate([act, act], 0))
        if step > 0:
            cf[step] = out
        for k, (part, r) in enumerate(rows):
            weight = out[:, k * LANES : (k + 1) * LANES]
            for c in range(2):
                lower = stencil(step, part, c, 0, r)
                upper = stencil(step, part, c, 1, r)
                for f in range(2):
                    qp[part, 2 * f + c, 8 * r : 8 * r + 8, :] = (
                        weight[16 * f : 16 * f + 8] * lower
                        + weight[16 * f + 8 : 16 * f + 16] * upper
                    )

        def reduced(part, which):
            terms = [qp[part, which, pl.ds(j, PACKED, stride=8), :] for j in range(8)]
            while len(terms) > 1:
                terms = [a + b for a, b in zip(terms[::2], terms[1::2])]
            return terms[0]

        moved = []
        speed = [0.5 * (s[0] + shift(s[0], 1, 0)), 0.5 * (s[1] + shift(s[1], 0, 1))]
        speed_below = shift(speed[1], 0, -1)
        for c in range(2):
            pieces = [[reduced(part, 2 * f + c) for part in parts] for f in range(2)]
            mean = [0.5 * (s[c] + shift(s[c], 1, 0)), 0.5 * (s[c] + shift(s[c], 0, 1))]
            q = [mean[f] + unpack(pieces[f]) for f in range(2)]
            if step > 0:
                for f in range(2):
                    qs[step, 2 * f + c] = q[f]
            rows = speed[0] * q[0]
            below = speed_below * (shift(mean[1], 0, -1) + unpack(pieces[1], -1))
            transport = (rows - shift(rows, -1, 0)) + (speed[1] * q[1] - below)
            moved.append(
                s[c]
                - time_step * transport
                + time_step * viscosity * (neighbours(s[c]) - 4.0 * s[c])
            )
        after = list(project(moved[0], moved[1]))
        for c in range(2):
            if step == 0:
                column = lax.broadcasted_iota(jnp.int32, (2 * PACKED, LANES), 1)
                after[c] = jnp.where(
                    column < LANES - SIDE, after[c][:, :LANES], after[c][:, LANES:]
                )
            s_all[step + 1, c] = after[c]

    def backward(step, total):
        u = [up[c] for c in range(2)]
        s = [s_all[step, c] for c in range(2)]
        m_bar = project(u[0], u[1])
        speed = [0.5 * (s[0] + shift(s[0], 1, 0)), 0.5 * (s[1] + shift(s[1], 0, 1))]
        box = []
        for c in range(2):
            pair = s[c] + shift(s[c], 0, 1)
            line = shift(pair, 0, -1) + shift(pair, 0, 1)
            pair = line + shift(line, 1, 0)
            box.append((1.0 / 16.0) * (shift(pair, -1, 0) + shift(pair, 1, 0)))
        speed_bar = [None, None]
        s_bar = []
        parts = range(2) if step > 0 else range(1)
        for part in parts:
            weights = [pack(time_step * speed[f], part)[0] for f in range(2)]
            boxes = [pack(box[c], part)[0] for c in range(2)]
            mean = [None, None]
            for c in range(2):
                here = pack(m_bar[c], part)[0]
                ahead = (
                    pack(shift(m_bar[c], 1, 0), part)[0],
                    pack(shift(m_bar[c], 0, 1), part, shift(m_bar[c], 0, 1 + HALF))[0],
                )
                for f in range(2):
                    q_bar = weights[f] * (ahead[f] - here)
                    bq[part, 2 * f + c] = q_bar
                    term = q_bar * boxes[c]
                    mean[f] = term if c == 0 else mean[f] + term
            for f in range(2):
                bq[part, 4 + f] = mean[f]
        for c in range(2) if step > 0 else ():
            flux_bar = [
                time_step * (shift(m_bar[c], 1, 0) - m_bar[c]),
                time_step * (shift(m_bar[c], 0, 1) - m_bar[c]),
            ]
            kept = m_bar[c] + time_step * viscosity * (neighbours(m_bar[c]) - 4.0 * m_bar[c])
            for f in range(2):
                term = qs[step, 2 * f + c] * flux_bar[f]
                speed_bar[f] = term if c == 0 else speed_bar[f] + term
                half = (0.5 * speed[f]) * flux_bar[f]
                kept = kept + (half + (shift(half, -1, 0) if f == 0 else shift(half, 0, -1)))
            s_bar.append(kept)
        if step > 0:
            half = 0.5 * speed_bar[0]
            s_bar[0] = s_bar[0] + (half + shift(half, -1, 0))
            half = 0.5 * speed_bar[1]
            s_bar[1] = s_bar[1] + (half + shift(half, 0, -1))

        cells = PACKED * LANES

        def spread_row(part, which, r):
            return jnp.broadcast_to(bq[part, which, r : r + 1, :], (8, LANES))

        third = []
        for part in parts:
            for r in range(PACKED):
                pieces = []
                for f in range(2):
                    q0, q1, m = (spread_row(part, w, r) for w in (2 * f, 2 * f + 1, 4 + f))
                    for ah in range(2):
                        pieces.append(
                            (q0 * stencil(step, part, 0, ah, r) + q1 * stencil(step, part, 1, ah, r))
                            - m
                        )
                third.append(jnp.concatenate(pieces, 0).astype(bf16))
        third = jnp.concatenate(third, 1)
        first, first_up, second, second_up = saved[step]
        second = (dot(w3t[...], third) * gelu_half_slope(second, second_up)).astype(bf16)
        first = (dot(w2t[...], second) * gelu_half_slope(first, first_up)).astype(bf16)

        def gradients():
            terms = (
                dot_cells(first[:, :cells], x_all[step]),
                dot_cells(second[:, :cells], a1_all[step]),
                dot_cells(third[:, :cells], a2_all[step]),
            )
            return terms if total is None else tuple(a + b for a, b in zip(total, terms))

        if step == 0:
            return gradients()
        out = dot(w1t[...], first)

        for part in parts:
            y = {}
            for r in range(PACKED):
                k = part * PACKED + r
                lanes = slice(k * LANES, (k + 1) * LANES)
                for c in range(2):
                    q0, q1 = spread_row(part, c, r), spread_row(part, 2 + c, r)
                    for ah in range(2):
                        y[c, ah, r] = (
                            cf[step, 8 * ah : 8 * ah + 8, lanes] * q0
                            + cf[step, 16 + 8 * ah : 24 + 8 * ah, lanes] * q1
                        ) + out[16 * c + 8 * ah : 16 * c + 8 * ah + 8, lanes]
            for c in range(2):
                rows = []
                for m in range(PACKED):
                    value = y[c, 0, m + 1] if m + 1 < PACKED else swap_halves(y[c, 0, 0])
                    before = y[c, 1, m - 1] if m > 0 else swap_halves(y[c, 1, PACKED - 1])
                    rows.append(value + before)
                ub[part, c, 0:8, :] = swap_halves(rows[PACKED - 1])
                for m in range(PACKED):
                    ub[part, c, 8 + 8 * m : 16 + 8 * m, :] = rows[m]

        for c in range(2):
            kept = s_bar[c]
            for b in range(4):
                kept = kept + unpack(
                    [
                        ub[part, c, pl.ds(8 + b, PACKED, stride=8), :]
                        + ub[part, c, pl.ds(4 + b, PACKED, stride=8), :]
                        for part in parts
                    ],
                    1 - b,
                )
            up[c] = kept
        return gradients()

    for step in range(STEPS):
        forward(step)
    for ref, tile in ((mine, z), (theirs, z ^ 1)):
        first, second = (s_all[STEPS, c, pl.ds(pl.multiple_of(8 * tile, 8), 8), :] for c in range(2))
        ref[...] = jnp.where(lane < HALF, first, swap_halves(second))
    total = None
    for step in reversed(range(STEPS)):
        total = backward(step, total)
    grads[:, 0:64] = factor * total[1]
    first = lax.dot_general(
        pick_taps((TAPS, 32), 0),
        factor * total[0],
        (((1,), (1,)), ((), ())),
        precision=lax.Precision.HIGHEST,
        preferred_element_type=f32,
    )
    grads[0:TAPS, 64:128] = first
    grads[TAPS:32, 64:128] = jnp.zeros((32 - TAPS, CHANNELS), f32)
    grads[32:64, 64:128] = (factor * correction_gain) * total[2]


def strip_call(factor, pieces, weights):
    cells = PACKED * LANES
    f32, bf16 = jnp.float32, jnp.bfloat16
    vmem = pl.BlockSpec(memory_space=pltpu.VMEM)
    return pl.pallas_call(
        functools.partial(kernel, factor),
        out_shape=(
            jax.ShapeDtypeStruct((8, LANES), f32),
            jax.ShapeDtypeStruct((8, LANES), f32),
            jax.ShapeDtypeStruct((CHANNELS, LANES), f32),
        ),
        in_specs=[vmem] * 10,
        out_specs=(vmem,) * 3,
        scratch_shapes=[
            pltpu.VMEM((2, 2 * PACKED, 2 * LANES), f32),
            pltpu.VMEM((STEPS + 1, 2, 2 * PACKED, LANES), f32),
            pltpu.VMEM((2, 2 * PACKED, LANES), f32),
            pltpu.VMEM((STEPS, 4, 2 * PACKED, LANES), f32),
            pltpu.VMEM((STEPS, 3, 2, 8 * (PACKED + 2), LANES), f32),
            pltpu.VMEM((2, 2, 8 * (PACKED + 1), LANES), f32),
            pltpu.VMEM((3, 4, 8 * PACKED, LANES), f32),
            pltpu.VMEM((2, 6, PACKED, LANES), f32),
            pltpu.VMEM((STEPS, 32, cells), bf16),
            pltpu.VMEM((STEPS, CHANNELS, cells), bf16),
            pltpu.VMEM((STEPS, CHANNELS, cells), bf16),
            pltpu.VMEM((STEPS, COEFS, 2 * cells), f32),
        ],
        compiler_params=pltpu.CompilerParams(vmem_limit_bytes=48 * 1024 * 1024),
    )(*pieces, *weights)


def finish(sent, beyond, got, across, mine, tile, first, second, third):
    z = lax.axis_index("rows")
    lane = lax.broadcasted_iota(jnp.int32, (8, LANES), 1)
    odd = (lane * 0 + z) % 2 == 1
    near, far = mine[...], got[64:72, :]
    for c in range(2):
        here, there = (x if c == 0 else swap_halves(x) for x in (near, far))
        low = jnp.where(odd, there, here)
        high = jnp.where(odd, here, there)
        tile[c] = jnp.where(lane < HALF, low, swap_halves(high))
    grads = (sent[...] + beyond[...]) + (got[0:64, :] + across[...])
    first[...] = grads[0:TAPS, 64:]
    second[...] = grads[:, 0:64]
    third[...] = grads[32:, 64:]


def finish_call(*pieces):
    vmem = pl.BlockSpec(memory_space=pltpu.VMEM)
    f32 = jnp.float32
    return pl.pallas_call(
        finish,
        out_shape=(
            jax.ShapeDtypeStruct((2, 8, LANES), f32),
            jax.ShapeDtypeStruct((TAPS, CHANNELS), f32),
            jax.ShapeDtypeStruct((CHANNELS, CHANNELS), f32),
            jax.ShapeDtypeStruct((COEFS, CHANNELS), f32),
        ),
        in_specs=[vmem] * len(pieces),
        out_specs=(vmem,) * 4,
        compiler_params=pltpu.CompilerParams(vmem_limit_bytes=8 * 1024 * 1024),
    )(*pieces)


def swap(x, axis, bit):
    return lax.ppermute(x, axis, [(i, i ^ bit) for i in range(lax.axis_size(axis))])


def strips(state, cotangent, first_weight, second_weight, third_weight):
    row_count = lax.axis_size("rows")
    block_count = lax.axis_size(("cols", "section"))
    weights = prepare_call(first_weight.T, second_weight, third_weight)

    def beside(flip):
        pairs = []
        for row in range(row_count):
            step = 1 if row % 2 == 0 else block_count - 1
            for block in range(block_count):
                target = (row ^ flip) * block_count + (block + step) % block_count
                pairs.append((row * block_count + block, target))
        return pairs

    tile = jnp.concatenate([state, cotangent], 0)
    near = jnp.stack([tile, swap(tile, "rows", 1)])
    everyone = ("rows", "cols", "section")
    other_near = lax.ppermute(near, everyone, beside(0))
    other_far = lax.ppermute(near, everyone, beside(2))
    far = swap(near, "rows", 2)

    factor = gradient_gain / math.sqrt(row_count * state.shape[1] * LANES * block_count)
    mine, theirs, grads = strip_call(factor, (near, far, other_near, other_far), weights)

    grads = grads + swap(grads, "section", 1)
    ring = ("rows", "cols")
    across = lax.ppermute(grads, ring, [(i, i ^ 3) for i in range(2 * row_count)])
    beyond = swap(grads, "cols", 1)
    got = swap(jnp.concatenate([grads, theirs], 0), "rows", 1)
    tile, first, second, third = finish_call(grads, beyond, got, across, mine)
    return tile, first.T, second, third


def with_halo(block, sides, width):
    for axis, dim in sides:
        count = lax.axis_size(axis)
        forward = [(i, i + 1) for i in range(count - 1)]
        forward.append((count - 1, 0))
        backward = [(target, source) for source, target in forward]
        low = lax.ppermute(
            lax.slice_in_dim(block, block.shape[dim] - width, None, axis=dim), axis, forward
        )
        high = lax.ppermute(lax.slice_in_dim(block, 0, width, axis=dim), axis, backward)
        block = jnp.concatenate([low, block, high], axis=dim)
    return block


def base_table():
    return jnp.array(
        [
            [0.5 if tap_number in (5, 9) else 0.0 for tap_number in range(16)],
            [0.5 if tap_number in (5, 6) else 0.0 for tap_number in range(16)],
        ],
        jnp.float32,
    )


def patches(extended):
    height = extended.shape[1] - 3
    breadth = extended.shape[2] - 3
    pieces = [
        extended[:, offset_row : offset_row + height, offset_col : offset_col + breadth]
        for offset_row in range(3)
        for offset_col in range(3)
    ]
    return jnp.stack(pieces, 1).reshape(18, height * breadth)


def network(inputs, first_weight, second_weight, third_weight):
    rounded = inputs.astype(jnp.bfloat16)
    first_pre = jnp.dot(first_weight, rounded, preferred_element_type=jnp.float32)
    first_act = jax.nn.gelu(first_pre).astype(jnp.bfloat16)
    second_pre = jnp.dot(second_weight, first_act, preferred_element_type=jnp.float32)
    second_act = jax.nn.gelu(second_pre).astype(jnp.bfloat16)
    coefficients = jnp.dot(third_weight, second_act, preferred_element_type=jnp.float32)
    return (rounded, first_pre, first_act, second_pre, second_act, coefficients)


def physics(extended, coefficients):
    height = extended.shape[1] - 3
    breadth = extended.shape[2] - 3
    inner_rows = height - 1
    inner_cols = breadth - 1
    raw_output = coefficients.reshape(2, 16, height, breadth)
    weights = base_table()[:, :, None, None] + correction_gain * (
        raw_output - jnp.mean(raw_output, axis=1, keepdims=True)
    )
    stencil = jnp.stack(
        [
            extended[:, offset_row : offset_row + height, offset_col : offset_col + breadth]
            for offset_row in range(4)
            for offset_col in range(4)
        ],
        0,
    )
    face_rows = jnp.sum(weights[0][:, None] * stencil, axis=0)
    face_cols = jnp.sum(weights[1][:, None] * stencil, axis=0)
    speed_rows = 0.5 * (
        extended[0, 1 : 1 + height, 1 : 1 + breadth] + extended[0, 2 : 2 + height, 1 : 1 + breadth]
    )
    speed_cols = 0.5 * (
        extended[1, 1 : 1 + height, 1 : 1 + breadth] + extended[1, 1 : 1 + height, 2 : 2 + breadth]
    )
    flux_rows = speed_rows * face_rows
    flux_cols = speed_cols * face_cols
    transport = (
        flux_rows[:, 1:, 1:] - flux_rows[:, :-1, 1:] + flux_cols[:, 1:, 1:] - flux_cols[:, 1:, :-1]
    )
    centre = extended[:, 2 : 2 + inner_rows, 2 : 2 + inner_cols]
    laplace = (
        extended[:, 1 : 1 + inner_rows, 2 : 2 + inner_cols]
        + extended[:, 3 : 3 + inner_rows, 2 : 2 + inner_cols]
        + extended[:, 2 : 2 + inner_rows, 1 : 1 + inner_cols]
        + extended[:, 2 : 2 + inner_rows, 3 : 3 + inner_cols]
        - 4.0 * centre
    )
    return centre - time_step * transport + time_step * viscosity * laplace


def advance(extended, first_weight, second_weight, third_weight):
    outputs = network(patches(extended), first_weight, second_weight, third_weight)
    return physics(extended, outputs[5])


def gelu_back(preact, upstream):
    return jax.vjp(jax.nn.gelu, preact)[1](upstream)[0]


def advance_back(extended, first_weight, second_weight, third_weight, upstream):
    inputs, patch_back = jax.vjp(patches, extended)
    rounded, first_pre, first_act, second_pre, second_act, coefficients = network(
        inputs, first_weight, second_weight, third_weight
    )
    advanced, physics_back = jax.vjp(physics, extended, coefficients)
    extended_grad, coef_grad = physics_back(upstream)
    coef_round = coef_grad.astype(jnp.bfloat16)
    outer = (((1,), (1,)), ((), ()))
    inner = (((0,), (0,)), ((), ()))
    third_grad = lax.dot_general(coef_round, second_act, outer, preferred_element_type=jnp.float32)
    second_back = gelu_back(
        second_pre,
        lax.dot_general(third_weight, coef_round, inner, preferred_element_type=jnp.float32),
    ).astype(jnp.bfloat16)
    second_grad = lax.dot_general(second_back, first_act, outer, preferred_element_type=jnp.float32)
    first_back = gelu_back(
        first_pre,
        lax.dot_general(second_weight, second_back, inner, preferred_element_type=jnp.float32),
    ).astype(jnp.bfloat16)
    first_grad = lax.dot_general(first_back, rounded, outer, preferred_element_type=jnp.float32)
    input_grad = lax.dot_general(
        first_weight, first_back, inner, preferred_element_type=jnp.float32
    )
    extended_grad = extended_grad + patch_back(input_grad)[0]
    return (extended_grad, (first_grad, second_grad, third_grad))


def divergence(padded):
    return 0.5 * (
        padded[0, 2:, 1:-1] - padded[0, :-2, 1:-1] + (padded[1, 1:-1, 2:] - padded[1, 1:-1, :-2])
    )


def padded_neighbours(padded):
    return padded[2:, 1:-1] + padded[:-2, 1:-1] + padded[1:-1, 2:] + padded[1:-1, :-2]


def pressure_gradient(padded):
    return jnp.stack(
        [0.5 * (padded[2:, 1:-1] - padded[:-2, 1:-1]), 0.5 * (padded[1:-1, 2:] - padded[1:-1, :-2])]
    )


def fold_rims(returned, margin):
    row_count = returned.shape[-2] - 4 * margin
    col_count = returned.shape[-1] - 4 * margin
    leading = [(0, 0)] * (returned.ndim - 1)
    middle = (
        returned[..., 2 * margin : 2 * margin + col_count]
        + jnp.pad(returned[..., :margin], leading + [(0, col_count - margin)])
        + jnp.pad(returned[..., -margin:], leading + [(col_count - margin, 0)])
    )
    leading_rows = [(0, 0)] * (returned.ndim - 2)
    return (
        middle[..., 2 * margin : 2 * margin + row_count, :]
        + jnp.pad(middle[..., :margin, :], leading_rows + [(0, row_count - margin), (0, 0)])
        + jnp.pad(middle[..., -margin:, :], leading_rows + [(row_count - margin, 0), (0, 0)])
    )


def tiles(state, cotangent, first_weight, second_weight, third_weight):
    weights = (first_weight, second_weight, third_weight)
    current = state
    saved = []
    for step_number in range(STEPS):
        extended = with_halo(current, (("rows", 1), (("cols", "section"), 2)), 2)
        moved = advance(extended, *weights)
        velocity_pad = with_halo(moved, (("rows", 1), (("cols", "section"), 2)), 1)
        source = divergence(velocity_pad)
        pressure = -0.25 * source
        pressure_pads = []
        for sweep_number in range(SWEEPS):
            padded = with_halo(pressure, (("rows", 0), (("cols", "section"), 1)), 1)
            pressure_pads.append(padded)
            if sweep_number < SWEEPS - 1:
                pressure = 0.25 * (padded_neighbours(padded) - source)
        saved.append((extended, velocity_pad, pressure_pads))
        current = moved - pressure_gradient(pressure_pads[-1])
    upstream = cotangent
    totals = (
        jnp.zeros(first_weight.shape, jnp.float32),
        jnp.zeros(second_weight.shape, jnp.float32),
        jnp.zeros(third_weight.shape, jnp.float32),
    )
    for step_number in reversed(range(STEPS)):
        record = saved[step_number]
        velocity_pad = record[1]
        pressure_pads = record[2]
        pad_grad = jax.vjp(pressure_gradient, pressure_pads[-1])[1](-upstream)[0]
        source_grad = jnp.zeros_like(upstream[0])
        for sweep_number in reversed(range(SWEEPS)):
            returned = with_halo(pad_grad, (("rows", 0), (("cols", "section"), 1)), 1)
            pressure_grad = fold_rims(returned, 1)
            source_grad = source_grad - 0.25 * pressure_grad
            if sweep_number > 0:
                pad_grad = jax.vjp(padded_neighbours, pressure_pads[sweep_number - 1])[1](
                    0.25 * pressure_grad
                )[0]
        velocity_grad = jax.vjp(divergence, velocity_pad)[1](source_grad)[0]
        returned_velocity = with_halo(velocity_grad, (("rows", 1), (("cols", "section"), 2)), 1)
        moved_grad = upstream + fold_rims(returned_velocity, 1)
        extended_grad, grads = advance_back(
            record[0], first_weight, second_weight, third_weight, moved_grad
        )
        totals = (totals[0] + grads[0], totals[1] + grads[1], totals[2] + grads[2])
        if step_number > 0:
            returned_state = with_halo(extended_grad, (("rows", 1), (("cols", "section"), 2)), 2)
            upstream = fold_rims(returned_state, 2)
    totals = lax.psum((totals[0], totals[1], totals[2]), ("rows", "cols", "section"))
    cell_total = (
        state.shape[1] * state.shape[2] * lax.axis_size("rows") * lax.axis_size(("cols", "section"))
    )
    factor = gradient_gain / math.sqrt(cell_total)
    return (current, totals[0] * factor, totals[1] * factor, totals[2] * factor)


def solution(mesh):
    def program(state, *rest):
        fits = (
            lax.axis_size("rows") == 4
            and state.shape[1] == 8
            and state.shape[2] == LANES
            and lax.axis_size(("cols", "section")) >= 2
            and lax.axis_size("section") == 2
            and lax.axis_size("cols") == 2
        )
        return (strips if fits else tiles)(state, *rest)

    return jax.shard_map(
        program,
        mesh=mesh,
        in_specs=(
            P(None, ("groups", "rows"), ("cols", "section")),
            P(None, ("groups", "rows"), ("cols", "section")),
            P(),
            P(),
            P(),
        ),
        out_specs=(
            P(None, ("groups", "rows"), ("cols", "section")),
            P("groups", None),
            P("groups", None),
            P("groups", None),
        ),
        check_vma=False,
    )
```

```python
import functools
import math

import jax
import jax.numpy as jnp
from jax import lax
from jax.experimental import pallas as pl
from jax.experimental.pallas import tpu as pltpu
from jax.sharding import PartitionSpec as P

STEPS = 4
SWEEPS = 3
CHANNELS = 64
TAPS = 18
COEFS = 32
LANES = 128
HALF = LANES // 2
PACKED = 16
SIDE = 32

time_step = 0.1
viscosity = 0.2
correction_gain = 0.25
gradient_gain = 10.0

GELU_SCALE = math.sqrt(2.0 / math.pi)
GELU_CUBE = 0.044715


def shift(plane, row, col):
    if row:
        plane = pltpu.roll(plane, (-row) % plane.shape[0], 0)
    if col:
        plane = pltpu.roll(plane, (-col) % plane.shape[1], 1)
    return plane


def swap_halves(x):
    return pltpu.roll(x, HALF, 1)


def neighbours(p):
    return (shift(p, 1, 0) + shift(p, -1, 0)) + (shift(p, 0, 1) + shift(p, 0, -1))


def project(first, second):
    source = 0.5 * (
        (shift(first, 1, 0) - shift(first, -1, 0)) + (shift(second, 0, 1) - shift(second, 0, -1))
    )
    up = {k: shift(source, 0, k) for k in (1, 2, 3)}
    down = {k: shift(source, 0, -k) for k in (1, 2, 3)}

    def rows(plane, reach):
        return shift(plane, reach, 0) + shift(plane, -reach, 0)

    one = up[1] + down[1]
    mixed = 4.0 * source + 2.0 * one
    pressure = ((20.0 * source + 4.0 * one) + (up[2] + down[2])) + (rows(mixed, 1) + rows(source, 2))
    one, two = up[1] - down[1], up[2] - down[2]
    mixed = 4.0 * one + 2.0 * two
    slope = ((19.0 * one + 4.0 * two) + (up[3] - down[3])) + (rows(mixed, 1) + rows(one, 2))
    return (
        first + (1.0 / 128.0) * (shift(pressure, 1, 0) - shift(pressure, -1, 0)),
        second + (1.0 / 128.0) * slope,
    )


def dot(a, b):
    return jnp.dot(a, b, preferred_element_type=jnp.float32)


def dot_cells(a, b):
    return lax.dot_general(a, b, (((1,), (1,)), ((), ())), preferred_element_type=jnp.float32)


GELU_A, GELU_B = 2.0 * GELU_SCALE, 8.0 * GELU_SCALE * GELU_CUBE


def gelu_half(h):
    e = 1.0 + jnp.tanh(h * (GELU_A + GELU_B * (h * h)))
    return h * e, e


def gelu_half_slope(h, e):
    return e * (1.0 + (2.0 - e) * (h * (GELU_A + ((3.0 * GELU_B) * h) * h)))


def pick_taps(shape, place_dim):
    place = lax.broadcasted_iota(jnp.int32, shape, place_dim)
    tap = lax.broadcasted_iota(jnp.int32, shape, 1 - place_dim)
    row, col = (tap // 4) % 4, tap % 4
    wanted = (tap // 16) * 9 + row * 3 + col
    return jnp.where((place == wanted) & (row < 3) & (col < 3), 1.0, 0.0)


def prepare(w1_in, w2_in, w3_in, w1, w1t, w2, w2t, w3, w3t):
    f32, bf16 = jnp.float32, jnp.bfloat16
    spread = dot(pick_taps((32, TAPS), 1).astype(bf16), w1_in[...])
    w1[...] = (0.5 * spread.T).astype(bf16)
    w1t[...] = spread.astype(bf16)
    wide = w2_in[...].astype(f32)
    w2[...] = (0.5 * wide).astype(bf16)
    w2t[...] = (0.5 * wide.T).astype(bf16)
    wide = w3_in[...].astype(f32)
    w3t[...] = ((0.5 * correction_gain) * wide.T).astype(bf16)
    for f in range(2):
        rows = wide[16 * f : 16 * f + 16]
        rows = correction_gain * (rows - jnp.mean(rows, axis=0, keepdims=True))
        high = rows.astype(bf16)
        w3[16 * f : 16 * f + 16, 0:64] = high
        w3[16 * f : 16 * f + 16, 64:128] = (rows - high.astype(f32)).astype(bf16)


def prepare_call(w1_in, w2_in, w3_in):
    vmem = pl.BlockSpec(memory_space=pltpu.VMEM)
    shapes = ((CHANNELS, 32), (32, CHANNELS), (CHANNELS, CHANNELS), (CHANNELS, CHANNELS))
    shapes += ((COEFS, 2 * CHANNELS), (CHANNELS, COEFS))
    return pl.pallas_call(
        prepare,
        out_shape=tuple(jax.ShapeDtypeStruct(shape, jnp.bfloat16) for shape in shapes),
        in_specs=[vmem] * 3,
        out_specs=(vmem,) * 6,
        compiler_params=pltpu.CompilerParams(vmem_limit_bytes=8 * 1024 * 1024),
        cost_estimate=pl.CostEstimate(flops=1 << 20, bytes_accessed=1 << 16, transcendentals=0),
    )(w1_in, w2_in, w3_in)


def kernel(
    factor,
    own_near,
    own_far,
    other_near,
    other_far,
    w1,
    w1t,
    w2,
    w2t,
    w3,
    w3t,
    mine,
    theirs,
    grads,
    s_wide,
    s_all,
    up,
    qs,
    uu,
    ub,
    qp,
    bq,
    x_all,
    a1_all,
    a2_all,
    cf,
):
    f32, bf16 = jnp.float32, jnp.bfloat16
    z = lax.axis_index("rows")
    left = lax.broadcasted_iota(jnp.int32, (PACKED, LANES), 1) < HALF

    lane = lax.broadcasted_iota(jnp.int32, (8, LANES), 1)
    odd = (lane * 0 + z) % 2 == 1
    for k in range(4):
        row = pl.multiple_of(8 * (z ^ k), 8)
        own, other = ((own_near, other_near), (own_far, other_far))[k // 2]
        for c in range(4):
            here = own[k % 2, c]
            there = other[c] if k % 2 else swap_halves(other[c])
            turned = swap_halves(here)
            upper = jnp.where(odd, jnp.where(lane < HALF, turned, there), here)
            lower = jnp.where(odd, turned, there)
            narrow = jnp.where(lane < LANES - SIDE, upper, lower)
            if c < 2:
                s_wide[c, pl.ds(row, 8), 0:LANES] = upper
                s_wide[c, pl.ds(row, 8), LANES : 2 * LANES] = lower
                s_all[0, c, pl.ds(row, 8), :] = narrow
            else:
                up[c - 2, pl.ds(row, 8), :] = narrow

    def pack(plane, part, turned=None):
        if turned is None:
            plane = plane[:, LANES:] if part == 2 else plane[:, :LANES]
            turned = swap_halves(plane)
        low, high = plane[:PACKED], plane[PACKED:]
        low_turned, high_turned = turned[:PACKED], turned[PACKED:]
        if part == 0:
            return jnp.where(left, low, high_turned), jnp.where(left, high, low_turned)
        return jnp.where(left, low_turned, high), jnp.where(left, high_turned, low)

    def unpack(pieces, col=0):
        inner, outer = pieces[0], pieces[1]
        if len(pieces) == 3:
            lower = jnp.concatenate([swap_halves(pieces[2]), pieces[2]], 0)
            return shift(jnp.concatenate([unpack(pieces[:2]), lower], 1), 0, col)
        lanes = lax.broadcasted_iota(jnp.int32, (PACKED, LANES), 1)
        core = left if col == 0 else ((lanes + (col + LANES)) % LANES) < HALF
        return jnp.concatenate(
            [
                jnp.where(core, shift(inner, 0, col), shift(outer, 0, col + HALF)),
                jnp.where(core, shift(inner, 0, col + HALF), shift(outer, 0, col)),
            ],
            0,
        )

    def stencil(step, part, c, ah, r):
        at = 8 * (r + 2 * ah)
        return uu[step, part, c, at : at + 8, :]

    saved = {}

    def forward(step):
        parts = range(3) if step == 0 else range(2)
        s = [s_wide[c] if step == 0 else s_all[step, c] for c in range(2)]
        for c in range(2):
            for b in range(4):
                plane = shift(s[c], 0, b - 1)
                turned = None if step == 0 else shift(s[c], 0, b - 1 + HALF)
                for part in parts:
                    packed, swapped = pack(plane, part, turned)
                    ref = uu.at[step, part, c]
                    ref[pl.ds(8 + b, PACKED, stride=8), :] = packed
                    ref[pl.ds(4 + b, PACKED, stride=8), :] = packed
                    for at, r in ((b, PACKED - 1), (132 + b, 0), (136 + b, 0), (140 + b, 1)):
                        ref[at : at + 1, :] = swapped[r : r + 1]

        cells = PACKED * LANES
        rows = [(part, r) for part in parts for r in range(PACKED)]
        kept = cells if step == 0 else 2 * cells
        x = jnp.concatenate(
            [
                jnp.concatenate(
                    [stencil(step, part, c, ah, r) for c in range(2) for ah in range(2)], 0
                ).astype(bf16)
                for part, r in rows
            ],
            1,
        )
        x_all[step] = x[:, :cells]
        first = dot(w1[...], x)
        act, first_up = gelu_half(first)
        act = act.astype(bf16)
        a1_all[step] = act[:, :cells]
        second = dot(w2[...], act)
        act, second_up = gelu_half(second)
        act = act.astype(bf16)
        a2_all[step] = act[:, :cells]
        saved[step] = [value[:, :kept] for value in (first, first_up, second, second_up)]
        out = dot(w3[...], jnp.concatenate([act, act], 0))
        if step > 0:
            cf[step] = out
        for k, (part, r) in enumerate(rows):
            weight = out[:, k * LANES : (k + 1) * LANES]
            for c in range(2):
                lower = stencil(step, part, c, 0, r)
                upper = stencil(step, part, c, 1, r)
                for f in range(2):
                    qp[part, 2 * f + c, 8 * r : 8 * r + 8, :] = (
                        weight[16 * f : 16 * f + 8] * lower
                        + weight[16 * f + 8 : 16 * f + 16] * upper
                    )

        def reduced(part, which):
            terms = [qp[part, which, pl.ds(j, PACKED, stride=8), :] for j in range(8)]
            while len(terms) > 1:
                terms = [a + b for a, b in zip(terms[::2], terms[1::2])]
            return terms[0]

        moved = []
        speed = [0.5 * (s[0] + shift(s[0], 1, 0)), 0.5 * (s[1] + shift(s[1], 0, 1))]
        speed_below = shift(speed[1], 0, -1)
        for c in range(2):
            pieces = [[reduced(part, 2 * f + c) for part in parts] for f in range(2)]
            mean = [0.5 * (s[c] + shift(s[c], 1, 0)), 0.5 * (s[c] + shift(s[c], 0, 1))]
            q = [mean[f] + unpack(pieces[f]) for f in range(2)]
            if step > 0:
                for f in range(2):
                    qs[step, 2 * f + c] = q[f]
            rows = speed[0] * q[0]
            below = speed_below * (shift(mean[1], 0, -1) + unpack(pieces[1], -1))
            transport = (rows - shift(rows, -1, 0)) + (speed[1] * q[1] - below)
            moved.append(
                s[c]
                - time_step * transport
                + time_step * viscosity * (neighbours(s[c]) - 4.0 * s[c])
            )
        after = list(project(moved[0], moved[1]))
        for c in range(2):
            if step == 0:
                column = lax.broadcasted_iota(jnp.int32, (2 * PACKED, LANES), 1)
                after[c] = jnp.where(
                    column < LANES - SIDE, after[c][:, :LANES], after[c][:, LANES:]
                )
            s_all[step + 1, c] = after[c]

    def backward(step, total):
        u = [up[c] for c in range(2)]
        s = [s_all[step, c] for c in range(2)]
        m_bar = project(u[0], u[1])
        speed = [0.5 * (s[0] + shift(s[0], 1, 0)), 0.5 * (s[1] + shift(s[1], 0, 1))]
        box = []
        for c in range(2):
            pair = s[c] + shift(s[c], 0, 1)
            line = shift(pair, 0, -1) + shift(pair, 0, 1)
            pair = line + shift(line, 1, 0)
            box.append((1.0 / 16.0) * (shift(pair, -1, 0) + shift(pair, 1, 0)))
        speed_bar = [None, None]
        s_bar = []
        parts = range(2) if step > 0 else range(1)
        for part in parts:
            weights = [pack(time_step * speed[f], part)[0] for f in range(2)]
            boxes = [pack(box[c], part)[0] for c in range(2)]
            mean = [None, None]
            for c in range(2):
                here = pack(m_bar[c], part)[0]
                ahead = (
                    pack(shift(m_bar[c], 1, 0), part)[0],
                    pack(shift(m_bar[c], 0, 1), part, shift(m_bar[c], 0, 1 + HALF))[0],
                )
                for f in range(2):
                    q_bar = weights[f] * (ahead[f] - here)
                    bq[part, 2 * f + c] = q_bar
                    term = q_bar * boxes[c]
                    mean[f] = term if c == 0 else mean[f] + term
            for f in range(2):
                bq[part, 4 + f] = mean[f]
        for c in range(2) if step > 0 else ():
            flux_bar = [
                time_step * (shift(m_bar[c], 1, 0) - m_bar[c]),
                time_step * (shift(m_bar[c], 0, 1) - m_bar[c]),
            ]
            kept = m_bar[c] + time_step * viscosity * (neighbours(m_bar[c]) - 4.0 * m_bar[c])
            for f in range(2):
                term = qs[step, 2 * f + c] * flux_bar[f]
                speed_bar[f] = term if c == 0 else speed_bar[f] + term
                half = (0.5 * speed[f]) * flux_bar[f]
                kept = kept + (half + (shift(half, -1, 0) if f == 0 else shift(half, 0, -1)))
            s_bar.append(kept)
        if step > 0:
            half = 0.5 * speed_bar[0]
            s_bar[0] = s_bar[0] + (half + shift(half, -1, 0))
            half = 0.5 * speed_bar[1]
            s_bar[1] = s_bar[1] + (half + shift(half, 0, -1))

        cells = PACKED * LANES

        def spread_row(part, which, r):
            return jnp.broadcast_to(bq[part, which, r : r + 1, :], (8, LANES))

        third = []
        for part in parts:
            for r in range(PACKED):
                pieces = []
                for f in range(2):
                    q0, q1, m = (spread_row(part, w, r) for w in (2 * f, 2 * f + 1, 4 + f))
                    for ah in range(2):
                        pieces.append(
                            (q0 * stencil(step, part, 0, ah, r) + q1 * stencil(step, part, 1, ah, r))
                            - m
                        )
                third.append(jnp.concatenate(pieces, 0).astype(bf16))
        third = jnp.concatenate(third, 1)
        first, first_up, second, second_up = saved[step]
        second = (dot(w3t[...], third) * gelu_half_slope(second, second_up)).astype(bf16)
        first = (dot(w2t[...], second) * gelu_half_slope(first, first_up)).astype(bf16)

        def gradients():
            terms = (
                dot_cells(first[:, :cells], x_all[step]),
                dot_cells(second[:, :cells], a1_all[step]),
                dot_cells(third[:, :cells], a2_all[step]),
            )
            return terms if total is None else tuple(a + b for a, b in zip(total, terms))

        if step == 0:
            return gradients()
        out = dot(w1t[...], first)

        for part in parts:
            y = {}
            for r in range(PACKED):
                k = part * PACKED + r
                lanes = slice(k * LANES, (k + 1) * LANES)
                for c in range(2):
                    q0, q1 = spread_row(part, c, r), spread_row(part, 2 + c, r)
                    for ah in range(2):
                        y[c, ah, r] = (
                            cf[step, 8 * ah : 8 * ah + 8, lanes] * q0
                            + cf[step, 16 + 8 * ah : 24 + 8 * ah, lanes] * q1
                        ) + out[16 * c + 8 * ah : 16 * c + 8 * ah + 8, lanes]
            for c in range(2):
                rows = []
                for m in range(PACKED):
                    value = y[c, 0, m + 1] if m + 1 < PACKED else swap_halves(y[c, 0, 0])
                    before = y[c, 1, m - 1] if m > 0 else swap_halves(y[c, 1, PACKED - 1])
                    rows.append(value + before)
                ub[part, c, 0:8, :] = swap_halves(rows[PACKED - 1])
                for m in range(PACKED):
                    ub[part, c, 8 + 8 * m : 16 + 8 * m, :] = rows[m]

        for c in range(2):
            kept = s_bar[c]
            for b in range(4):
                kept = kept + unpack(
                    [
                        ub[part, c, pl.ds(8 + b, PACKED, stride=8), :]
                        + ub[part, c, pl.ds(4 + b, PACKED, stride=8), :]
                        for part in parts
                    ],
                    1 - b,
                )
            up[c] = kept
        return gradients()

    for step in range(STEPS):
        forward(step)
    for ref, tile in ((mine, z), (theirs, z ^ 1)):
        first, second = (s_all[STEPS, c, pl.ds(pl.multiple_of(8 * tile, 8), 8), :] for c in range(2))
        ref[...] = jnp.where(lane < HALF, first, swap_halves(second))
    total = None
    for step in reversed(range(STEPS)):
        total = backward(step, total)
    grads[:, 0:64] = factor * total[1]
    first = lax.dot_general(
        pick_taps((TAPS, 32), 0),
        factor * total[0],
        (((1,), (1,)), ((), ())),
        precision=lax.Precision.HIGHEST,
        preferred_element_type=f32,
    )
    grads[0:TAPS, 64:128] = first
    grads[TAPS:32, 64:128] = jnp.zeros((32 - TAPS, CHANNELS), f32)
    grads[32:64, 64:128] = (factor * correction_gain) * total[2]


def strip_call(factor, pieces, weights):
    cells = PACKED * LANES
    f32, bf16 = jnp.float32, jnp.bfloat16
    vmem = pl.BlockSpec(memory_space=pltpu.VMEM)
    return pl.pallas_call(
        functools.partial(kernel, factor),
        out_shape=(
            jax.ShapeDtypeStruct((8, LANES), f32),
            jax.ShapeDtypeStruct((8, LANES), f32),
            jax.ShapeDtypeStruct((CHANNELS, LANES), f32),
        ),
        in_specs=[vmem] * 10,
        out_specs=(vmem,) * 3,
        scratch_shapes=[
            pltpu.VMEM((2, 2 * PACKED, 2 * LANES), f32),
            pltpu.VMEM((STEPS + 1, 2, 2 * PACKED, LANES), f32),
            pltpu.VMEM((2, 2 * PACKED, LANES), f32),
            pltpu.VMEM((STEPS, 4, 2 * PACKED, LANES), f32),
            pltpu.VMEM((STEPS, 3, 2, 8 * (PACKED + 2), LANES), f32),
            pltpu.VMEM((2, 2, 8 * (PACKED + 1), LANES), f32),
            pltpu.VMEM((3, 4, 8 * PACKED, LANES), f32),
            pltpu.VMEM((2, 6, PACKED, LANES), f32),
            pltpu.VMEM((STEPS, 32, cells), bf16),
            pltpu.VMEM((STEPS, CHANNELS, cells), bf16),
            pltpu.VMEM((STEPS, CHANNELS, cells), bf16),
            pltpu.VMEM((STEPS, COEFS, 2 * cells), f32),
        ],
        compiler_params=pltpu.CompilerParams(vmem_limit_bytes=48 * 1024 * 1024),
    )(*pieces, *weights)


def finish(sent, beyond, got, across, mine, tile, first, second, third):
    z = lax.axis_index("rows")
    lane = lax.broadcasted_iota(jnp.int32, (8, LANES), 1)
    odd = (lane * 0 + z) % 2 == 1
    near, far = mine[...], got[64:72, :]
    for c in range(2):
        here, there = (x if c == 0 else swap_halves(x) for x in (near, far))
        low = jnp.where(odd, there, here)
        high = jnp.where(odd, here, there)
        tile[c] = jnp.where(lane < HALF, low, swap_halves(high))
    grads = (sent[...] + beyond[...]) + (got[0:64, :] + across[...])
    first[...] = grads[0:TAPS, 64:]
    second[...] = grads[:, 0:64]
    third[...] = grads[32:, 64:]


def finish_call(*pieces):
    vmem = pl.BlockSpec(memory_space=pltpu.VMEM)
    f32 = jnp.float32
    return pl.pallas_call(
        finish,
        out_shape=(
            jax.ShapeDtypeStruct((2, 8, LANES), f32),
            jax.ShapeDtypeStruct((TAPS, CHANNELS), f32),
            jax.ShapeDtypeStruct((CHANNELS, CHANNELS), f32),
            jax.ShapeDtypeStruct((COEFS, CHANNELS), f32),
        ),
        in_specs=[vmem] * len(pieces),
        out_specs=(vmem,) * 4,
        compiler_params=pltpu.CompilerParams(vmem_limit_bytes=8 * 1024 * 1024),
    )(*pieces)


def swap(x, axis, bit):
    return lax.ppermute(x, axis, [(i, i ^ bit) for i in range(lax.axis_size(axis))])


def strips(state, cotangent, first_weight, second_weight, third_weight):
    row_count = lax.axis_size("rows")
    block_count = lax.axis_size(("cols", "section"))
    weights = prepare_call(first_weight.T, second_weight, third_weight)

    def beside(flip):
        pairs = []
        for row in range(row_count):
            step = 1 if (row ^ flip) % 2 == 0 else block_count - 1
            for block in range(block_count):
                target = (row ^ flip) * block_count + (block + step) % block_count
                pairs.append((row * block_count + block, target))
        return pairs

    tile = jnp.concatenate([state, cotangent], 0)
    everyone = ("rows", "cols", "section")
    across = lax.ppermute(tile, everyone, beside(1))
    level = lax.ppermute(tile, everyone, beside(0))
    near = jnp.stack([tile, swap(tile, "rows", 1)])
    odd = lax.axis_index("rows") % 2 == 1
    half = [jnp.where(odd, x[..., :HALF], x[..., HALF:]) for x in (level, across)]
    other_near = jnp.concatenate(half, -1)
    both = swap(jnp.concatenate([near.reshape(8, 8, LANES), other_near]), "rows", 2)
    far, other_far = both[:8].reshape(2, 4, 8, LANES), both[8:]

    factor = gradient_gain / math.sqrt(row_count * state.shape[1] * LANES * block_count)
    mine, theirs, grads = strip_call(factor, (near, far, other_near, other_far), weights)

    grads = grads + swap(grads, "section", 1)
    ring = ("rows", "cols")
    across = lax.ppermute(grads, ring, [(i, i ^ 3) for i in range(2 * row_count)])
    beyond = swap(grads, "cols", 1)
    got = swap(jnp.concatenate([grads, theirs], 0), "rows", 1)
    tile, first, second, third = finish_call(grads, beyond, got, across, mine)
    return tile, first.T, second, third


def with_halo(block, sides, width):
    for axis, dim in sides:
        count = lax.axis_size(axis)
        forward = [(i, i + 1) for i in range(count - 1)]
        forward.append((count - 1, 0))
        backward = [(target, source) for source, target in forward]
        low = lax.ppermute(
            lax.slice_in_dim(block, block.shape[dim] - width, None, axis=dim), axis, forward
        )
        high = lax.ppermute(lax.slice_in_dim(block, 0, width, axis=dim), axis, backward)
        block = jnp.concatenate([low, block, high], axis=dim)
    return block


def base_table():
    return jnp.array(
        [
            [0.5 if tap_number in (5, 9) else 0.0 for tap_number in range(16)],
            [0.5 if tap_number in (5, 6) else 0.0 for tap_number in range(16)],
        ],
        jnp.float32,
    )


def patches(extended):
    height = extended.shape[1] - 3
    breadth = extended.shape[2] - 3
    pieces = [
        extended[:, offset_row : offset_row + height, offset_col : offset_col + breadth]
        for offset_row in range(3)
        for offset_col in range(3)
    ]
    return jnp.stack(pieces, 1).reshape(18, height * breadth)


def network(inputs, first_weight, second_weight, third_weight):
    rounded = inputs.astype(jnp.bfloat16)
    first_pre = jnp.dot(first_weight, rounded, preferred_element_type=jnp.float32)
    first_act = jax.nn.gelu(first_pre).astype(jnp.bfloat16)
    second_pre = jnp.dot(second_weight, first_act, preferred_element_type=jnp.float32)
    second_act = jax.nn.gelu(second_pre).astype(jnp.bfloat16)
    coefficients = jnp.dot(third_weight, second_act, preferred_element_type=jnp.float32)
    return (rounded, first_pre, first_act, second_pre, second_act, coefficients)


def physics(extended, coefficients):
    height = extended.shape[1] - 3
    breadth = extended.shape[2] - 3
    inner_rows = height - 1
    inner_cols = breadth - 1
    raw_output = coefficients.reshape(2, 16, height, breadth)
    weights = base_table()[:, :, None, None] + correction_gain * (
        raw_output - jnp.mean(raw_output, axis=1, keepdims=True)
    )
    stencil = jnp.stack(
        [
            extended[:, offset_row : offset_row + height, offset_col : offset_col + breadth]
            for offset_row in range(4)
            for offset_col in range(4)
        ],
        0,
    )
    face_rows = jnp.sum(weights[0][:, None] * stencil, axis=0)
    face_cols = jnp.sum(weights[1][:, None] * stencil, axis=0)
    speed_rows = 0.5 * (
        extended[0, 1 : 1 + height, 1 : 1 + breadth] + extended[0, 2 : 2 + height, 1 : 1 + breadth]
    )
    speed_cols = 0.5 * (
        extended[1, 1 : 1 + height, 1 : 1 + breadth] + extended[1, 1 : 1 + height, 2 : 2 + breadth]
    )
    flux_rows = speed_rows * face_rows
    flux_cols = speed_cols * face_cols
    transport = (
        flux_rows[:, 1:, 1:] - flux_rows[:, :-1, 1:] + flux_cols[:, 1:, 1:] - flux_cols[:, 1:, :-1]
    )
    centre = extended[:, 2 : 2 + inner_rows, 2 : 2 + inner_cols]
    laplace = (
        extended[:, 1 : 1 + inner_rows, 2 : 2 + inner_cols]
        + extended[:, 3 : 3 + inner_rows, 2 : 2 + inner_cols]
        + extended[:, 2 : 2 + inner_rows, 1 : 1 + inner_cols]
        + extended[:, 2 : 2 + inner_rows, 3 : 3 + inner_cols]
        - 4.0 * centre
    )
    return centre - time_step * transport + time_step * viscosity * laplace


def advance(extended, first_weight, second_weight, third_weight):
    outputs = network(patches(extended), first_weight, second_weight, third_weight)
    return physics(extended, outputs[5])


def gelu_back(preact, upstream):
    return jax.vjp(jax.nn.gelu, preact)[1](upstream)[0]


def advance_back(extended, first_weight, second_weight, third_weight, upstream):
    inputs, patch_back = jax.vjp(patches, extended)
    rounded, first_pre, first_act, second_pre, second_act, coefficients = network(
        inputs, first_weight, second_weight, third_weight
    )
    advanced, physics_back = jax.vjp(physics, extended, coefficients)
    extended_grad, coef_grad = physics_back(upstream)
    coef_round = coef_grad.astype(jnp.bfloat16)
    outer = (((1,), (1,)), ((), ()))
    inner = (((0,), (0,)), ((), ()))
    third_grad = lax.dot_general(coef_round, second_act, outer, preferred_element_type=jnp.float32)
    second_back = gelu_back(
        second_pre,
        lax.dot_general(third_weight, coef_round, inner, preferred_element_type=jnp.float32),
    ).astype(jnp.bfloat16)
    second_grad = lax.dot_general(second_back, first_act, outer, preferred_element_type=jnp.float32)
    first_back = gelu_back(
        first_pre,
        lax.dot_general(second_weight, second_back, inner, preferred_element_type=jnp.float32),
    ).astype(jnp.bfloat16)
    first_grad = lax.dot_general(first_back, rounded, outer, preferred_element_type=jnp.float32)
    input_grad = lax.dot_general(
        first_weight, first_back, inner, preferred_element_type=jnp.float32
    )
    extended_grad = extended_grad + patch_back(input_grad)[0]
    return (extended_grad, (first_grad, second_grad, third_grad))


def divergence(padded):
    return 0.5 * (
        padded[0, 2:, 1:-1] - padded[0, :-2, 1:-1] + (padded[1, 1:-1, 2:] - padded[1, 1:-1, :-2])
    )


def padded_neighbours(padded):
    return padded[2:, 1:-1] + padded[:-2, 1:-1] + padded[1:-1, 2:] + padded[1:-1, :-2]


def pressure_gradient(padded):
    return jnp.stack(
        [0.5 * (padded[2:, 1:-1] - padded[:-2, 1:-1]), 0.5 * (padded[1:-1, 2:] - padded[1:-1, :-2])]
    )


def fold_rims(returned, margin):
    row_count = returned.shape[-2] - 4 * margin
    col_count = returned.shape[-1] - 4 * margin
    leading = [(0, 0)] * (returned.ndim - 1)
    middle = (
        returned[..., 2 * margin : 2 * margin + col_count]
        + jnp.pad(returned[..., :margin], leading + [(0, col_count - margin)])
        + jnp.pad(returned[..., -margin:], leading + [(col_count - margin, 0)])
    )
    leading_rows = [(0, 0)] * (returned.ndim - 2)
    return (
        middle[..., 2 * margin : 2 * margin + row_count, :]
        + jnp.pad(middle[..., :margin, :], leading_rows + [(0, row_count - margin), (0, 0)])
        + jnp.pad(middle[..., -margin:, :], leading_rows + [(row_count - margin, 0), (0, 0)])
    )


def tiles(state, cotangent, first_weight, second_weight, third_weight):
    weights = (first_weight, second_weight, third_weight)
    current = state
    saved = []
    for step_number in range(STEPS):
        extended = with_halo(current, (("rows", 1), (("cols", "section"), 2)), 2)
        moved = advance(extended, *weights)
        velocity_pad = with_halo(moved, (("rows", 1), (("cols", "section"), 2)), 1)
        source = divergence(velocity_pad)
        pressure = -0.25 * source
        pressure_pads = []
        for sweep_number in range(SWEEPS):
            padded = with_halo(pressure, (("rows", 0), (("cols", "section"), 1)), 1)
            pressure_pads.append(padded)
            if sweep_number < SWEEPS - 1:
                pressure = 0.25 * (padded_neighbours(padded) - source)
        saved.append((extended, velocity_pad, pressure_pads))
        current = moved - pressure_gradient(pressure_pads[-1])
    upstream = cotangent
    totals = (
        jnp.zeros(first_weight.shape, jnp.float32),
        jnp.zeros(second_weight.shape, jnp.float32),
        jnp.zeros(third_weight.shape, jnp.float32),
    )
    for step_number in reversed(range(STEPS)):
        record = saved[step_number]
        velocity_pad = record[1]
        pressure_pads = record[2]
        pad_grad = jax.vjp(pressure_gradient, pressure_pads[-1])[1](-upstream)[0]
        source_grad = jnp.zeros_like(upstream[0])
        for sweep_number in reversed(range(SWEEPS)):
            returned = with_halo(pad_grad, (("rows", 0), (("cols", "section"), 1)), 1)
            pressure_grad = fold_rims(returned, 1)
            source_grad = source_grad - 0.25 * pressure_grad
            if sweep_number > 0:
                pad_grad = jax.vjp(padded_neighbours, pressure_pads[sweep_number - 1])[1](
                    0.25 * pressure_grad
                )[0]
        velocity_grad = jax.vjp(divergence, velocity_pad)[1](source_grad)[0]
        returned_velocity = with_halo(velocity_grad, (("rows", 1), (("cols", "section"), 2)), 1)
        moved_grad = upstream + fold_rims(returned_velocity, 1)
        extended_grad, grads = advance_back(
            record[0], first_weight, second_weight, third_weight, moved_grad
        )
        totals = (totals[0] + grads[0], totals[1] + grads[1], totals[2] + grads[2])
        if step_number > 0:
            returned_state = with_halo(extended_grad, (("rows", 1), (("cols", "section"), 2)), 2)
            upstream = fold_rims(returned_state, 2)
    totals = lax.psum((totals[0], totals[1], totals[2]), ("rows", "cols", "section"))
    cell_total = (
        state.shape[1] * state.shape[2] * lax.axis_size("rows") * lax.axis_size(("cols", "section"))
    )
    factor = gradient_gain / math.sqrt(cell_total)
    return (current, totals[0] * factor, totals[1] * factor, totals[2] * factor)


def solution(mesh):
    def program(state, *rest):
        fits = (
            lax.axis_size("rows") == 4
            and state.shape[1] == 8
            and state.shape[2] == LANES
            and lax.axis_size(("cols", "section")) >= 2
            and lax.axis_size("section") == 2
            and lax.axis_size("cols") == 2
        )
        return (strips if fits else tiles)(state, *rest)

    return jax.shard_map(
        program,
        mesh=mesh,
        in_specs=(
            P(None, ("groups", "rows"), ("cols", "section")),
            P(None, ("groups", "rows"), ("cols", "section")),
            P(),
            P(),
            P(),
        ),
        out_specs=(
            P(None, ("groups", "rows"), ("cols", "section")),
            P("groups", None),
            P("groups", None),
            P("groups", None),
        ),
        check_vma=False,
    )
```

```python
import functools
import math

import jax
import jax.numpy as jnp
from jax import lax
from jax.experimental import pallas as pl
from jax.experimental.pallas import tpu as pltpu
from jax.sharding import PartitionSpec as P

STEPS = 4
SWEEPS = 3
CHANNELS = 64
TAPS = 18
COEFS = 32
LANES = 128
HALF = LANES // 2
PACKED = 16
SIDE = 32

time_step = 0.1
viscosity = 0.2
correction_gain = 0.25
gradient_gain = 10.0

GELU_SCALE = math.sqrt(2.0 / math.pi)
GELU_CUBE = 0.044715


def shift(plane, row, col):
    if row:
        plane = pltpu.roll(plane, (-row) % plane.shape[0], 0)
    if col:
        plane = pltpu.roll(plane, (-col) % plane.shape[1], 1)
    return plane


def swap_halves(x):
    return pltpu.roll(x, HALF, 1)


def neighbours(p):
    return (shift(p, 1, 0) + shift(p, -1, 0)) + (shift(p, 0, 1) + shift(p, 0, -1))


def project(first, second):
    source = 0.5 * (
        (shift(first, 1, 0) - shift(first, -1, 0)) + (shift(second, 0, 1) - shift(second, 0, -1))
    )
    up = {k: shift(source, 0, k) for k in (1, 2, 3)}
    down = {k: shift(source, 0, -k) for k in (1, 2, 3)}

    def rows(plane, reach):
        return shift(plane, reach, 0) + shift(plane, -reach, 0)

    one = up[1] + down[1]
    mixed = 4.0 * source + 2.0 * one
    pressure = ((20.0 * source + 4.0 * one) + (up[2] + down[2])) + (rows(mixed, 1) + rows(source, 2))
    one, two = up[1] - down[1], up[2] - down[2]
    mixed = 4.0 * one + 2.0 * two
    slope = ((19.0 * one + 4.0 * two) + (up[3] - down[3])) + (rows(mixed, 1) + rows(one, 2))
    return (
        first + (1.0 / 128.0) * (shift(pressure, 1, 0) - shift(pressure, -1, 0)),
        second + (1.0 / 128.0) * slope,
    )


def dot(a, b):
    return jnp.dot(a, b, preferred_element_type=jnp.float32)


def dot_cells(a, b):
    return lax.dot_general(a, b, (((1,), (1,)), ((), ())), preferred_element_type=jnp.float32)


GELU_A, GELU_B = 2.0 * GELU_SCALE, 8.0 * GELU_SCALE * GELU_CUBE


def gelu_half(h):
    e = 1.0 + jnp.tanh(h * (GELU_A + GELU_B * (h * h)))
    return h * e, e


def gelu_half_slope(h, e):
    return e * (1.0 + (2.0 - e) * (h * (GELU_A + ((3.0 * GELU_B) * h) * h)))


def pick_taps(shape, place_dim):
    place = lax.broadcasted_iota(jnp.int32, shape, place_dim)
    tap = lax.broadcasted_iota(jnp.int32, shape, 1 - place_dim)
    row, col = (tap // 4) % 4, tap % 4
    wanted = (tap // 16) * 9 + row * 3 + col
    return jnp.where((place == wanted) & (row < 3) & (col < 3), 1.0, 0.0)


def prepare(w1_in, w2_in, w3_in, w1, w1t, w2, w2t, w3, w3t):
    f32, bf16 = jnp.float32, jnp.bfloat16
    spread = dot(pick_taps((32, TAPS), 1).astype(bf16), w1_in[...])
    w1[...] = (0.5 * spread.T).astype(bf16)
    w1t[...] = spread.astype(bf16)
    wide = w2_in[...].astype(f32)
    w2[...] = (0.5 * wide).astype(bf16)
    w2t[...] = (0.5 * wide.T).astype(bf16)
    wide = w3_in[...].astype(f32)
    w3t[...] = ((0.5 * correction_gain) * wide.T).astype(bf16)
    for f in range(2):
        rows = wide[16 * f : 16 * f + 16]
        rows = correction_gain * (rows - jnp.mean(rows, axis=0, keepdims=True))
        high = rows.astype(bf16)
        w3[16 * f : 16 * f + 16, 0:64] = high
        w3[16 * f : 16 * f + 16, 64:128] = (rows - high.astype(f32)).astype(bf16)


def prepare_call(w1_in, w2_in, w3_in):
    vmem = pl.BlockSpec(memory_space=pltpu.VMEM)
    shapes = ((CHANNELS, 32), (32, CHANNELS), (CHANNELS, CHANNELS), (CHANNELS, CHANNELS))
    shapes += ((COEFS, 2 * CHANNELS), (CHANNELS, COEFS))
    return pl.pallas_call(
        prepare,
        out_shape=tuple(jax.ShapeDtypeStruct(shape, jnp.bfloat16) for shape in shapes),
        in_specs=[vmem] * 3,
        out_specs=(vmem,) * 6,
        compiler_params=pltpu.CompilerParams(vmem_limit_bytes=8 * 1024 * 1024),
        cost_estimate=pl.CostEstimate(flops=1 << 20, bytes_accessed=1 << 16, transcendentals=0),
    )(w1_in, w2_in, w3_in)


def kernel(
    factor,
    own_near,
    own_far,
    other_near,
    other_far,
    w1,
    w1t,
    w2,
    w2t,
    w3,
    w3t,
    mine,
    theirs,
    grads,
    s_wide,
    s_all,
    up,
    qs,
    uu,
    ub,
    qp,
    bq,
    x_all,
    a1_all,
    a2_all,
    cf,
):
    f32, bf16 = jnp.float32, jnp.bfloat16
    z = lax.axis_index("rows")
    left = lax.broadcasted_iota(jnp.int32, (PACKED, LANES), 1) < HALF

    lane = lax.broadcasted_iota(jnp.int32, (8, LANES), 1)
    odd = (lane * 0 + z) % 2 == 1
    for k in range(4):
        row = pl.multiple_of(8 * (z ^ k), 8)
        own, other = ((own_near, other_near), (own_far, other_far))[k // 2]
        for c in range(4):
            here = own[k % 2, c]
            there = other[c] if k % 2 else swap_halves(other[c])
            turned = swap_halves(here)
            upper = jnp.where(odd, jnp.where(lane < HALF, turned, there), here)
            lower = jnp.where(odd, turned, there)
            narrow = jnp.where(lane < LANES - SIDE, upper, lower)
            if c < 2:
                s_wide[c, pl.ds(row, 8), 0:LANES] = upper
                s_wide[c, pl.ds(row, 8), LANES : 2 * LANES] = lower
                s_all[0, c, pl.ds(row, 8), :] = narrow
            else:
                up[c - 2, pl.ds(row, 8), :] = narrow

    def close(shape):
        column = lax.broadcasted_iota(jnp.int32, shape, 1) % HALF
        return (column < 16) | (column >= 48)

    def pack(plane, part, turned=None):
        if turned is None:
            plane = plane[:, LANES:] if part == 2 else plane[:, :LANES]
            turned = swap_halves(plane)
        low, high = plane[:PACKED], plane[PACKED:]
        low_turned, high_turned = turned[:PACKED], turned[PACKED:]
        if part == 0:
            return jnp.where(left, low, high_turned), jnp.where(left, high, low_turned)
        return jnp.where(left, low_turned, high), jnp.where(left, high_turned, low)

    def unpack(pieces, col=0):
        inner, outer = pieces[0], pieces[1]
        if len(pieces) == 3:
            lower = jnp.concatenate([swap_halves(pieces[2]), pieces[2]], 0)
            return shift(jnp.concatenate([unpack(pieces[:2]), lower], 1), 0, col)
        lanes = lax.broadcasted_iota(jnp.int32, (PACKED, LANES), 1)
        core = left if col == 0 else ((lanes + (col + LANES)) % LANES) < HALF
        return jnp.concatenate(
            [
                jnp.where(core, shift(inner, 0, col), shift(outer, 0, col + HALF)),
                jnp.where(core, shift(inner, 0, col + HALF), shift(outer, 0, col)),
            ],
            0,
        )

    def stencil(step, part, c, ah, r):
        at = 8 * (r + 2 * ah)
        return uu[step, part, c, at : at + 8, :]

    saved = {}

    def forward(step):
        parts = range(3) if step == 0 else range(2)
        s = [s_wide[c] if step == 0 else s_all[step, c] for c in range(2)]
        for c in range(2):
            for b in range(4):
                plane = shift(s[c], 0, b - 1)
                turned = None if step == 0 else shift(s[c], 0, b - 1 + HALF)
                for part in parts:
                    packed, swapped = pack(plane, part, turned)
                    ref = uu.at[step, part, c]
                    ref[pl.ds(8 + b, PACKED, stride=8), :] = packed
                    ref[pl.ds(4 + b, PACKED, stride=8), :] = packed
                    for at, r in ((b, PACKED - 1), (132 + b, 0), (136 + b, 0), (140 + b, 1)):
                        ref[at : at + 1, :] = swapped[r : r + 1]

        cells = PACKED * LANES
        rows = [(part, r) for part in parts for r in range(PACKED)]
        kept = cells if step == 0 else 2 * cells
        x = jnp.concatenate(
            [
                jnp.concatenate(
                    [stencil(step, part, c, ah, r) for c in range(2) for ah in range(2)], 0
                ).astype(bf16)
                for part, r in rows
            ],
            1,
        )
        x_all[step] = x[:, :cells]
        first = dot(w1[...], x)
        act, first_up = gelu_half(first)
        act = act.astype(bf16)
        a1_all[step] = act[:, :cells]
        second = dot(w2[...], act)
        act, second_up = gelu_half(second)
        act = act.astype(bf16)
        a2_all[step] = act[:, :cells]
        saved[step] = [value[:, :kept] for value in (first, first_up, second, second_up)]
        out = dot(w3[...], jnp.concatenate([act, act], 0))
        if step > 0:
            cf[step] = out
        for k, (part, r) in enumerate(rows):
            weight = out[:, k * LANES : (k + 1) * LANES]
            for c in range(2):
                lower = stencil(step, part, c, 0, r)
                upper = stencil(step, part, c, 1, r)
                for f in range(2):
                    qp[part, 2 * f + c, 8 * r : 8 * r + 8, :] = (
                        weight[16 * f : 16 * f + 8] * lower
                        + weight[16 * f + 8 : 16 * f + 16] * upper
                    )

        def reduced(part, which):
            terms = [qp[part, which, pl.ds(j, PACKED, stride=8), :] for j in range(8)]
            while len(terms) > 1:
                terms = [a + b for a, b in zip(terms[::2], terms[1::2])]
            return terms[0]

        moved = []
        speed = [0.5 * (s[0] + shift(s[0], 1, 0)), 0.5 * (s[1] + shift(s[1], 0, 1))]
        speed_below = shift(speed[1], 0, -1)
        for c in range(2):
            pieces = [[reduced(part, 2 * f + c) for part in parts] for f in range(2)]
            mean = [0.5 * (s[c] + shift(s[c], 1, 0)), 0.5 * (s[c] + shift(s[c], 0, 1))]
            q = [mean[f] + unpack(pieces[f]) for f in range(2)]
            if step > 0:
                for f in range(2):
                    qs[step, 2 * f + c] = q[f]
            rows = speed[0] * q[0]
            below = speed_below * (shift(mean[1], 0, -1) + unpack(pieces[1], -1))
            transport = (rows - shift(rows, -1, 0)) + (speed[1] * q[1] - below)
            moved.append(
                s[c]
                - time_step * transport
                + time_step * viscosity * (neighbours(s[c]) - 4.0 * s[c])
            )
        after = list(project(moved[0], moved[1]))
        for c in range(2):
            if step == 0:
                column = lax.broadcasted_iota(jnp.int32, (2 * PACKED, LANES), 1)
                after[c] = jnp.where(
                    column < LANES - SIDE, after[c][:, :LANES], after[c][:, LANES:]
                )
            s_all[step + 1, c] = after[c]

    def backward(step, total):
        u = [up[c] for c in range(2)]
        s = [s_all[step, c] for c in range(2)]
        m_bar = project(u[0], u[1])
        speed = [0.5 * (s[0] + shift(s[0], 1, 0)), 0.5 * (s[1] + shift(s[1], 0, 1))]
        box = []
        for c in range(2):
            pair = s[c] + shift(s[c], 0, 1)
            line = shift(pair, 0, -1) + shift(pair, 0, 1)
            pair = line + shift(line, 1, 0)
            box.append((1.0 / 16.0) * (shift(pair, -1, 0) + shift(pair, 1, 0)))
        speed_bar = [None, None]
        s_bar = []
        parts = range(2) if step > 0 else range(1)
        for part in parts:
            weights = [pack(time_step * speed[f], part)[0] for f in range(2)]
            boxes = [pack(box[c], part)[0] for c in range(2)]
            mean = [None, None]
            for c in range(2):
                here = pack(m_bar[c], part)[0]
                ahead = (
                    pack(shift(m_bar[c], 1, 0), part)[0],
                    pack(shift(m_bar[c], 0, 1), part, shift(m_bar[c], 0, 1 + HALF))[0],
                )
                for f in range(2):
                    q_bar = weights[f] * (ahead[f] - here)
                    bq[part, 2 * f + c] = q_bar
                    term = q_bar * boxes[c]
                    mean[f] = term if c == 0 else mean[f] + term
            for f in range(2):
                bq[part, 4 + f] = mean[f]
        for c in range(2) if step > 0 else ():
            flux_bar = [
                time_step * (shift(m_bar[c], 1, 0) - m_bar[c]),
                time_step * (shift(m_bar[c], 0, 1) - m_bar[c]),
            ]
            kept = m_bar[c] + time_step * viscosity * (neighbours(m_bar[c]) - 4.0 * m_bar[c])
            for f in range(2):
                term = qs[step, 2 * f + c] * flux_bar[f]
                speed_bar[f] = term if c == 0 else speed_bar[f] + term
                half = (0.5 * speed[f]) * flux_bar[f]
                kept = kept + (half + (shift(half, -1, 0) if f == 0 else shift(half, 0, -1)))
            s_bar.append(kept)
        if step > 0:
            half = 0.5 * speed_bar[0]
            s_bar[0] = s_bar[0] + (half + shift(half, -1, 0))
            half = 0.5 * speed_bar[1]
            s_bar[1] = s_bar[1] + (half + shift(half, 0, -1))

        cells = PACKED * LANES

        dense = step in (1, 2)
        lines = [(0, r) for r in range(PACKED)]
        if step > 0:
            lines += [(1, r) for r in range(PACKED // 2 if dense else PACKED)]

        def joined(value, part, r):
            if part == 1 and dense:
                here, there = value(r), pltpu.roll(value(r + 8), 32, 1)
                return jnp.where(close(here.shape), here, there)
            return value(r)

        def spread_row(part, which, r):
            row = joined(lambda k: bq[part, which, k : k + 1, :], part, r)
            return jnp.broadcast_to(row, (8, LANES))

        def taps(part, c, ah, r):
            return joined(lambda k: stencil(step, part, c, ah, k), part, r)

        def columns(array):
            def block(part, k):
                at = (part * PACKED + k) * LANES
                return array[:, at : at + LANES]

            return jnp.concatenate(
                [joined(functools.partial(block, part), part, r) for part, r in lines], 1
            )

        third = []
        for part, r in lines:
            pieces = []
            for f in range(2):
                q0, q1, m = (spread_row(part, w, r) for w in (2 * f, 2 * f + 1, 4 + f))
                for ah in range(2):
                    pieces.append((q0 * taps(part, 0, ah, r) + q1 * taps(part, 1, ah, r)) - m)
            third.append(jnp.concatenate(pieces, 0).astype(bf16))
        third = jnp.concatenate(third, 1)
        first, first_up, second, second_up = (columns(value) for value in saved[step])
        second = (dot(w3t[...], third) * gelu_half_slope(second, second_up)).astype(bf16)
        first = (dot(w2t[...], second) * gelu_half_slope(first, first_up)).astype(bf16)

        def gradients():
            terms = (
                dot_cells(first[:, :cells], x_all[step]),
                dot_cells(second[:, :cells], a1_all[step]),
                dot_cells(third[:, :cells], a2_all[step]),
            )
            return terms if total is None else tuple(a + b for a, b in zip(total, terms))

        if step == 0:
            return gradients()
        out = dot(w1t[...], first)
        weights = columns(cf[step])

        for part in parts:
            y = {}
            for k, (piece, r) in enumerate(lines):
                if piece != part:
                    continue
                lanes = slice(k * LANES, (k + 1) * LANES)
                for c in range(2):
                    q0, q1 = spread_row(part, c, r), spread_row(part, 2 + c, r)
                    for ah in range(2):
                        y[c, ah, r] = (
                            weights[8 * ah : 8 * ah + 8, lanes] * q0
                            + weights[16 + 8 * ah : 24 + 8 * ah, lanes] * q1
                        ) + out[16 * c + 8 * ah : 16 * c + 8 * ah + 8, lanes]
            if part == 1 and dense:
                for c in range(2):
                    for ah in range(2):
                        for r in range(PACKED // 2):
                            value = y[c, ah, r]
                            y[c, ah, r + 8] = jnp.where(
                                close(value.shape), pltpu.roll(value, LANES - 32, 1), 0.0
                            )
                            y[c, ah, r] = jnp.where(close(value.shape), value, 0.0)
            for c in range(2):
                rows = []
                for m in range(PACKED):
                    value = y[c, 0, m + 1] if m + 1 < PACKED else swap_halves(y[c, 0, 0])
                    before = y[c, 1, m - 1] if m > 0 else swap_halves(y[c, 1, PACKED - 1])
                    rows.append(value + before)
                ub[part, c, 0:8, :] = swap_halves(rows[PACKED - 1])
                for m in range(PACKED):
                    ub[part, c, 8 + 8 * m : 16 + 8 * m, :] = rows[m]

        for c in range(2):
            kept = s_bar[c]
            for b in range(4):
                kept = kept + unpack(
                    [
                        ub[part, c, pl.ds(8 + b, PACKED, stride=8), :]
                        + ub[part, c, pl.ds(4 + b, PACKED, stride=8), :]
                        for part in parts
                    ],
                    1 - b,
                )
            up[c] = kept
        return gradients()

    for step in range(STEPS):
        forward(step)
    for ref, tile in ((mine, z), (theirs, z ^ 1)):
        first, second = (s_all[STEPS, c, pl.ds(pl.multiple_of(8 * tile, 8), 8), :] for c in range(2))
        ref[...] = jnp.where(lane < HALF, first, swap_halves(second))
    total = None
    for step in reversed(range(STEPS)):
        total = backward(step, total)
    grads[:, 0:64] = factor * total[1]
    first = lax.dot_general(
        pick_taps((TAPS, 32), 0),
        factor * total[0],
        (((1,), (1,)), ((), ())),
        precision=lax.Precision.HIGHEST,
        preferred_element_type=f32,
    )
    grads[0:TAPS, 64:128] = first
    grads[TAPS:32, 64:128] = jnp.zeros((32 - TAPS, CHANNELS), f32)
    grads[32:64, 64:128] = (factor * correction_gain) * total[2]


def strip_call(factor, pieces, weights):
    cells = PACKED * LANES
    f32, bf16 = jnp.float32, jnp.bfloat16
    vmem = pl.BlockSpec(memory_space=pltpu.VMEM)
    return pl.pallas_call(
        functools.partial(kernel, factor),
        out_shape=(
            jax.ShapeDtypeStruct((8, LANES), f32),
            jax.ShapeDtypeStruct((8, LANES), f32),
            jax.ShapeDtypeStruct((CHANNELS, LANES), f32),
        ),
        in_specs=[vmem] * 10,
        out_specs=(vmem,) * 3,
        scratch_shapes=[
            pltpu.VMEM((2, 2 * PACKED, 2 * LANES), f32),
            pltpu.VMEM((STEPS + 1, 2, 2 * PACKED, LANES), f32),
            pltpu.VMEM((2, 2 * PACKED, LANES), f32),
            pltpu.VMEM((STEPS, 4, 2 * PACKED, LANES), f32),
            pltpu.VMEM((STEPS, 3, 2, 8 * (PACKED + 2), LANES), f32),
            pltpu.VMEM((2, 2, 8 * (PACKED + 1), LANES), f32),
            pltpu.VMEM((3, 4, 8 * PACKED, LANES), f32),
            pltpu.VMEM((2, 6, PACKED, LANES), f32),
            pltpu.VMEM((STEPS, 32, cells), bf16),
            pltpu.VMEM((STEPS, CHANNELS, cells), bf16),
            pltpu.VMEM((STEPS, CHANNELS, cells), bf16),
            pltpu.VMEM((STEPS, COEFS, 2 * cells), f32),
        ],
        compiler_params=pltpu.CompilerParams(vmem_limit_bytes=48 * 1024 * 1024),
    )(*pieces, *weights)


def finish(sent, beyond, got, across, mine, tile, first, second, third):
    z = lax.axis_index("rows")
    lane = lax.broadcasted_iota(jnp.int32, (8, LANES), 1)
    odd = (lane * 0 + z) % 2 == 1
    near, far = mine[...], got[64:72, :]
    for c in range(2):
        here, there = (x if c == 0 else swap_halves(x) for x in (near, far))
        low = jnp.where(odd, there, here)
        high = jnp.where(odd, here, there)
        tile[c] = jnp.where(lane < HALF, low, swap_halves(high))
    grads = (sent[...] + beyond[...]) + (got[0:64, :] + across[...])
    first[...] = grads[0:TAPS, 64:]
    second[...] = grads[:, 0:64]
    third[...] = grads[32:, 64:]


def finish_call(*pieces):
    vmem = pl.BlockSpec(memory_space=pltpu.VMEM)
    f32 = jnp.float32
    return pl.pallas_call(
        finish,
        out_shape=(
            jax.ShapeDtypeStruct((2, 8, LANES), f32),
            jax.ShapeDtypeStruct((TAPS, CHANNELS), f32),
            jax.ShapeDtypeStruct((CHANNELS, CHANNELS), f32),
            jax.ShapeDtypeStruct((COEFS, CHANNELS), f32),
        ),
        in_specs=[vmem] * len(pieces),
        out_specs=(vmem,) * 4,
        compiler_params=pltpu.CompilerParams(vmem_limit_bytes=8 * 1024 * 1024),
    )(*pieces)


def swap(x, axis, bit):
    return lax.ppermute(x, axis, [(i, i ^ bit) for i in range(lax.axis_size(axis))])


def strips(state, cotangent, first_weight, second_weight, third_weight):
    row_count = lax.axis_size("rows")
    block_count = lax.axis_size(("cols", "section"))
    weights = prepare_call(first_weight.T, second_weight, third_weight)

    def beside(flip):
        pairs = []
        for row in range(row_count):
            step = 1 if (row ^ flip) % 2 == 0 else block_count - 1
            for block in range(block_count):
                target = (row ^ flip) * block_count + (block + step) % block_count
                pairs.append((row * block_count + block, target))
        return pairs

    tile = jnp.concatenate([state, cotangent], 0)
    everyone = ("rows", "cols", "section")
    across = lax.ppermute(tile, everyone, beside(1))
    level = lax.ppermute(tile, everyone, beside(0))
    near = jnp.stack([tile, swap(tile, "rows", 1)])
    odd = lax.axis_index("rows") % 2 == 1
    half = [jnp.where(odd, x[..., :HALF], x[..., HALF:]) for x in (level, across)]
    other_near = jnp.concatenate(half, -1)
    both = swap(jnp.concatenate([near.reshape(8, 8, LANES), other_near]), "rows", 2)
    far, other_far = both[:8].reshape(2, 4, 8, LANES), both[8:]

    factor = gradient_gain / math.sqrt(row_count * state.shape[1] * LANES * block_count)
    mine, theirs, grads = strip_call(factor, (near, far, other_near, other_far), weights)

    grads = grads + swap(grads, "section", 1)
    ring = ("rows", "cols")
    across = lax.ppermute(grads, ring, [(i, i ^ 3) for i in range(2 * row_count)])
    beyond = swap(grads, "cols", 1)
    got = swap(jnp.concatenate([grads, theirs], 0), "rows", 1)
    tile, first, second, third = finish_call(grads, beyond, got, across, mine)
    return tile, first.T, second, third


def with_halo(block, sides, width):
    for axis, dim in sides:
        count = lax.axis_size(axis)
        forward = [(i, i + 1) for i in range(count - 1)]
        forward.append((count - 1, 0))
        backward = [(target, source) for source, target in forward]
        low = lax.ppermute(
            lax.slice_in_dim(block, block.shape[dim] - width, None, axis=dim), axis, forward
        )
        high = lax.ppermute(lax.slice_in_dim(block, 0, width, axis=dim), axis, backward)
        block = jnp.concatenate([low, block, high], axis=dim)
    return block


def base_table():
    return jnp.array(
        [
            [0.5 if tap_number in (5, 9) else 0.0 for tap_number in range(16)],
            [0.5 if tap_number in (5, 6) else 0.0 for tap_number in range(16)],
        ],
        jnp.float32,
    )


def patches(extended):
    height = extended.shape[1] - 3
    breadth = extended.shape[2] - 3
    pieces = [
        extended[:, offset_row : offset_row + height, offset_col : offset_col + breadth]
        for offset_row in range(3)
        for offset_col in range(3)
    ]
    return jnp.stack(pieces, 1).reshape(18, height * breadth)


def network(inputs, first_weight, second_weight, third_weight):
    rounded = inputs.astype(jnp.bfloat16)
    first_pre = jnp.dot(first_weight, rounded, preferred_element_type=jnp.float32)
    first_act = jax.nn.gelu(first_pre).astype(jnp.bfloat16)
    second_pre = jnp.dot(second_weight, first_act, preferred_element_type=jnp.float32)
    second_act = jax.nn.gelu(second_pre).astype(jnp.bfloat16)
    coefficients = jnp.dot(third_weight, second_act, preferred_element_type=jnp.float32)
    return (rounded, first_pre, first_act, second_pre, second_act, coefficients)


def physics(extended, coefficients):
    height = extended.shape[1] - 3
    breadth = extended.shape[2] - 3
    inner_rows = height - 1
    inner_cols = breadth - 1
    raw_output = coefficients.reshape(2, 16, height, breadth)
    weights = base_table()[:, :, None, None] + correction_gain * (
        raw_output - jnp.mean(raw_output, axis=1, keepdims=True)
    )
    stencil = jnp.stack(
        [
            extended[:, offset_row : offset_row + height, offset_col : offset_col + breadth]
            for offset_row in range(4)
            for offset_col in range(4)
        ],
        0,
    )
    face_rows = jnp.sum(weights[0][:, None] * stencil, axis=0)
    face_cols = jnp.sum(weights[1][:, None] * stencil, axis=0)
    speed_rows = 0.5 * (
        extended[0, 1 : 1 + height, 1 : 1 + breadth] + extended[0, 2 : 2 + height, 1 : 1 + breadth]
    )
    speed_cols = 0.5 * (
        extended[1, 1 : 1 + height, 1 : 1 + breadth] + extended[1, 1 : 1 + height, 2 : 2 + breadth]
    )
    flux_rows = speed_rows * face_rows
    flux_cols = speed_cols * face_cols
    transport = (
        flux_rows[:, 1:, 1:] - flux_rows[:, :-1, 1:] + flux_cols[:, 1:, 1:] - flux_cols[:, 1:, :-1]
    )
    centre = extended[:, 2 : 2 + inner_rows, 2 : 2 + inner_cols]
    laplace = (
        extended[:, 1 : 1 + inner_rows, 2 : 2 + inner_cols]
        + extended[:, 3 : 3 + inner_rows, 2 : 2 + inner_cols]
        + extended[:, 2 : 2 + inner_rows, 1 : 1 + inner_cols]
        + extended[:, 2 : 2 + inner_rows, 3 : 3 + inner_cols]
        - 4.0 * centre
    )
    return centre - time_step * transport + time_step * viscosity * laplace


def advance(extended, first_weight, second_weight, third_weight):
    outputs = network(patches(extended), first_weight, second_weight, third_weight)
    return physics(extended, outputs[5])


def gelu_back(preact, upstream):
    return jax.vjp(jax.nn.gelu, preact)[1](upstream)[0]


def advance_back(extended, first_weight, second_weight, third_weight, upstream):
    inputs, patch_back = jax.vjp(patches, extended)
    rounded, first_pre, first_act, second_pre, second_act, coefficients = network(
        inputs, first_weight, second_weight, third_weight
    )
    advanced, physics_back = jax.vjp(physics, extended, coefficients)
    extended_grad, coef_grad = physics_back(upstream)
    coef_round = coef_grad.astype(jnp.bfloat16)
    outer = (((1,), (1,)), ((), ()))
    inner = (((0,), (0,)), ((), ()))
    third_grad = lax.dot_general(coef_round, second_act, outer, preferred_element_type=jnp.float32)
    second_back = gelu_back(
        second_pre,
        lax.dot_general(third_weight, coef_round, inner, preferred_element_type=jnp.float32),
    ).astype(jnp.bfloat16)
    second_grad = lax.dot_general(second_back, first_act, outer, preferred_element_type=jnp.float32)
    first_back = gelu_back(
        first_pre,
        lax.dot_general(second_weight, second_back, inner, preferred_element_type=jnp.float32),
    ).astype(jnp.bfloat16)
    first_grad = lax.dot_general(first_back, rounded, outer, preferred_element_type=jnp.float32)
    input_grad = lax.dot_general(
        first_weight, first_back, inner, preferred_element_type=jnp.float32
    )
    extended_grad = extended_grad + patch_back(input_grad)[0]
    return (extended_grad, (first_grad, second_grad, third_grad))


def divergence(padded):
    return 0.5 * (
        padded[0, 2:, 1:-1] - padded[0, :-2, 1:-1] + (padded[1, 1:-1, 2:] - padded[1, 1:-1, :-2])
    )


def padded_neighbours(padded):
    return padded[2:, 1:-1] + padded[:-2, 1:-1] + padded[1:-1, 2:] + padded[1:-1, :-2]


def pressure_gradient(padded):
    return jnp.stack(
        [0.5 * (padded[2:, 1:-1] - padded[:-2, 1:-1]), 0.5 * (padded[1:-1, 2:] - padded[1:-1, :-2])]
    )


def fold_rims(returned, margin):
    row_count = returned.shape[-2] - 4 * margin
    col_count = returned.shape[-1] - 4 * margin
    leading = [(0, 0)] * (returned.ndim - 1)
    middle = (
        returned[..., 2 * margin : 2 * margin + col_count]
        + jnp.pad(returned[..., :margin], leading + [(0, col_count - margin)])
        + jnp.pad(returned[..., -margin:], leading + [(col_count - margin, 0)])
    )
    leading_rows = [(0, 0)] * (returned.ndim - 2)
    return (
        middle[..., 2 * margin : 2 * margin + row_count, :]
        + jnp.pad(middle[..., :margin, :], leading_rows + [(0, row_count - margin), (0, 0)])
        + jnp.pad(middle[..., -margin:, :], leading_rows + [(row_count - margin, 0), (0, 0)])
    )


def tiles(state, cotangent, first_weight, second_weight, third_weight):
    weights = (first_weight, second_weight, third_weight)
    current = state
    saved = []
    for step_number in range(STEPS):
        extended = with_halo(current, (("rows", 1), (("cols", "section"), 2)), 2)
        moved = advance(extended, *weights)
        velocity_pad = with_halo(moved, (("rows", 1), (("cols", "section"), 2)), 1)
        source = divergence(velocity_pad)
        pressure = -0.25 * source
        pressure_pads = []
        for sweep_number in range(SWEEPS):
            padded = with_halo(pressure, (("rows", 0), (("cols", "section"), 1)), 1)
            pressure_pads.append(padded)
            if sweep_number < SWEEPS - 1:
                pressure = 0.25 * (padded_neighbours(padded) - source)
        saved.append((extended, velocity_pad, pressure_pads))
        current = moved - pressure_gradient(pressure_pads[-1])
    upstream = cotangent
    totals = (
        jnp.zeros(first_weight.shape, jnp.float32),
        jnp.zeros(second_weight.shape, jnp.float32),
        jnp.zeros(third_weight.shape, jnp.float32),
    )
    for step_number in reversed(range(STEPS)):
        record = saved[step_number]
        velocity_pad = record[1]
        pressure_pads = record[2]
        pad_grad = jax.vjp(pressure_gradient, pressure_pads[-1])[1](-upstream)[0]
        source_grad = jnp.zeros_like(upstream[0])
        for sweep_number in reversed(range(SWEEPS)):
            returned = with_halo(pad_grad, (("rows", 0), (("cols", "section"), 1)), 1)
            pressure_grad = fold_rims(returned, 1)
            source_grad = source_grad - 0.25 * pressure_grad
            if sweep_number > 0:
                pad_grad = jax.vjp(padded_neighbours, pressure_pads[sweep_number - 1])[1](
                    0.25 * pressure_grad
                )[0]
        velocity_grad = jax.vjp(divergence, velocity_pad)[1](source_grad)[0]
        returned_velocity = with_halo(velocity_grad, (("rows", 1), (("cols", "section"), 2)), 1)
        moved_grad = upstream + fold_rims(returned_velocity, 1)
        extended_grad, grads = advance_back(
            record[0], first_weight, second_weight, third_weight, moved_grad
        )
        totals = (totals[0] + grads[0], totals[1] + grads[1], totals[2] + grads[2])
        if step_number > 0:
            returned_state = with_halo(extended_grad, (("rows", 1), (("cols", "section"), 2)), 2)
            upstream = fold_rims(returned_state, 2)
    totals = lax.psum((totals[0], totals[1], totals[2]), ("rows", "cols", "section"))
    cell_total = (
        state.shape[1] * state.shape[2] * lax.axis_size("rows") * lax.axis_size(("cols", "section"))
    )
    factor = gradient_gain / math.sqrt(cell_total)
    return (current, totals[0] * factor, totals[1] * factor, totals[2] * factor)


def solution(mesh):
    def program(state, *rest):
        fits = (
            lax.axis_size("rows") == 4
            and state.shape[1] == 8
            and state.shape[2] == LANES
            and lax.axis_size(("cols", "section")) >= 2
            and lax.axis_size("section") == 2
            and lax.axis_size("cols") == 2
        )
        return (strips if fits else tiles)(state, *rest)

    return jax.shard_map(
        program,
        mesh=mesh,
        in_specs=(
            P(None, ("groups", "rows"), ("cols", "section")),
            P(None, ("groups", "rows"), ("cols", "section")),
            P(),
            P(),
            P(),
        ),
        out_specs=(
            P(None, ("groups", "rows"), ("cols", "section")),
            P("groups", None),
            P("groups", None),
            P("groups", None),
        ),
        check_vma=False,
    )
```

```python
import functools
import math

import jax
import jax.numpy as jnp
from jax import lax
from jax.experimental import pallas as pl
from jax.experimental.pallas import tpu as pltpu
from jax.sharding import PartitionSpec as P

STEPS = 4
SWEEPS = 3
CHANNELS = 64
TAPS = 18
COEFS = 32
LANES = 128
HALF = LANES // 2
PACKED = 16
SIDE = 32

time_step = 0.1
viscosity = 0.2
correction_gain = 0.25
gradient_gain = 10.0

GELU_SCALE = math.sqrt(2.0 / math.pi)
GELU_CUBE = 0.044715


def shift(plane, row, col):
    if row:
        plane = pltpu.roll(plane, (-row) % plane.shape[0], 0)
    if col:
        plane = pltpu.roll(plane, (-col) % plane.shape[1], 1)
    return plane


def swap_halves(x):
    return pltpu.roll(x, HALF, 1)


def neighbours(p):
    return (shift(p, 1, 0) + shift(p, -1, 0)) + (shift(p, 0, 1) + shift(p, 0, -1))


def project(first, second):
    source = 0.5 * (
        (shift(first, 1, 0) - shift(first, -1, 0)) + (shift(second, 0, 1) - shift(second, 0, -1))
    )
    up = {k: shift(source, 0, k) for k in (1, 2, 3)}
    down = {k: shift(source, 0, -k) for k in (1, 2, 3)}

    def rows(plane, reach):
        return shift(plane, reach, 0) + shift(plane, -reach, 0)

    one = up[1] + down[1]
    mixed = 4.0 * source + 2.0 * one
    pressure = ((20.0 * source + 4.0 * one) + (up[2] + down[2])) + (rows(mixed, 1) + rows(source, 2))
    one, two = up[1] - down[1], up[2] - down[2]
    mixed = 4.0 * one + 2.0 * two
    slope = ((19.0 * one + 4.0 * two) + (up[3] - down[3])) + (rows(mixed, 1) + rows(one, 2))
    return (
        first + (1.0 / 128.0) * (shift(pressure, 1, 0) - shift(pressure, -1, 0)),
        second + (1.0 / 128.0) * slope,
    )


def dot(a, b):
    return jnp.dot(a, b, preferred_element_type=jnp.float32)


def dot_cells(a, b):
    return lax.dot_general(a, b, (((1,), (1,)), ((), ())), preferred_element_type=jnp.float32)


GELU_A, GELU_B = 2.0 * GELU_SCALE, 8.0 * GELU_SCALE * GELU_CUBE


def gelu_half(h):
    e = 1.0 + jnp.tanh(h * (GELU_A + GELU_B * (h * h)))
    return h * e, e


def gelu_half_slope(h, e):
    return e * (1.0 + (2.0 - e) * (h * (GELU_A + ((3.0 * GELU_B) * h) * h)))


def pick_taps(shape, place_dim):
    place = lax.broadcasted_iota(jnp.int32, shape, place_dim)
    tap = lax.broadcasted_iota(jnp.int32, shape, 1 - place_dim)
    row, col = (tap // 4) % 4, tap % 4
    wanted = (tap // 16) * 9 + row * 3 + col
    return jnp.where((place == wanted) & (row < 3) & (col < 3), 1.0, 0.0)


def prepare(w1_in, w2_in, w3_in, w1, w1t, w2, w2t, w3, w3t):
    f32, bf16 = jnp.float32, jnp.bfloat16
    spread = dot(pick_taps((32, TAPS), 1).astype(bf16), w1_in[...])
    w1[...] = (0.5 * spread.T).astype(bf16)
    w1t[...] = spread.astype(bf16)
    wide = w2_in[...].astype(f32)
    w2[...] = (0.5 * wide).astype(bf16)
    w2t[...] = (0.5 * wide.T).astype(bf16)
    wide = w3_in[...].astype(f32)
    w3t[...] = ((0.5 * correction_gain) * wide.T).astype(bf16)
    for f in range(2):
        rows = wide[16 * f : 16 * f + 16]
        rows = correction_gain * (rows - jnp.mean(rows, axis=0, keepdims=True))
        high = rows.astype(bf16)
        w3[16 * f : 16 * f + 16, 0:64] = high
        w3[16 * f : 16 * f + 16, 64:128] = (rows - high.astype(f32)).astype(bf16)


def prepare_call(w1_in, w2_in, w3_in):
    vmem = pl.BlockSpec(memory_space=pltpu.VMEM)
    shapes = ((CHANNELS, 32), (32, CHANNELS), (CHANNELS, CHANNELS), (CHANNELS, CHANNELS))
    shapes += ((COEFS, 2 * CHANNELS), (CHANNELS, COEFS))
    return pl.pallas_call(
        prepare,
        out_shape=tuple(jax.ShapeDtypeStruct(shape, jnp.bfloat16) for shape in shapes),
        in_specs=[vmem] * 3,
        out_specs=(vmem,) * 6,
        compiler_params=pltpu.CompilerParams(vmem_limit_bytes=8 * 1024 * 1024),
        cost_estimate=pl.CostEstimate(flops=1 << 20, bytes_accessed=1 << 16, transcendentals=0),
    )(w1_in, w2_in, w3_in)


def kernel(
    factor,
    own_near,
    own_far,
    other_near,
    other_far,
    w1,
    w1t,
    w2,
    w2t,
    w3,
    w3t,
    mine,
    theirs,
    grads,
    s_wide,
    s_all,
    up,
    qs,
    uu,
    ub,
    qp,
    bq,
    x_all,
    a1_all,
    a2_all,
    cf,
):
    f32, bf16 = jnp.float32, jnp.bfloat16
    z = lax.axis_index("rows")
    left = lax.broadcasted_iota(jnp.int32, (PACKED, LANES), 1) < HALF

    lane = lax.broadcasted_iota(jnp.int32, (8, LANES), 1)
    odd = (lane * 0 + z) % 2 == 1
    for k in range(4):
        row = pl.multiple_of(8 * (z ^ k), 8)
        own, other = ((own_near, other_near), (own_far, other_far))[k // 2]
        for c in range(4):
            here = own[k % 2, c]
            there = other[c] if k % 2 else swap_halves(other[c])
            turned = swap_halves(here)
            upper = jnp.where(odd, jnp.where(lane < HALF, turned, there), here)
            lower = jnp.where(odd, turned, there)
            narrow = jnp.where(lane < LANES - SIDE, upper, lower)
            if c < 2:
                s_wide[c, pl.ds(row, 8), 0:LANES] = upper
                s_wide[c, pl.ds(row, 8), LANES : 2 * LANES] = lower
                s_all[0, c, pl.ds(row, 8), :] = narrow
            else:
                up[c - 2, pl.ds(row, 8), :] = narrow

    def close(shape):
        column = lax.broadcasted_iota(jnp.int32, shape, 1) % HALF
        return (column < 16) | (column >= 48)

    def pack(plane, part, turned=None):
        if turned is None:
            plane = plane[:, LANES:] if part == 2 else plane[:, :LANES]
            turned = swap_halves(plane)
        low, high = plane[:PACKED], plane[PACKED:]
        low_turned, high_turned = turned[:PACKED], turned[PACKED:]
        if part == 0:
            return jnp.where(left, low, high_turned), jnp.where(left, high, low_turned)
        return jnp.where(left, low_turned, high), jnp.where(left, high_turned, low)

    def unpack(pieces, col=0):
        inner, outer = pieces[0], pieces[1]
        if len(pieces) == 3:
            lower = jnp.concatenate([swap_halves(pieces[2]), pieces[2]], 0)
            return shift(jnp.concatenate([unpack(pieces[:2]), lower], 1), 0, col)
        lanes = lax.broadcasted_iota(jnp.int32, (PACKED, LANES), 1)
        core = left if col == 0 else ((lanes + (col + LANES)) % LANES) < HALF
        return jnp.concatenate(
            [
                jnp.where(core, shift(inner, 0, col), shift(outer, 0, col + HALF)),
                jnp.where(core, shift(inner, 0, col + HALF), shift(outer, 0, col)),
            ],
            0,
        )

    def stencil(step, part, c, ah, r):
        at = 8 * (r + 2 * ah)
        return uu[step, part, c, at : at + 8, :]

    saved = {}

    def forward(step):
        parts = range(3) if step == 0 else range(2)
        s = [s_wide[c] if step == 0 else s_all[step, c] for c in range(2)]
        for c in range(2):
            for b in range(4):
                plane = shift(s[c], 0, b - 1)
                turned = None if step == 0 else shift(s[c], 0, b - 1 + HALF)
                for part in parts:
                    packed, swapped = pack(plane, part, turned)
                    ref = uu.at[step, part, c]
                    ref[pl.ds(8 + b, PACKED, stride=8), :] = packed
                    ref[pl.ds(4 + b, PACKED, stride=8), :] = packed
                    for at, r in ((b, PACKED - 1), (132 + b, 0), (136 + b, 0), (140 + b, 1)):
                        ref[at : at + 1, :] = swapped[r : r + 1]

        cells = PACKED * LANES
        rows = [(part, r) for part in parts for r in range(PACKED)]
        kept = cells if step == 0 else 2 * cells
        x = jnp.concatenate(
            [
                jnp.concatenate(
                    [stencil(step, part, c, ah, r) for c in range(2) for ah in range(2)], 0
                ).astype(bf16)
                for part, r in rows
            ],
            1,
        )
        x_all[step] = x[:, :cells]
        first = dot(w1[...], x)
        act, first_up = gelu_half(first)
        act = act.astype(bf16)
        a1_all[step] = act[:, :cells]
        second = dot(w2[...], act)
        act, second_up = gelu_half(second)
        act = act.astype(bf16)
        a2_all[step] = act[:, :cells]
        saved[step] = [value[:, :kept] for value in (first, first_up, second, second_up)]
        out = dot(w3[...], jnp.concatenate([act, act], 0))
        if step > 0:
            cf[step] = out
        for k, (part, r) in enumerate(rows):
            weight = out[:, k * LANES : (k + 1) * LANES]
            for c in range(2):
                lower = stencil(step, part, c, 0, r)
                upper = stencil(step, part, c, 1, r)
                for f in range(2):
                    qp[part, 2 * f + c, 8 * r : 8 * r + 8, :] = (
                        weight[16 * f : 16 * f + 8] * lower
                        + weight[16 * f + 8 : 16 * f + 16] * upper
                    )

        def reduced(part, which):
            terms = [qp[part, which, pl.ds(j, PACKED, stride=8), :] for j in range(8)]
            while len(terms) > 1:
                terms = [a + b for a, b in zip(terms[::2], terms[1::2])]
            return terms[0]

        moved = []
        speed = [0.5 * (s[0] + shift(s[0], 1, 0)), 0.5 * (s[1] + shift(s[1], 0, 1))]
        speed_below = shift(speed[1], 0, -1)
        for c in range(2):
            pieces = [[reduced(part, 2 * f + c) for part in parts] for f in range(2)]
            mean = [0.5 * (s[c] + shift(s[c], 1, 0)), 0.5 * (s[c] + shift(s[c], 0, 1))]
            q = [mean[f] + unpack(pieces[f]) for f in range(2)]
            if step > 0:
                for f in range(2):
                    qs[step, 2 * f + c] = q[f]
            rows = speed[0] * q[0]
            below = speed_below * (shift(mean[1], 0, -1) + unpack(pieces[1], -1))
            transport = (rows - shift(rows, -1, 0)) + (speed[1] * q[1] - below)
            moved.append(
                s[c]
                - time_step * transport
                + time_step * viscosity * (neighbours(s[c]) - 4.0 * s[c])
            )
        after = list(project(moved[0], moved[1]))
        for c in range(2):
            if step == 0:
                column = lax.broadcasted_iota(jnp.int32, (2 * PACKED, LANES), 1)
                after[c] = jnp.where(
                    column < LANES - SIDE, after[c][:, :LANES], after[c][:, LANES:]
                )
            s_all[step + 1, c] = after[c]

    def backward(step, total):
        u = [up[c] for c in range(2)]
        s = [s_all[step, c] for c in range(2)]
        m_bar = project(u[0], u[1])
        speed = [0.5 * (s[0] + shift(s[0], 1, 0)), 0.5 * (s[1] + shift(s[1], 0, 1))]
        box = []
        for c in range(2):
            pair = s[c] + shift(s[c], 0, 1)
            line = shift(pair, 0, -1) + shift(pair, 0, 1)
            pair = line + shift(line, 1, 0)
            box.append((1.0 / 16.0) * (shift(pair, -1, 0) + shift(pair, 1, 0)))
        speed_bar = [None, None]
        s_bar = []
        parts = range(2) if step > 0 else range(1)
        for part in parts:
            weights = [pack(time_step * speed[f], part)[0] for f in range(2)]
            boxes = [pack(box[c], part)[0] for c in range(2)]
            mean = [None, None]
            for c in range(2):
                here = pack(m_bar[c], part)[0]
                ahead = (
                    pack(shift(m_bar[c], 1, 0), part)[0],
                    pack(shift(m_bar[c], 0, 1), part, shift(m_bar[c], 0, 1 + HALF))[0],
                )
                for f in range(2):
                    q_bar = weights[f] * (ahead[f] - here)
                    bq[part, 2 * f + c] = q_bar
                    term = q_bar * boxes[c]
                    mean[f] = term if c == 0 else mean[f] + term
            for f in range(2):
                bq[part, 4 + f] = mean[f]
        for c in range(2) if step > 0 else ():
            flux_bar = [
                time_step * (shift(m_bar[c], 1, 0) - m_bar[c]),
                time_step * (shift(m_bar[c], 0, 1) - m_bar[c]),
            ]
            kept = m_bar[c] + time_step * viscosity * (neighbours(m_bar[c]) - 4.0 * m_bar[c])
            for f in range(2):
                term = qs[step, 2 * f + c] * flux_bar[f]
                speed_bar[f] = term if c == 0 else speed_bar[f] + term
                half = (0.5 * speed[f]) * flux_bar[f]
                kept = kept + (half + (shift(half, -1, 0) if f == 0 else shift(half, 0, -1)))
            s_bar.append(kept)
        if step > 0:
            half = 0.5 * speed_bar[0]
            s_bar[0] = s_bar[0] + (half + shift(half, -1, 0))
            half = 0.5 * speed_bar[1]
            s_bar[1] = s_bar[1] + (half + shift(half, 0, -1))

        cells = PACKED * LANES

        dense = step in (1, 2)
        lines = [(0, r) for r in range(PACKED)]
        if step > 0:
            lines += [(1, r) for r in range(PACKED // 2 if dense else PACKED)]

        def joined(value, part, r):
            if part == 1 and dense:
                here, there = value(r), pltpu.roll(value(r + 8), 32, 1)
                return jnp.where(close(here.shape), here, there)
            return value(r)

        def spread_row(part, which, r):
            row = joined(lambda k: bq[part, which, k : k + 1, :], part, r)
            return jnp.broadcast_to(row, (8, LANES))

        def taps(part, c, ah, r):
            return joined(lambda k: stencil(step, part, c, ah, k), part, r)

        def columns(array):
            def block(part, k):
                at = (part * PACKED + k) * LANES
                return array[:, at : at + LANES]

            return jnp.concatenate(
                [joined(functools.partial(block, part), part, r) for part, r in lines], 1
            )

        third = []
        for part, r in lines:
            pieces = []
            for f in range(2):
                q0, q1, m = (spread_row(part, w, r) for w in (2 * f, 2 * f + 1, 4 + f))
                for ah in range(2):
                    pieces.append((q0 * taps(part, 0, ah, r) + q1 * taps(part, 1, ah, r)) - m)
            third.append(jnp.concatenate(pieces, 0).astype(bf16))
        third = jnp.concatenate(third, 1)
        first, first_up, second, second_up = (columns(value) for value in saved[step])
        second = (dot(w3t[...], third) * gelu_half_slope(second, second_up)).astype(bf16)
        first = (dot(w2t[...], second) * gelu_half_slope(first, first_up)).astype(bf16)

        def gradients():
            terms = (
                dot_cells(x_all[step], first[:, :cells]),
                dot_cells(second[:, :cells], a1_all[step]),
                dot_cells(third[:, :cells], a2_all[step]),
            )
            return terms if total is None else tuple(a + b for a, b in zip(total, terms))

        if step == 0:
            return gradients()
        out = dot(w1t[...], first)
        weights = columns(cf[step])

        for part in parts:
            y = {}
            for k, (piece, r) in enumerate(lines):
                if piece != part:
                    continue
                lanes = slice(k * LANES, (k + 1) * LANES)
                for c in range(2):
                    q0, q1 = spread_row(part, c, r), spread_row(part, 2 + c, r)
                    for ah in range(2):
                        y[c, ah, r] = (
                            weights[8 * ah : 8 * ah + 8, lanes] * q0
                            + weights[16 + 8 * ah : 24 + 8 * ah, lanes] * q1
                        ) + out[16 * c + 8 * ah : 16 * c + 8 * ah + 8, lanes]
            if part == 1 and dense:
                for c in range(2):
                    for ah in range(2):
                        for r in range(PACKED // 2):
                            value = y[c, ah, r]
                            y[c, ah, r + 8] = jnp.where(
                                close(value.shape), pltpu.roll(value, LANES - 32, 1), 0.0
                            )
                            y[c, ah, r] = jnp.where(close(value.shape), value, 0.0)
            for c in range(2):
                rows = []
                for m in range(PACKED):
                    value = y[c, 0, m + 1] if m + 1 < PACKED else swap_halves(y[c, 0, 0])
                    before = y[c, 1, m - 1] if m > 0 else swap_halves(y[c, 1, PACKED - 1])
                    rows.append(value + before)
                ub[part, c, 0:8, :] = swap_halves(rows[PACKED - 1])
                for m in range(PACKED):
                    ub[part, c, 8 + 8 * m : 16 + 8 * m, :] = rows[m]

        for c in range(2):
            kept = s_bar[c]
            for b in range(4):
                kept = kept + unpack(
                    [
                        ub[part, c, pl.ds(8 + b, PACKED, stride=8), :]
                        + ub[part, c, pl.ds(4 + b, PACKED, stride=8), :]
                        for part in parts
                    ],
                    1 - b,
                )
            up[c] = kept
        return gradients()

    for step in range(STEPS):
        forward(step)
    for ref, tile in ((mine, z), (theirs, z ^ 1)):
        first, second = (s_all[STEPS, c, pl.ds(pl.multiple_of(8 * tile, 8), 8), :] for c in range(2))
        ref[...] = jnp.where(lane < HALF, first, swap_halves(second))
    total = None
    for step in reversed(range(STEPS)):
        total = backward(step, total)
    grads[:, 0:64] = factor * total[1]
    first = factor * total[0]
    for c in range(2):
        for a in range(3):
            grads[9 * c + 3 * a : 9 * c + 3 * a + 3, 64:128] = first[16 * c + 4 * a : 16 * c + 4 * a + 3]
    grads[TAPS:32, 64:128] = jnp.zeros((32 - TAPS, CHANNELS), f32)
    grads[32:64, 64:128] = (factor * correction_gain) * total[2]


def strip_call(factor, pieces, weights):
    cells = PACKED * LANES
    f32, bf16 = jnp.float32, jnp.bfloat16
    vmem = pl.BlockSpec(memory_space=pltpu.VMEM)
    return pl.pallas_call(
        functools.partial(kernel, factor),
        out_shape=(
            jax.ShapeDtypeStruct((8, LANES), f32),
            jax.ShapeDtypeStruct((8, LANES), f32),
            jax.ShapeDtypeStruct((CHANNELS, LANES), f32),
        ),
        in_specs=[vmem] * 10,
        out_specs=(vmem,) * 3,
        scratch_shapes=[
            pltpu.VMEM((2, 2 * PACKED, 2 * LANES), f32),
            pltpu.VMEM((STEPS + 1, 2, 2 * PACKED, LANES), f32),
            pltpu.VMEM((2, 2 * PACKED, LANES), f32),
            pltpu.VMEM((STEPS, 4, 2 * PACKED, LANES), f32),
            pltpu.VMEM((STEPS, 3, 2, 8 * (PACKED + 2), LANES), f32),
            pltpu.VMEM((2, 2, 8 * (PACKED + 1), LANES), f32),
            pltpu.VMEM((3, 4, 8 * PACKED, LANES), f32),
            pltpu.VMEM((2, 6, PACKED, LANES), f32),
            pltpu.VMEM((STEPS, 32, cells), bf16),
            pltpu.VMEM((STEPS, CHANNELS, cells), bf16),
            pltpu.VMEM((STEPS, CHANNELS, cells), bf16),
            pltpu.VMEM((STEPS, COEFS, 2 * cells), f32),
        ],
        compiler_params=pltpu.CompilerParams(vmem_limit_bytes=48 * 1024 * 1024),
    )(*pieces, *weights)


def finish(sent, beyond, got, across, mine, tile, first, second, third):
    z = lax.axis_index("rows")
    lane = lax.broadcasted_iota(jnp.int32, (8, LANES), 1)
    odd = (lane * 0 + z) % 2 == 1
    near, far = mine[...], got[64:72, :]
    for c in range(2):
        here, there = (x if c == 0 else swap_halves(x) for x in (near, far))
        low = jnp.where(odd, there, here)
        high = jnp.where(odd, here, there)
        tile[c] = jnp.where(lane < HALF, low, swap_halves(high))
    grads = (sent[...] + beyond[...]) + (got[0:64, :] + across[...])
    first[...] = grads[0:TAPS, 64:]
    second[...] = grads[:, 0:64]
    third[...] = grads[32:, 64:]


def finish_call(*pieces):
    vmem = pl.BlockSpec(memory_space=pltpu.VMEM)
    f32 = jnp.float32
    return pl.pallas_call(
        finish,
        out_shape=(
            jax.ShapeDtypeStruct((2, 8, LANES), f32),
            jax.ShapeDtypeStruct((TAPS, CHANNELS), f32),
            jax.ShapeDtypeStruct((CHANNELS, CHANNELS), f32),
            jax.ShapeDtypeStruct((COEFS, CHANNELS), f32),
        ),
        in_specs=[vmem] * len(pieces),
        out_specs=(vmem,) * 4,
        compiler_params=pltpu.CompilerParams(vmem_limit_bytes=8 * 1024 * 1024),
    )(*pieces)


def swap(x, axis, bit):
    return lax.ppermute(x, axis, [(i, i ^ bit) for i in range(lax.axis_size(axis))])


def strips(state, cotangent, first_weight, second_weight, third_weight):
    row_count = lax.axis_size("rows")
    block_count = lax.axis_size(("cols", "section"))
    weights = prepare_call(first_weight.T, second_weight, third_weight)

    def beside(flip):
        pairs = []
        for row in range(row_count):
            step = 1 if (row ^ flip) % 2 == 0 else block_count - 1
            for block in range(block_count):
                target = (row ^ flip) * block_count + (block + step) % block_count
                pairs.append((row * block_count + block, target))
        return pairs

    tile = jnp.concatenate([state, cotangent], 0)
    everyone = ("rows", "cols", "section")
    across = lax.ppermute(tile, everyone, beside(1))
    level = lax.ppermute(tile, everyone, beside(0))
    near = jnp.stack([tile, swap(tile, "rows", 1)])
    odd = lax.axis_index("rows") % 2 == 1
    half = [jnp.where(odd, x[..., :HALF], x[..., HALF:]) for x in (level, across)]
    other_near = jnp.concatenate(half, -1)
    both = swap(jnp.concatenate([near.reshape(8, 8, LANES), other_near]), "rows", 2)
    far, other_far = both[:8].reshape(2, 4, 8, LANES), both[8:]

    factor = gradient_gain / math.sqrt(row_count * state.shape[1] * LANES * block_count)
    mine, theirs, grads = strip_call(factor, (near, far, other_near, other_far), weights)

    grads = grads + swap(grads, "section", 1)
    ring = ("rows", "cols")
    across = lax.ppermute(grads, ring, [(i, i ^ 3) for i in range(2 * row_count)])
    beyond = swap(grads, "cols", 1)
    got = swap(jnp.concatenate([grads, theirs], 0), "rows", 1)
    tile, first, second, third = finish_call(grads, beyond, got, across, mine)
    return tile, first.T, second, third


def with_halo(block, sides, width):
    for axis, dim in sides:
        count = lax.axis_size(axis)
        forward = [(i, i + 1) for i in range(count - 1)]
        forward.append((count - 1, 0))
        backward = [(target, source) for source, target in forward]
        low = lax.ppermute(
            lax.slice_in_dim(block, block.shape[dim] - width, None, axis=dim), axis, forward
        )
        high = lax.ppermute(lax.slice_in_dim(block, 0, width, axis=dim), axis, backward)
        block = jnp.concatenate([low, block, high], axis=dim)
    return block


def base_table():
    return jnp.array(
        [
            [0.5 if tap_number in (5, 9) else 0.0 for tap_number in range(16)],
            [0.5 if tap_number in (5, 6) else 0.0 for tap_number in range(16)],
        ],
        jnp.float32,
    )


def patches(extended):
    height = extended.shape[1] - 3
    breadth = extended.shape[2] - 3
    pieces = [
        extended[:, offset_row : offset_row + height, offset_col : offset_col + breadth]
        for offset_row in range(3)
        for offset_col in range(3)
    ]
    return jnp.stack(pieces, 1).reshape(18, height * breadth)


def network(inputs, first_weight, second_weight, third_weight):
    rounded = inputs.astype(jnp.bfloat16)
    first_pre = jnp.dot(first_weight, rounded, preferred_element_type=jnp.float32)
    first_act = jax.nn.gelu(first_pre).astype(jnp.bfloat16)
    second_pre = jnp.dot(second_weight, first_act, preferred_element_type=jnp.float32)
    second_act = jax.nn.gelu(second_pre).astype(jnp.bfloat16)
    coefficients = jnp.dot(third_weight, second_act, preferred_element_type=jnp.float32)
    return (rounded, first_pre, first_act, second_pre, second_act, coefficients)


def physics(extended, coefficients):
    height = extended.shape[1] - 3
    breadth = extended.shape[2] - 3
    inner_rows = height - 1
    inner_cols = breadth - 1
    raw_output = coefficients.reshape(2, 16, height, breadth)
    weights = base_table()[:, :, None, None] + correction_gain * (
        raw_output - jnp.mean(raw_output, axis=1, keepdims=True)
    )
    stencil = jnp.stack(
        [
            extended[:, offset_row : offset_row + height, offset_col : offset_col + breadth]
            for offset_row in range(4)
            for offset_col in range(4)
        ],
        0,
    )
    face_rows = jnp.sum(weights[0][:, None] * stencil, axis=0)
    face_cols = jnp.sum(weights[1][:, None] * stencil, axis=0)
    speed_rows = 0.5 * (
        extended[0, 1 : 1 + height, 1 : 1 + breadth] + extended[0, 2 : 2 + height, 1 : 1 + breadth]
    )
    speed_cols = 0.5 * (
        extended[1, 1 : 1 + height, 1 : 1 + breadth] + extended[1, 1 : 1 + height, 2 : 2 + breadth]
    )
    flux_rows = speed_rows * face_rows
    flux_cols = speed_cols * face_cols
    transport = (
        flux_rows[:, 1:, 1:] - flux_rows[:, :-1, 1:] + flux_cols[:, 1:, 1:] - flux_cols[:, 1:, :-1]
    )
    centre = extended[:, 2 : 2 + inner_rows, 2 : 2 + inner_cols]
    laplace = (
        extended[:, 1 : 1 + inner_rows, 2 : 2 + inner_cols]
        + extended[:, 3 : 3 + inner_rows, 2 : 2 + inner_cols]
        + extended[:, 2 : 2 + inner_rows, 1 : 1 + inner_cols]
        + extended[:, 2 : 2 + inner_rows, 3 : 3 + inner_cols]
        - 4.0 * centre
    )
    return centre - time_step * transport + time_step * viscosity * laplace


def advance(extended, first_weight, second_weight, third_weight):
    outputs = network(patches(extended), first_weight, second_weight, third_weight)
    return physics(extended, outputs[5])


def gelu_back(preact, upstream):
    return jax.vjp(jax.nn.gelu, preact)[1](upstream)[0]


def advance_back(extended, first_weight, second_weight, third_weight, upstream):
    inputs, patch_back = jax.vjp(patches, extended)
    rounded, first_pre, first_act, second_pre, second_act, coefficients = network(
        inputs, first_weight, second_weight, third_weight
    )
    advanced, physics_back = jax.vjp(physics, extended, coefficients)
    extended_grad, coef_grad = physics_back(upstream)
    coef_round = coef_grad.astype(jnp.bfloat16)
    outer = (((1,), (1,)), ((), ()))
    inner = (((0,), (0,)), ((), ()))
    third_grad = lax.dot_general(coef_round, second_act, outer, preferred_element_type=jnp.float32)
    second_back = gelu_back(
        second_pre,
        lax.dot_general(third_weight, coef_round, inner, preferred_element_type=jnp.float32),
    ).astype(jnp.bfloat16)
    second_grad = lax.dot_general(second_back, first_act, outer, preferred_element_type=jnp.float32)
    first_back = gelu_back(
        first_pre,
        lax.dot_general(second_weight, second_back, inner, preferred_element_type=jnp.float32),
    ).astype(jnp.bfloat16)
    first_grad = lax.dot_general(first_back, rounded, outer, preferred_element_type=jnp.float32)
    input_grad = lax.dot_general(
        first_weight, first_back, inner, preferred_element_type=jnp.float32
    )
    extended_grad = extended_grad + patch_back(input_grad)[0]
    return (extended_grad, (first_grad, second_grad, third_grad))


def divergence(padded):
    return 0.5 * (
        padded[0, 2:, 1:-1] - padded[0, :-2, 1:-1] + (padded[1, 1:-1, 2:] - padded[1, 1:-1, :-2])
    )


def padded_neighbours(padded):
    return padded[2:, 1:-1] + padded[:-2, 1:-1] + padded[1:-1, 2:] + padded[1:-1, :-2]


def pressure_gradient(padded):
    return jnp.stack(
        [0.5 * (padded[2:, 1:-1] - padded[:-2, 1:-1]), 0.5 * (padded[1:-1, 2:] - padded[1:-1, :-2])]
    )


def fold_rims(returned, margin):
    row_count = returned.shape[-2] - 4 * margin
    col_count = returned.shape[-1] - 4 * margin
    leading = [(0, 0)] * (returned.ndim - 1)
    middle = (
        returned[..., 2 * margin : 2 * margin + col_count]
        + jnp.pad(returned[..., :margin], leading + [(0, col_count - margin)])
        + jnp.pad(returned[..., -margin:], leading + [(col_count - margin, 0)])
    )
    leading_rows = [(0, 0)] * (returned.ndim - 2)
    return (
        middle[..., 2 * margin : 2 * margin + row_count, :]
        + jnp.pad(middle[..., :margin, :], leading_rows + [(0, row_count - margin), (0, 0)])
        + jnp.pad(middle[..., -margin:, :], leading_rows + [(row_count - margin, 0), (0, 0)])
    )


def tiles(state, cotangent, first_weight, second_weight, third_weight):
    weights = (first_weight, second_weight, third_weight)
    current = state
    saved = []
    for step_number in range(STEPS):
        extended = with_halo(current, (("rows", 1), (("cols", "section"), 2)), 2)
        moved = advance(extended, *weights)
        velocity_pad = with_halo(moved, (("rows", 1), (("cols", "section"), 2)), 1)
        source = divergence(velocity_pad)
        pressure = -0.25 * source
        pressure_pads = []
        for sweep_number in range(SWEEPS):
            padded = with_halo(pressure, (("rows", 0), (("cols", "section"), 1)), 1)
            pressure_pads.append(padded)
            if sweep_number < SWEEPS - 1:
                pressure = 0.25 * (padded_neighbours(padded) - source)
        saved.append((extended, velocity_pad, pressure_pads))
        current = moved - pressure_gradient(pressure_pads[-1])
    upstream = cotangent
    totals = (
        jnp.zeros(first_weight.shape, jnp.float32),
        jnp.zeros(second_weight.shape, jnp.float32),
        jnp.zeros(third_weight.shape, jnp.float32),
    )
    for step_number in reversed(range(STEPS)):
        record = saved[step_number]
        velocity_pad = record[1]
        pressure_pads = record[2]
        pad_grad = jax.vjp(pressure_gradient, pressure_pads[-1])[1](-upstream)[0]
        source_grad = jnp.zeros_like(upstream[0])
        for sweep_number in reversed(range(SWEEPS)):
            returned = with_halo(pad_grad, (("rows", 0), (("cols", "section"), 1)), 1)
            pressure_grad = fold_rims(returned, 1)
            source_grad = source_grad - 0.25 * pressure_grad
            if sweep_number > 0:
                pad_grad = jax.vjp(padded_neighbours, pressure_pads[sweep_number - 1])[1](
                    0.25 * pressure_grad
                )[0]
        velocity_grad = jax.vjp(divergence, velocity_pad)[1](source_grad)[0]
        returned_velocity = with_halo(velocity_grad, (("rows", 1), (("cols", "section"), 2)), 1)
        moved_grad = upstream + fold_rims(returned_velocity, 1)
        extended_grad, grads = advance_back(
            record[0], first_weight, second_weight, third_weight, moved_grad
        )
        totals = (totals[0] + grads[0], totals[1] + grads[1], totals[2] + grads[2])
        if step_number > 0:
            returned_state = with_halo(extended_grad, (("rows", 1), (("cols", "section"), 2)), 2)
            upstream = fold_rims(returned_state, 2)
    totals = lax.psum((totals[0], totals[1], totals[2]), ("rows", "cols", "section"))
    cell_total = (
        state.shape[1] * state.shape[2] * lax.axis_size("rows") * lax.axis_size(("cols", "section"))
    )
    factor = gradient_gain / math.sqrt(cell_total)
    return (current, totals[0] * factor, totals[1] * factor, totals[2] * factor)


def solution(mesh):
    def program(state, *rest):
        fits = (
            lax.axis_size("rows") == 4
            and state.shape[1] == 8
            and state.shape[2] == LANES
            and lax.axis_size(("cols", "section")) >= 2
            and lax.axis_size("section") == 2
            and lax.axis_size("cols") == 2
        )
        return (strips if fits else tiles)(state, *rest)

    return jax.shard_map(
        program,
        mesh=mesh,
        in_specs=(
            P(None, ("groups", "rows"), ("cols", "section")),
            P(None, ("groups", "rows"), ("cols", "section")),
            P(),
            P(),
            P(),
        ),
        out_specs=(
            P(None, ("groups", "rows"), ("cols", "section")),
            P("groups", None),
            P("groups", None),
            P("groups", None),
        ),
        check_vma=False,
    )
```
